32 devices in a mesh: seg: 16 (over z, y, x), rep: 2 (over core).
Axes of the slice: x: 2, y: 2, z: 4, core: 2. Of those that a mesh axis runs over, the one named last changes fastest.
Arguments:
- tokens: bfloat16 [2, 64, 128, 768], P(None, ('seg', 'rep')), may hold values from -6 to 6
- token_counts: int32 [2, 64], replicated, may hold values from 0 to 128, as said below
- segment_project: bfloat16 [768, 2304], P(('seg', 'rep')), may hold values from -0.21875 to 0.21875
- segment_output: bfloat16 [768, 768], P(('seg', 'rep')), may hold values from -0.875 to 0.875
- segment_up: bfloat16 [768, 3072], P(('seg', 'rep')), may hold values from -0.21875 to 0.21875
- segment_down: bfloat16 [3072, 768], P(('seg', 'rep')), may hold values from -0.109375 to 0.109375
- segment_scale: bfloat16 [768], P(('seg', 'rep')), may hold values from 0.25 to 1.75
- segment_offset: bfloat16 [768], P(('seg', 'rep')), may hold values from -3 to 3
- segment_gain: bfloat16 [768], P(('seg', 'rep')), may hold values from 0.25 to 1.75
- segment_shift: bfloat16 [768], P(('seg', 'rep')), may hold values from -3 to 3
- document_project: bfloat16 [768, 2304], P(('seg', 'rep')), may hold values from -0.21875 to 0.21875
- document_output: bfloat16 [768, 768], P(('seg', 'rep')), may hold values from -0.875 to 0.875
- document_up: bfloat16 [768, 3072], P(('seg', 'rep')), may hold values from -0.21875 to 0.21875
- document_down: bfloat16 [3072, 768], P(('seg', 'rep')), may hold values from -0.109375 to 0.109375
- document_scale: bfloat16 [768], P(('seg', 'rep')), may hold values from 0.25 to 1.75
- document_offset: bfloat16 [768], P(('seg', 'rep')), may hold values from -3 to 3
- document_gain: bfloat16 [768], P(('seg', 'rep')), may hold values from 0.25 to 1.75
- document_shift: bfloat16 [768], P(('seg', 'rep')), may hold values from -3 to 3
- position: bfloat16 [768, 32], P(('seg', 'rep')), may hold values from -3 to 3
- cotangent: bfloat16 [2, 64, 128, 768], P(None, ('seg', 'rep')), may hold values from -6 to 6
Outputs:
- output: bfloat16 [2, 64, 128, 768], P(None, ('seg', 'rep'))
- input_gradient: float32 [2, 64, 128, 768], P(None, ('seg', 'rep'))
- segment_project_gradient: float32 [768, 2304], P(('seg', 'rep'))
- segment_output_gradient: float32 [768, 768], P(('seg', 'rep'))
- segment_up_gradient: float32 [768, 3072], P(('seg', 'rep'))
- segment_down_gradient: float32 [3072, 768], P(('seg', 'rep'))
- segment_scale_gradient: float32 [768], P(('seg', 'rep'))
- segment_offset_gradient: float32 [768], P(('seg', 'rep'))
- segment_gain_gradient: float32 [768], P(('seg', 'rep'))
- segment_shift_gradient: float32 [768], P(('seg', 'rep'))
- document_project_gradient: float32 [768, 2304], P(('seg', 'rep'))
- document_output_gradient: float32 [768, 768], P(('seg', 'rep'))
- document_up_gradient: float32 [768, 3072], P(('seg', 'rep'))
- document_down_gradient: float32 [3072, 768], P(('seg', 'rep'))
- document_scale_gradient: float32 [768], P(('seg', 'rep'))
- document_offset_gradient: float32 [768], P(('seg', 'rep'))
- document_gain_gradient: float32 [768], P(('seg', 'rep'))
- document_shift_gradient: float32 [768], P(('seg', 'rep'))
- position_gradient: float32 [768, 32], P(('seg', 'rep'))
The draws below stay inside these ranges and needn't reach their ends.
Inputs may be any that keep to these rules, and one draw needn't show every extreme that they name: `token_counts`: within each document of 32 segments the counts are 128 up to one segment, which holds between 1 and 128 tokens, and 0 after it; the first segment of every document is full.
All inputs are finite; a program needn't handle non-finite values.
Results may differ from the reference program's by a relative error of at most 0.025.
Values may be sent and summed in bfloat16 or wider, within the bound.
A program may use at most 256 MiB of HBM per device.

```python
import math
import jax
import jax.numpy as jnp
from jax import lax

D = 768
HEADS = 12
FF = 3072
SEG_LEN = 128
DOC_SEGS = 32
MB = 2
SEGS = 64
DOCS = 2


def draw_token_counts(key, part):
    total_length = DOC_SEGS * SEG_LEN
    lengths = jax.random.randint(key, (MB, DOCS), total_length // 2, total_length + 1)
    lengths = lengths.at[:, 0].set(total_length - SEG_LEN - SEG_LEN // 2)
    starts = jnp.arange(DOC_SEGS) * SEG_LEN
    counts = jnp.clip(lengths[:, :, None] - starts[None, None, :], 0, SEG_LEN)
    return counts.reshape(MB, DOCS * DOC_SEGS).astype(jnp.int32)


def with_spikes(values, rng, source, target, shards_of, factor):
    def block_of(axis_at):
        return (jnp.arange(values.shape[axis_at]) // (values.shape[axis_at] // shards_of)).reshape((-1,) + (1,) * (values.ndim - 1 - axis_at))

    near = jax.random.permutation(rng, shards_of)[block_of(target)]
    far = (block_of(target) + shards_of // 2) % shards_of
    return jnp.where((block_of(source) == near) | (block_of(source) == far), factor * values, values)


def steps_of(key, shape, shards, low, top_value):
    level, own = 1.0, jax.random.fold_in(key, 6)
    for dim, blocks in shards:
        draws = jnp.exp(jax.random.uniform(jax.random.fold_in(own, dim), (blocks,), jnp.float32, low / len(shards), top_value / len(shards)))
        level = level * jnp.repeat(draws, shape[dim] // blocks).reshape([-1 if axis == dim else 1 for axis in range(len(shape))])
    return level


def scatter_about(rng, shape, spread, limit, pieces=(), held_as=jnp.bfloat16):
    drawn = spread * jax.random.normal(rng, shape, jnp.float32)
    if pieces:
        drawn = drawn * steps_of(rng, shape, pieces, -0.22, 0.18)
    return jnp.clip(drawn, -limit, limit).astype(held_as)


def heavy_noise(rng, dims, spread, bound, shards, heavy, dtype=jnp.bfloat16):
    drawn = spread * jax.random.normal(rng, dims, jnp.float32)
    if shards:
        drawn = drawn * steps_of(rng, dims, shards, -0.22, 0.18)
    return jnp.clip(with_spikes(drawn, jax.random.fold_in(rng, 3), *heavy), -bound, bound).astype(dtype)


def setup_inputs(seed: int = 0) -> dict:
    streams_of = jax.random.split(jax.random.key(seed), 21)
    tokens = scatter_about(streams_of[0], (MB, SEGS, SEG_LEN, D), 1.0, 6.0, ((1, 32),))
    token_counts = draw_token_counts(jax.random.fold_in(streams_of[20], 71), 0)
    segment_project = scatter_about(streams_of[2], (D, 3 * D), D ** -0.5, 0.21875, ((0, 32),))
    segment_output = scatter_about(streams_of[3], (D, D), (D // 16) ** -0.5, 0.875, ((0, 32),))
    segment_up = scatter_about(streams_of[4], (D, FF), D ** -0.5, 0.21875, ((0, 32),))
    segment_down = scatter_about(streams_of[5], (FF, D), FF ** -0.5, 0.109375, ((0, 32),))
    segment_scale = jnp.clip(1.0 + 0.15 * jax.random.normal(streams_of[6], (D,), jnp.float32), 0.25, 1.75).astype(jnp.bfloat16)
    segment_offset = scatter_about(streams_of[7], (D,), 0.3, 3.0, ((0, 32),))
    segment_gain = jnp.clip(1.0 + 0.15 * jax.random.normal(streams_of[8], (D,), jnp.float32), 0.25, 1.75).astype(jnp.bfloat16)
    segment_shift = scatter_about(streams_of[9], (D,), 0.3, 3.0, ((0, 32),))
    document_project = scatter_about(streams_of[10], (D, 3 * D), D ** -0.5, 0.21875, ((0, 32),))
    document_output = scatter_about(streams_of[11], (D, D), (D // 16) ** -0.5, 0.875, ((0, 32),))
    document_up = scatter_about(streams_of[12], (D, FF), D ** -0.5, 0.21875, ((0, 32),))
    document_down = scatter_about(streams_of[13], (FF, D), FF ** -0.5, 0.109375, ((0, 32),))
    document_scale = jnp.clip(1.0 + 0.15 * jax.random.normal(streams_of[14], (D,), jnp.float32), 0.25, 1.75).astype(jnp.bfloat16)
    document_offset = scatter_about(streams_of[15], (D,), 0.3, 3.0, ((0, 32),))
    document_gain = jnp.clip(1.0 + 0.15 * jax.random.normal(streams_of[16], (D,), jnp.float32), 0.25, 1.75).astype(jnp.bfloat16)
    document_shift = scatter_about(streams_of[17], (D,), 0.3, 3.0, ((0, 32),))
    position = scatter_about(streams_of[18], (D, DOC_SEGS), 0.5, 3.0, ((0, 32),))
    cotangent = heavy_noise(streams_of[19], (MB, SEGS, SEG_LEN, D), 1.0, 6.0, ((1, 32),), (1, 3, 32, 2.75))
    return {"tokens": tokens, "token_counts": token_counts, "segment_project": segment_project, "segment_output": segment_output, "segment_up": segment_up, "segment_down": segment_down, "segment_scale": segment_scale, "segment_offset": segment_offset, "segment_gain": segment_gain, "segment_shift": segment_shift, "document_project": document_project, "document_output": document_output, "document_up": document_up, "document_down": document_down, "document_scale": document_scale, "document_offset": document_offset, "document_gain": document_gain, "document_shift": document_shift, "position": position, "cotangent": cotangent}


@jax.custom_vjp
def low(v):
    return lax.optimization_barrier(v.astype(jnp.bfloat16)).astype(jnp.float32)

@jax.custom_vjp
def low_back(v):
    return v

def low_keep(v):
    return (low(v), None)

def low_pass(kept, grad):
    return (grad,)

def back_keep(v):
    return (v, None)

def back_low(kept, grad):
    return (low(grad),)
low.defvjp(low_keep, low_pass)
low_back.defvjp(back_keep, back_low)
epsilon = 1e-05
floor_score = -1e+30
root_half = 1.0 / math.sqrt(2.0)

def exact_product(left, right):
    return jnp.matmul(left, right, precision=lax.Precision.HIGHEST)

def gelu_value(value):
    return 0.5 * value * (1.0 + lax.erf(value * root_half))

def norm_apply(value, gain, shift):
    centred = value - lax.optimization_barrier(jnp.mean(value, axis=-1, keepdims=True))
    inverse = lax.rsqrt(lax.optimization_barrier(jnp.mean(centred * centred, axis=-1, keepdims=True)) + epsilon)
    return centred * inverse * gain + shift

def block(inputs, valid, layer):
    project_weight, output_weight, up_weight, down_weight, first_gain, first_shift, second_gain, second_shift = layer
    groups, length, width = inputs.shape
    head_width = width // HEADS
    projected = low(low_back(exact_product(low(inputs), project_weight)))
    parts = projected.reshape(groups, length, 3, HEADS, head_width)
    scores = jnp.einsum('bqhe,bkhe->bhqk', parts[:, :, 0], parts[:, :, 1], precision=lax.Precision.HIGHEST) * (1.0 / math.sqrt(head_width))
    scores = low_back(jnp.where(valid[:, None, None, :], scores, floor_score))
    highest = lax.optimization_barrier(jnp.max(scores, axis=-1, keepdims=True))
    raised = jnp.exp(scores - highest)
    shares = raised / lax.optimization_barrier(jnp.sum(raised, axis=-1, keepdims=True))
    context = jnp.einsum('bhqk,bkhe->bqhe', low(shares), parts[:, :, 2], precision=lax.Precision.HIGHEST)
    context = low(low_back(context)).reshape(groups, length, width)
    mixed = low_back(exact_product(context, output_weight))
    first = norm_apply(inputs + mixed, first_gain, first_shift)
    hidden = low_back(exact_product(low(first), up_weight))
    branch = low_back(exact_product(low(gelu_value(hidden)), down_weight))
    return norm_apply(first + branch, second_gain, second_shift)

def document(document_tokens, document_counts, weights):
    positions = jnp.arange(SEG_LEN)
    token_valid = (positions[None, :] < document_counts[:, None]) | (positions[None, :] == 0)
    rows = block(document_tokens, token_valid, weights[0:8])
    summary = rows[:, 0, :] + jnp.transpose(weights[16])
    summary_out = block(summary[None], (document_counts > 0)[None], weights[8:16])[0]
    return rows.at[:, 0, :].set(summary_out)

def reference(tokens, token_counts, segment_project, segment_output, segment_up, segment_down, segment_scale, segment_offset, segment_gain, segment_shift, document_project, document_output, document_up, document_down, document_scale, document_offset, document_gain, document_shift, position, cotangent):
    weights = tuple((item.astype(jnp.float32) for item in (segment_project, segment_output, segment_up, segment_down, segment_scale, segment_offset, segment_gain, segment_shift, document_project, document_output, document_up, document_down, document_scale, document_offset, document_gain, document_shift, position)))
    count_documents = MB * DOCS
    all_tokens = tokens.astype(jnp.float32).reshape(count_documents, DOC_SEGS, SEG_LEN, D)
    all_counts = token_counts.reshape(count_documents, DOC_SEGS)
    all_cotangent = cotangent.astype(jnp.float32).reshape(count_documents, DOC_SEGS, SEG_LEN, D)

    def step(carry, item):
        part_tokens, part_counts, part_cotangent = item

        def forward(inner_tokens, inner_weights):
            return document(inner_tokens, part_counts, inner_weights)
        result, pullback = jax.vjp(forward, part_tokens, weights)
        delta_tokens, delta_weights = pullback(part_cotangent)
        carry = tuple((left + right for left, right in zip(carry, delta_weights)))
        return (carry, (result.astype(jnp.bfloat16), delta_tokens))
    start = tuple((jnp.zeros_like(item) for item in weights))
    totals, (results, delta_all) = lax.scan(step, start, (all_tokens, all_counts, all_cotangent))
    output = results.reshape(MB, SEGS, SEG_LEN, D)
    input_gradient = delta_all.reshape(MB, SEGS, SEG_LEN, D)
    return (output, input_gradient, totals[0], totals[1], totals[2], totals[3], totals[4], totals[5], totals[6], totals[7], totals[8], totals[9], totals[10], totals[11], totals[12], totals[13], totals[14], totals[15], totals[16])
```

```python
import math
import jax
import jax.numpy as jnp
from jax import lax
from jax.experimental import pallas as pl
from jax.experimental.pallas import tpu as pltpu
from jax.sharding import PartitionSpec as P

MESH = pl.DeviceIdType.MESH
F32 = jnp.float32
BF = jnp.bfloat16
HEADS = 12
DOC_SEGS = 32
epsilon = 1e-05
floor_score = -1e30
root_half = 1.0 / math.sqrt(2.0)
inverse_root_tau = 1.0 / math.sqrt(2.0 * math.pi)


class Spot:
    def __init__(self):
        s, c = lax.axis_index("seg"), lax.axis_index("rep")
        z, y, x = lax.div(s, 4), lax.rem(lax.div(s, 2), 2), lax.rem(s, 2)
        self.s, self.c, self.z = s, c, z
        self.o = 1 - c
        y1, x1 = y + c * (1 - 2 * y), x + (1 - c) * (1 - 2 * x)
        y2, x2 = y + (1 - c) * (1 - 2 * y), x + c * (1 - 2 * x)
        self.q = 2 * y + x
        self.q1 = 2 * y1 + x1
        self.q2 = 2 * y2 + x2
        self.q12 = 3 - self.q
        self.sib = (s, 1 - c)
        self.n1 = (4 * z + self.q1, c)
        self.n2 = (4 * z + self.q2, c)
        self.zz = [lax.rem(z + k, 4) for k in (1, 2, 3)]
        self.zn = [(4 * zz + self.q, c) for zz in self.zz]
        self.qq = [lax.rem(self.q + k, 4) for k in (0, 1, 2, 3)]
        self.plane = [(4 * z + qq, c) for qq in self.qq]
        self.half = lax.rem(z, 2)
        self.zo = z + 1 - 2 * self.half
        self.i = 8 * self.half + 2 * self.q + c
        self.dev = 2 * s + c


def remote(src, dst, ssem, rsem, dev):
    return pltpu.make_async_remote_copy(
        src_ref=src, dst_ref=dst, send_sem=ssem, recv_sem=rsem, device_id=dev, device_id_type=MESH
    )


def enter(t):
    bar = pltpu.get_barrier_semaphore()
    everyone = [t.sib]
    for k in range(4):
        for e in range(4):
            if k or e:
                s = 4 * lax.rem(t.z + k, 4) + lax.rem(t.q + e, 4)
                everyone += [(s, t.c), (s, t.o)]
    for dev in everyone:
        pl.semaphore_signal(bar, inc=1, device_id=dev, device_id_type=MESH)
    pl.semaphore_wait(bar, len(everyone))


class Sender:
    def __init__(self, t, ss, rs):
        self.t, self.ss, self.rs, self.pending = t, ss, rs, []

    def send(self, at, src, dst, dev):
        d = remote(src, dst, self.ss.at[at], self.rs.at[at], dev)
        d.start()
        self.pending.append(d)

    def arrived(self, at, ref):
        remote(ref, ref, self.ss.at[at], self.rs.at[at], self.t.sib).wait_recv()

    def drain(self):
        for d in self.pending:
            d.wait_send()
        self.pending = []


def off(at, size, step=128):
    return pl.ds(pl.multiple_of(at * size, step), size)


def join_pair(t, shard, got, tmp, dest):
    rd, n2 = got.shape
    wide = tmp.shape[1]
    for j in range(0, n2, wide):
        mine = pl.ds(pl.multiple_of(t.c * n2 + j, 128), wide)
        tmp[off(t.c, rd, 8), :] = shard[:, mine].astype(F32)
        tmp[off(t.o, rd, 8), :] = got[:, j : j + wide].astype(F32)
        dest[:, pl.ds(j, wide)] = tmp[...].astype(dest.dtype)


class Gather(Sender):
    def __init__(self, t, shard, w, got, tmp, windows, ss, rs):
        super().__init__(t, ss, rs)
        self.shard, self.w, self.got, self.tmp, self.windows = shard, w, got, tmp, windows

    def pair(self):
        n2 = self.got.shape[1]
        self.send((0, 0), self.shard.at[:, off(self.t.o, n2)], self.got, self.t.sib)

    def join(self):
        t = self.t
        self.arrived((0, 0), self.got)
        join_pair(t, self.shard, self.got, self.tmp, self.w.at[t.c, t.z, t.q])

    def pick(self, k, *lead):
        rows, cols = self.windows[k]
        return self.w.at[(self.t.c,) + lead + (pl.ds(*rows), pl.ds(*cols))]

    def line(self, k, q):
        return self.pick(k, slice(None), q)

    def spread(self, k):
        t = self.t
        own = self.pick(k, t.z, t.q)
        for dev in t.zn:
            self.send((k, 1), own, own, dev)

    def first(self, k):
        t = self.t
        self.arrived((k, 1), self.pick(k, pl.ds(0, 3), t.q))
        line = self.line(k, t.q)
        self.send((k, 2), line, line, t.n1)
        self.send((k, 4), line, line, t.sib)

    def second(self, k):
        t = self.t
        line, other = self.line(k, t.q), self.line(k, t.q1)
        self.arrived((k, 2), other)
        self.send((k, 3), line, line, t.n2)
        self.send((k, 7), other, other, t.n2)
        self.send((k, 5), other, other, t.sib)

    def third(self, k):
        t = self.t
        for i in (3, 7):
            self.arrived((k, i), self.line(k, t.q))
        for i, q in ((6, t.q2), (8, t.q12)):
            self.send((k, i), self.line(k, q), self.line(k, q), t.sib)

    def finish(self, k):
        for i in (4, 5, 6, 8):
            self.arrived((k, i), self.line(k, self.t.q))


class DocGather(Sender):
    def __init__(self, t, shards, stages, gots, tmps, dpu, do, dd, ss, rs, ls):
        super().__init__(t, ss, rs)
        self.shards, self.stages, self.gots, self.tmps = shards, stages, gots, tmps
        self.dpu, self.do, self.dd, self.ls = dpu, do, dd, ls

    def pair(self):
        for i in range(2):
            n2 = self.gots[i].shape[1]
            self.send(i, self.shards[i].at[:, off(self.t.o, n2)], self.gots[i], self.t.sib)

    def join(self):
        t = self.t
        for i in range(2):
            self.arrived(i, self.gots[i])
            join_pair(t, self.shards[i], self.gots[i], self.tmps[i], self.stages[i].at[t.z])

    def spread(self, i):
        own = self.stages[i].at[self.t.z]
        for dev in self.t.zn:
            self.send(2 + i, own, own, dev)

    def plane(self):
        t = self.t
        main, down = self.stages
        for i in range(2):
            self.arrived(2 + i, self.stages[i].at[pl.ds(0, 3)])
        self.local = []
        for k in (1, 2, 3, 0):
            q = t.qq[k]
            moves = (
                (main.at[:, :, off(q, 768)], self.dpu.at[t.c, :, t.q]),
                (main.at[q, :, pl.ds(3072, 384)], self.do.at[t.c, pl.ds(pl.multiple_of(48 * t.q, 16), 48)]),
                (down.at[q], self.dd.at[t.c, t.q]),
            )
            for i, (src, dst) in enumerate(moves):
                if k:
                    self.send(4 + i, src, dst, t.plane[k])
                else:
                    d = pltpu.make_async_copy(src, dst, self.ls.at[i])
                    d.start()
                    self.local.append(d)

    def share(self):
        t = self.t
        self.arrived(4, self.dpu.at[t.c, :, pl.ds(0, 3)])
        self.arrived(5, self.do.at[t.c, pl.ds(0, 144)])
        self.arrived(6, self.dd.at[t.c, pl.ds(0, 3)])
        for d in self.local:
            d.wait()
        for i, ref in enumerate((self.dpu, self.do, self.dd)):
            view = ref.at[t.c, pl.ds(0, 192)] if i == 1 else ref.at[t.c]
            self.send(7 + i, view, view, t.sib)

    def finish(self):
        for i, ref in enumerate((self.dpu, self.do, self.dd)):
            view = ref.at[self.t.o, pl.ds(0, 192)] if i == 1 else ref.at[self.t.o]
            self.arrived(7 + i, view)


class Reduce(Sender):
    def __init__(self, t, w, rc_, r1, r2, r3, fin, fin2, out, ss, rs):
        super().__init__(t, ss, rs)
        self.w, self.rc, self.r1, self.r2, self.r3 = w, rc_, r1, r2, r3
        self.fin, self.fin2, self.out = fin, fin2, out

    def pair(self):
        self.send(0, self.w.at[self.t.o], self.rc, self.t.sib)

    def add(self, q, part):
        w, c = self.w, self.t.c

        @pl.loop(0, 4)
        def _(z):
            w[c, z, q] = (w[c, z, q].astype(F32) + part[z].astype(F32)).astype(w.dtype)

    def first(self):
        t = self.t
        self.arrived(0, self.rc)
        for i, q in ((0, t.q2), (1, t.q12)):
            self.add(q, self.rc.at[:, q])
            self.send(1 + i, self.w.at[t.c, :, q], self.r1.at[i], t.n2)
        for q in (t.q, t.q1):
            self.add(q, self.rc.at[:, q])

    def second(self):
        t = self.t
        self.arrived(2, self.r1.at[1])
        self.add(t.q1, self.r1.at[1])
        self.send(3, self.w.at[t.c, :, t.q1], self.r2, t.n1)
        self.arrived(1, self.r1.at[0])
        self.add(t.q, self.r1.at[0])

    def third(self):
        t = self.t
        self.arrived(3, self.r2)
        self.add(t.q, self.r2)
        for k in range(3):
            self.send(4, self.w.at[t.c, t.zz[k], t.q], self.r3.at[2 - k], t.zn[k])

    def fourth(self):
        t = self.t
        self.arrived(4, self.r3)
        total = self.w[t.c, t.z, t.q].astype(F32)
        for k in range(3):
            total = total + self.r3[k].astype(F32)
        self.fin[...] = total
        rd = self.fin.shape[0] // 2
        self.send(5, self.fin.at[off(t.o, rd, 8)], self.fin2, t.sib)

    def fifth(self):
        t = self.t
        rd, n2 = self.fin2.shape
        self.arrived(5, self.fin2)
        self.out[:, off(t.c, n2)] = self.fin[off(t.c, rd, 8), :]
        self.out[:, off(t.o, n2)] = self.fin2[...]


def dot(a, b):
    return jnp.dot(a, b, preferred_element_type=F32)


def dot_rt(a, b):
    return lax.dot_general(a, b, (((1,), (1,)), ((), ())), preferred_element_type=F32)


def dot_lt(a, b):
    return lax.dot_general(a, b, (((0,), (0,)), ((), ())), preferred_element_type=F32)


def normed(v):
    centred = v - jnp.mean(v, axis=-1, keepdims=True)
    inverse = lax.rsqrt(jnp.mean(centred * centred, axis=-1, keepdims=True) + epsilon)
    return centred * inverse, inverse


def norm_back(g, n, inverse, gain):
    v = g * gain
    return inverse * (
        v - jnp.mean(v, axis=-1, keepdims=True) - n * jnp.mean(v * n, axis=-1, keepdims=True)
    )


def gelu_pair(v):
    share = 0.5 * (1.0 + lax.erf(v * root_half))
    return v * share, share + v * jnp.exp(-0.5 * v * v) * inverse_root_tau


SIZES = ((24, 128, F32), (24, 1152, BF), (24, 384, BF), (24, 1536, BF), (96, 384, BF))
WINDOWS = (
    [((0, 48), (0, 128))],
    [((0, 48), (384 * j, 384)) for j in range(3)],
    [((0, 48), (0, 384))],
    [((0, 48), (384 * j, 384)) for j in range(4)],
    [((48 * j, 48), (0, 384)) for j in range(4)],
)
SCRATCH = {
    "got": [((rd, n2), dt) for rd, n2, dt in SIZES] + [((24, 3456), BF), ((96, 384), BF)],
    "w": [((2, 4, 4, 2 * rd, n2), dt) for rd, n2, dt in SIZES],
    "fin": [((2 * rd, n2), F32) for rd, n2, dt in SIZES],
    "fin2": [((rd, n2), F32) for rd, n2, dt in SIZES],
    "rc": [((4, 4, 2 * rd, n2), dt) for rd, n2, dt in SIZES if n2 not in (1152, 384) or rd == 96],
    "r1": [((2, 4, 2 * rd, n2), dt) for rd, n2, dt in SIZES],
    "r2": [((4, 2 * rd, n2), dt) for rd, n2, dt in SIZES],
    "r3": [((3, 2 * rd, n2), dt) for rd, n2, dt in SIZES],
    "stage": [((4, 48, 3456), BF), ((4, 192, 384), BF)],
    "dpu": [((2, 4, 4, 48, 768), BF)],
    "do": [((2, 256, 384), BF)],
    "dd": [((2, 4, 192, 384), BF)],
    "vec": [((16, 768), F32)],
    "table": [((16, 2, 768), F32)],
    "pr": [((512, 2304), BF)],
    "ctx": [((512, 768), BF)],
    "sh": [((24, 256, 128), BF)],
    "n1": [((512, 768), BF)],
    "i1": [((512, 1), F32)],
    "n2": [((512, 768), BF)],
    "i2": [((512, 1), F32)],
    "fl": [((512, 768), BF)],
    "act": [((512, 3072), BF)],
    "gp": [((512, 3072), BF)],
    "row": [((512, 768), F32)],
    "low": [((512, 768), BF)],
    "ob": [((512, 768), BF)],
    "hid": [((256, 384), F32)],
    "src": [((2, 2, 768), F32)] * 2,
    "slots": [((16, 2, 768), F32)] * 4,
    "sdr": [((2, 4, 2, 768), F32)],
    "pairs": [((2, 2, 768), F32)] * 2,
    "soo": [((2, 768), F32)],
    "mat": [((32, 768), F32)] * 2,
    "ars": [((4, 32, 768), BF)],
    "arb": [((4, 3, 32, 768), BF)],
    "fq": [((2, 4, 4, 32, 1280), BF)],
    "fz": [((2, 4, 32, 1536), BF)],
    "vg": [((128, 768), F32)],
    "flip": [((768, 128), F32)],
}
SEMS = {
    "gs": (5, 4, 9),
    "gr": (5, 4, 9),
    "ds": (10,),
    "dr": (10,),
    "ls": (4,),
    "rs": (5, 6),
    "rr": (5, 6),
    "xs": (12,),
    "xr": (12,),
    "fs": (2, 9),
    "fr": (2, 9),
    "os": (8,),
}
INS = ("tok", "cot", "tmask", "dmask", "small", "sp", "so", "su", "sd", "dmain", "ddown")
OUTS = (
    ("out", (512, 768), BF),
    ("gin", (512, 768), F32),
    ("gsmall", (24, 256), F32),
    ("gsp", (24, 2304), F32),
    ("gso", (24, 768), F32),
    ("gsu", (24, 3072), F32),
    ("gsd", (96, 768), F32),
    ("gdp", (24, 3072), F32),
    ("gdo", (24, 768), F32),
    ("gdu", (24, 3072), F32),
    ("gdd", (96, 768), F32),
)


class Box:
    pass


def kernel(*refs):
    b = Box()
    refs = list(refs)

    def take(n):
        got, refs[:n] = refs[:n], []
        return got

    for name in INS:
        setattr(b, name, take(1)[0])
    for name, _, _ in OUTS:
        setattr(b, name, take(1)[0])
    for name, items in SCRATCH.items():
        got = take(len(items))
        setattr(b, name, got if len(got) > 1 else got[0])
    for name in SEMS:
        setattr(b, name, take(1)[0])
    b.credit = take(1)[0]
    b.t = Spot()
    run(b)


def run(b):
    t = b.t
    b.x = Sender(t, b.xs, b.xr)
    b.do[...] = jnp.zeros(b.do.shape, BF)
    b.vg[...] = jnp.zeros(b.vg.shape, F32)
    enter(t)
    shards = (b.small, b.sp, b.so, b.su, b.sd)
    gs = [
        Gather(t, shards[i], b.w[i], b.got[i], b.fin[i], WINDOWS[i], b.gs.at[i], b.gr.at[i])
        for i in range(5)
    ]
    dg = DocGather(
        t, (b.dmain, b.ddown), b.stage, b.got[5:], (b.fin[1], b.fin[4]), b.dpu, b.do, b.dd, b.ds, b.dr, b.ls
    )
    for g in gs[:2]:
        g.pair()
    for g in gs[2:]:
        g.pair()
    dg.pair()
    events = [(g, k) for g in gs for k in range(len(g.windows))]
    clock = [0]

    def do(name, at):
        if 0 <= at < len(events):
            getattr(events[at][0], name)(events[at][1])

    def tick(upto):
        while clock[0] <= upto:
            at = clock[0]
            do("first", at)
            do("spread", at + 2)
            if at + 2 == len(events):
                dg.spread(0)
                dg.spread(1)
            do("second", at - 1)
            do("third", at - 2)
            do("finish", at - 3)
            clock[0] += 1

    gs[0].join()
    gs[1].join()
    do("spread", 0)
    do("spread", 1)
    for g in gs[2:]:
        g.join()
    dg.join()
    send_cotangents(b)
    tick(3)
    vectors_in(b)
    tick(6)
    segment_project(b)
    for seg in range(4):
        attend(b, seg)
        tick(7 + seg // 2)
    segment_mix(b)
    tick(9)
    for j in range(4):
        segment_up(b, j)
        tick(10 + j)
    tick(14)
    dg.plane()
    tick(15)
    segment_down(b)
    send_summaries(b)
    dg.share()
    for g in gs:
        g.drain()
    dg.finish()
    dg.drain()
    document(b)
    finish_output(b)

    small_rc, up_rc, down_rc = b.rc
    rcs = (small_rc, up_rc.at[:, :, :, 0:1152], up_rc.at[:, :, :, 1152:1536], up_rc, down_rc)
    rs = [
        Reduce(t, b.w[i], rcs[i], b.r1[i], b.r2[i], b.r3[i], b.fin[i], b.fin2[i], out, b.rs.at[i], b.rr.at[i])
        for i, out in enumerate((b.gsmall, b.gsp, b.gso, b.gsu, b.gsd))
    ]
    rsmall, rproject, routput, rup, rdown = rs
    second_back(b)
    hidden_back(b)
    down_terms(b)
    rdown.pair()
    first_back(b)
    rdown.first()
    up_terms(b)
    rup.pair()
    mixed_back(b)
    rdown.second()
    output_terms(b)
    rup.first()
    pl.semaphore_signal(b.credit, inc=1, device_id=t.sib, device_id_type=MESH)
    pl.semaphore_wait(b.credit, 1)
    routput.pair()
    rdown.third()
    attend_back(b, 0)
    attend_back(b, 1)
    rup.second()
    routput.first()
    rdown.fourth()
    attend_back(b, 2)
    attend_back(b, 3)
    project_terms(b)
    rproject.pair()
    rup.third()
    routput.second()
    rdown.fifth()
    vectors_out(b)
    rsmall.pair()
    rproject.first()
    routput.third()
    rup.fourth()
    document_terms(b)
    rsmall.first()
    rproject.second()
    routput.fourth()
    rup.fifth()
    rsmall.second()
    rproject.third()
    routput.fifth()
    rsmall.third()
    rproject.fourth()
    rsmall.fourth()
    rproject.fifth()
    rsmall.fifth()
    for r in rs:
        r.drain()
    b.x.drain()
    for d in b.flying:
        d.wait()


def send_cotangents(b):
    for m in range(2):
        for s in range(2):
            rows = b.cot[pl.ds(128 * (2 * m + s), 16), :].astype(F32)
            b.src[0][m, s : s + 1, :] = rows[0:1]
    send_rows(b, 0)


def send_rows(b, n):
    t, src, slots = b.t, b.src[n], b.slots[n]
    mine = src.at[t.half]
    other = src.at[1 - t.half]
    for k in (1, 2, 3):
        b.x.send(n, mine, slots.at[t.i], t.plane[k])
    for k in (0, 1, 2, 3):
        b.x.send(n, mine, slots.at[t.i], (4 * t.z + t.qq[k], t.o))
        b.x.send(n, other, slots.at[t.i], (4 * t.zo + t.qq[k], t.c))
        b.x.send(n, other, slots.at[t.i], (4 * t.zo + t.qq[k], t.o))
    slots[t.i] = src[t.half]


def take_rows(b, n):
    slots = b.slots[n]
    b.x.arrived(n, slots.at[pl.ds(0, 15)])
    for i in range(16):
        b.mat[n][2 * i : 2 * i + 2, :] = slots[i]
    return b.mat[n][...]


def vectors_in(b):
    small = b.w[0]
    b.vec[...] = jnp.transpose(small[0].reshape(768, 128))[0:16]
    table = jnp.transpose(small[1].reshape(768, 128))[0:32]
    for i in range(16):
        b.table[i] = table[2 * i : 2 * i + 2]


def vec(b, i):
    return b.vec[i : i + 1, :]


def segment_project(b):
    w = b.w[1]

    @pl.loop(0, 6)
    def _(i):
        h, j = lax.div(i, 3), lax.rem(i, 3)
        part = w[h, :, :, :, off(j, 384)].reshape(768, 384)
        b.pr[:, off(i, 384)] = dot(b.tok[...], part).astype(BF)


def lane_masks():
    lane = lax.broadcasted_iota(jnp.int32, (1, 128), 1)
    low = (lane < 64).astype(F32)
    return low.astype(BF), (1.0 - low).astype(BF)


def attend(b, seg):
    low, high = lane_masks()
    keep = b.tmask[seg : seg + 1, :] > 0.0
    rows = pl.ds(128 * seg, 128)

    @pl.loop(0, 6)
    def _(p):
        q2 = b.pr[rows, off(p, 128)]
        k2 = b.pr[rows, off(p + 6, 128)]
        v2 = b.pr[rows, off(p + 12, 128)]
        qs = jnp.concatenate((q2 * low, q2 * high), axis=0)
        scores = jnp.where(keep, dot_rt(qs, k2) * 0.125, floor_score)
        raised = jnp.exp(scores - jnp.max(scores, axis=-1, keepdims=True))
        shares = (raised * (1.0 / jnp.sum(raised, axis=-1, keepdims=True))).astype(BF)
        b.sh[6 * seg + p] = shares
        both = dot(shares, v2)
        lane = lax.broadcasted_iota(jnp.int32, (128, 128), 1)
        b.ctx[rows, off(p, 128)] = jnp.where(lane < 64, both[:128], both[128:]).astype(BF)


def segment_mix(b):
    w = b.w[2]
    for r in range(2):
        rows = pl.ds(256 * r, 256)
        for h in range(2):
            b.row[rows, pl.ds(384 * h, 384)] = dot(b.ctx[rows, :], w[h].reshape(768, 384))
    scale, offset = vec(b, 0), vec(b, 1)

    @pl.loop(0, 16)
    def _(i):
        rows = off(i, 32, 32)
        n, inverse = normed(b.tok[rows, :].astype(F32) + b.row[rows, :])
        first = n * scale + offset
        b.n1[rows, :] = n.astype(BF)
        b.i1[rows, :] = inverse
        b.row[rows, :] = first
        b.fl[rows, :] = first.astype(BF)


def segment_up(b, j):
    w = b.w[3]
    for h, r in ((0, 0), (0, 1), (1, 0), (1, 1)):
        up = w[h, :, :, :, pl.ds(384 * j, 384)].reshape(768, 384)
        b.hid[...] = dot(b.fl[256 * r : 256 * r + 256, :], up)
        cols = pl.ds(1536 * h + 384 * j, 384)

        @pl.loop(0, 8)
        def _(i):
            rows = off(i + 8 * r, 32, 32)
            value, slope = gelu_pair(b.hid[off(i, 32, 32), :])
            b.act[rows, cols] = value.astype(BF)
            b.gp[rows, cols] = slope.astype(BF)


def segment_down(b):
    w = b.w[4]

    @pl.loop(0, 4)
    def _(i):
        h, r = lax.div(i, 2), lax.rem(i, 2)
        rows = off(r, 256, 256)
        b.row[rows, off(h, 384)] += dot(b.act[rows, :], w[h].reshape(3072, 384))

    gain, shift = vec(b, 2), vec(b, 3)

    @pl.loop(0, 16)
    def _(i):
        rows = off(i, 32, 32)
        n, inverse = normed(b.row[rows, :])
        b.n2[rows, :] = n.astype(BF)
        b.i2[rows, :] = inverse
        second = n * gain + shift
        b.row[rows, :] = second
        b.ob[rows, :] = second.astype(BF)


def send_summaries(b):
    t = b.t
    places = b.table[t.i]
    for m in range(2):
        for s in range(2):
            rows = b.row[pl.ds(128 * (2 * m + s), 8), :]
            b.src[1][m, s : s + 1, :] = rows[0:1] + places[s : s + 1]
    send_rows(b, 1)


def plane_sum(b, n, partial):
    t = b.t
    b.ars[n] = partial.astype(BF)
    for k in (1, 2, 3):
        b.x.send(2 + n, b.ars.at[n], b.arb.at[n, k - 1], t.plane[k])
    b.x.arrived(2 + n, b.arb.at[n])
    total = b.ars[n].astype(F32)
    for k in range(3):
        total = total + b.arb[n, k].astype(F32)
    return total


def document(b):
    t = b.t
    dp = b.dpu[0].reshape(768, 768)
    du = b.dpu[1].reshape(768, 768)
    lane = lax.broadcasted_iota(jnp.int32, (1, 256), 1)
    heads = [((lane >= 64 * h) & (lane < 64 * h + 64)).astype(F32).astype(BF) for h in range(3)]
    keep = b.dmask[...] > 0.0
    h_in = take_rows(b, 1)
    h_low = h_in.astype(BF)
    pr = dot(h_low, dp).astype(BF)
    q3, k3, v3 = pr[:, 0:256], pr[:, 256:512], pr[:, 512:768]
    qs = jnp.concatenate([q3 * m for m in heads], axis=0)
    scores = jnp.where(keep, dot_rt(qs, k3) * 0.125, floor_score)
    raised = jnp.exp(scores - jnp.max(scores, axis=-1, keepdims=True))
    shares = raised * (1.0 / jnp.sum(raised, axis=-1, keepdims=True))
    shares_low = shares.astype(BF)
    three = dot(shares_low, v3)
    ctx = sum(three[32 * h : 32 * h + 32] * heads[h].astype(F32) for h in range(3)).astype(BF)
    mixed = jnp.concatenate([dot(ctx, b.do[h]) for h in range(2)], axis=1)
    n1, i1 = normed(h_in + plane_sum(b, 0, mixed))
    first = n1 * vec(b, 4) + vec(b, 5)
    first_low = first.astype(BF)
    active, slope = gelu_pair(dot(first_low, du))
    active = active.astype(BF)
    branch = jnp.concatenate([dot(active, b.dd[h].reshape(768, 384)) for h in range(2)], axis=1)
    n2, i2 = normed(first + plane_sum(b, 1, branch))
    out = n2 * vec(b, 6) + vec(b, 7)
    for i in range(16):
        b.slots[2][i] = out[2 * i : 2 * i + 2]
    other_i = 8 * (1 - t.half) + 2 * t.q + t.c
    b.x.send(6, b.slots[2].at[other_i], b.soo, (4 * t.zo + t.q, t.c))

    g = take_rows(b, 0)
    b.vg[6:7, :] = jnp.sum(g * n2, axis=0, keepdims=True) * 0.125
    b.vg[7:8, :] = jnp.sum(g, axis=0, keepdims=True) * 0.125
    delta = norm_back(g, n2, i2, vec(b, 6))
    branch_low = delta.astype(BF)
    back = sum(dot_rt(branch_low[:, 384 * h : 384 * h + 384], b.dd[h].reshape(768, 384)) for h in range(2))
    hidden_delta = (back * slope).astype(BF)
    first_delta = delta + plane_sum(b, 2, dot_rt(hidden_delta, du))
    b.vg[4:5, :] = jnp.sum(first_delta * n1, axis=0, keepdims=True) * 0.125
    b.vg[5:6, :] = jnp.sum(first_delta, axis=0, keepdims=True) * 0.125
    mixed_delta = norm_back(first_delta, n1, i1, vec(b, 4))
    mixed_low = mixed_delta.astype(BF)
    ctx_delta = sum(dot_rt(mixed_low[:, 384 * h : 384 * h + 384], b.do[h]) for h in range(2)).astype(BF)
    cs = jnp.concatenate([ctx_delta * m for m in heads], axis=0)
    shares_delta = dot_rt(cs, v3)
    inner = jnp.sum(shares_delta * shares, axis=-1, keepdims=True)
    scores_delta = (shares * (shares_delta - inner)).astype(BF)
    dq3 = dot(scores_delta, k3) * 0.125
    dq = sum(dq3[32 * h : 32 * h + 32] * heads[h].astype(F32) for h in range(3))
    dk = dot_lt(scores_delta, qs) * 0.125
    dv = dot_lt(shares_low, cs)
    pd = jnp.concatenate((dq, dk, dv), axis=1).astype(BF)
    h_delta = dot_rt(pd, dp) + 0.25 * mixed_delta
    for i in range(16):
        b.slots[3][i] = h_delta[2 * i : 2 * i + 2]
    for k in (0, 1, 2, 3):
        if k:
            b.x.send(7, b.slots[3].at[8 * t.half + 2 * t.qq[k] + t.c], b.sdr.at[0, k], t.plane[k])
        b.x.send(
            8, b.slots[3].at[8 * (1 - t.half) + 2 * t.qq[k] + t.c], b.sdr.at[1, k], (4 * t.zo + t.qq[k], t.c)
        )
    b.sdr[0, 0] = b.slots[3][t.i]

    @pl.when(t.c == 0)
    def _():
        b.fq[0, t.z, t.q, :, 0:768] = pd
        b.fq[0, t.z, t.q, :, 768:1024] = ctx
        b.fq[0, t.z, t.q, :, 1024:1280] = active[:, 0:256]
        b.fz[0, t.z, :, 0:768] = h_low
        b.fz[0, t.z, :, 768:1536] = mixed_low

    @pl.when(t.c == 1)
    def _():
        b.fq[1, t.z, t.q, :, 0:768] = hidden_delta
        b.fq[1, t.z, t.q, :, 768:1280] = active[:, 256:768]
        b.fz[1, t.z, :, 0:768] = first_low
        b.fz[1, t.z, :, 768:1536] = branch_low

    b.f = Gather(t, None, b.fq, None, None, [((0, 32), (0, 1280))], b.fs, b.fr)
    b.f.spread(0)
    for dev in t.zn:
        b.f.send((1, 0), b.fz.at[t.c, t.z], b.fz.at[t.c, t.z], dev)
    b.x.arrived(6, b.soo)
    b.pairs[0][t.half] = b.slots[2][t.i]
    b.pairs[0][1 - t.half] = b.soo[...]
    b.x.arrived(7, b.sdr.at[0, pl.ds(0, 3)])
    b.x.arrived(8, b.sdr.at[1])
    b.pairs[1][t.half] = b.sdr[0, 0] + b.sdr[0, 1] + b.sdr[0, 2] + b.sdr[0, 3]
    b.pairs[1][1 - t.half] = b.sdr[1, 0] + b.sdr[1, 1] + b.sdr[1, 2] + b.sdr[1, 3]
    b.f.first(0)
    b.f.arrived((1, 0), b.fz.at[t.c, pl.ds(0, 3)])
    b.f.send((1, 1), b.fz.at[t.c], b.fz.at[t.c], t.sib)
    b.f.second(0)


def finish_output(b):
    first_row = lax.broadcasted_iota(jnp.int32, (16, 768), 0) == 0
    for m in range(2):
        for s in range(2):
            rows = pl.ds(128 * (2 * m + s), 16)
            fresh = jnp.where(first_row, b.pairs[0][m, s : s + 1, :], b.ob[rows, :].astype(F32))
            b.ob[rows, :] = fresh.astype(BF)
    d = pltpu.make_async_copy(b.ob, b.out, b.os.at[0])
    d.start()
    b.flying = [d]


def second_back(b):
    gain = vec(b, 2)

    def body(i, carry):
        gains, shifts = carry
        rows = off(i, 16, 16)
        seg = lax.div(i, 8)
        fresh = (lax.broadcasted_iota(jnp.int32, (16, 768), 0) + 16 * lax.rem(i, 8)) == 0
        own = b.pairs[1][lax.div(seg, 2)]
        own = jnp.where(lax.rem(seg, 2) == 0, own[0:1], own[1:2])
        g = jnp.where(fresh, own, b.cot[rows, :].astype(F32))
        n = b.n2[rows, :].astype(F32)
        delta = norm_back(g, n, b.i2[rows, :], gain)
        b.row[rows, :] = delta
        b.low[rows, :] = delta.astype(BF)
        return gains + g * n, shifts + g

    zero = jnp.zeros((16, 768), F32)
    gains, shifts = lax.fori_loop(0, 32, body, (zero, zero))
    b.vg[2:3, :] = jnp.sum(gains, axis=0, keepdims=True)
    b.vg[3:4, :] = jnp.sum(shifts, axis=0, keepdims=True)


def hidden_back(b):
    w = b.w[4]

    @pl.loop(0, 4)
    def _(z):
        cols = off(z, 768)
        for r in range(2):
            rows = pl.ds(256 * r, 256)
            back = dot_rt(b.low[rows, 0:384], w[0, z].reshape(768, 384)) + dot_rt(
                b.low[rows, 384:768], w[1, z].reshape(768, 384)
            )
            b.gp[rows, cols] = (back * b.gp[rows, cols].astype(F32)).astype(BF)


def down_terms(b):
    w = b.w[4]

    @pl.loop(0, 4)
    def _(z):
        a = b.act[:, off(z, 768)]
        for h in range(2):
            w[h, z] = dot_lt(a, b.low[:, 384 * h : 384 * h + 384]).astype(BF).reshape(4, 192, 384)


def first_back(b):
    w = b.w[3]

    @pl.loop(0, 2)
    def _(r):
        rows = off(r, 256, 256)
        for h in range(2):
            b.row[rows, :] += dot_rt(b.gp[rows, 1536 * h : 1536 * h + 1536], w[h].reshape(768, 1536))


def up_terms(b):
    w = b.w[3]

    @pl.loop(0, 8)
    def _(i):
        h, j = lax.div(i, 4), lax.rem(i, 4)
        part = dot_lt(b.fl[...], b.gp[:, off(i, 384)])
        w[h, :, :, :, off(j, 384)] = part.astype(BF).reshape(4, 4, 48, 384)


def mixed_back(b):
    scale = vec(b, 0)

    def body(i, carry):
        scales, offsets = carry
        rows = off(i, 16, 16)
        g = b.row[rows, :]
        n = b.n1[rows, :].astype(F32)
        delta = norm_back(g, n, b.i1[rows, :], scale)
        b.row[rows, :] = delta
        b.low[rows, :] = delta.astype(BF)
        return scales + g * n, offsets + g

    zero = jnp.zeros((16, 768), F32)
    scales, offsets = lax.fori_loop(0, 32, body, (zero, zero))
    b.vg[0:1, :] = jnp.sum(scales, axis=0, keepdims=True)
    b.vg[1:2, :] = jnp.sum(offsets, axis=0, keepdims=True)


def output_terms(b):
    w = b.w[2]
    b.flying[0].wait()
    b.flying = []
    for r in range(2):
        rows = pl.ds(256 * r, 256)
        back = dot_rt(b.low[rows, 0:384], w[0].reshape(768, 384)) + dot_rt(
            b.low[rows, 384:768], w[1].reshape(768, 384)
        )
        b.ob[rows, :] = back.astype(BF)
    for h in range(2):
        w[h] = dot_lt(b.ctx[...], b.low[:, 384 * h : 384 * h + 384]).astype(BF).reshape(4, 4, 48, 384)


def attend_back(b, seg):
    low, high = lane_masks()
    rows = pl.ds(128 * seg, 128)

    @pl.loop(0, 6)
    def _(p):
        q2 = b.pr[rows, off(p, 128)]
        k2 = b.pr[rows, off(p + 6, 128)]
        v2 = b.pr[rows, off(p + 12, 128)]
        d2 = b.ob[rows, off(p, 128)]
        qs = jnp.concatenate((q2 * low, q2 * high), axis=0)
        cs = jnp.concatenate((d2 * low, d2 * high), axis=0)
        shares_low = b.sh[6 * seg + p]
        shares = shares_low.astype(F32)
        shares_delta = dot_rt(cs, v2)
        inner = jnp.sum(shares_delta * shares, axis=-1, keepdims=True)
        scores_delta = (shares * (shares_delta - inner)).astype(BF)
        dq = dot(scores_delta, k2) * 0.125
        lane = lax.broadcasted_iota(jnp.int32, (128, 128), 1)
        b.pr[rows, off(p, 128)] = jnp.where(lane < 64, dq[:128], dq[128:]).astype(BF)
        b.pr[rows, off(p + 6, 128)] = (dot_lt(scores_delta, qs) * 0.125).astype(BF)
        b.pr[rows, off(p + 12, 128)] = dot_lt(shares_low, cs).astype(BF)


def project_terms(b):
    w = b.w[1]

    @pl.loop(0, 2)
    def _(r):
        rows = off(r, 256, 256)
        for h in range(2):
            b.row[rows, :] += dot_rt(b.pr[rows, 1152 * h : 1152 * h + 1152], w[h].reshape(768, 1152))

    d = pltpu.make_async_copy(b.row, b.gin, b.os.at[1])
    d.start()
    b.flying = [d]

    @pl.loop(0, 6)
    def _(i):
        h, j = lax.div(i, 3), lax.rem(i, 3)
        part = dot_lt(b.tok[...], b.pr[:, off(i, 384)])
        w[h, :, :, :, off(j, 384)] = part.astype(BF).reshape(4, 4, 48, 384)


def vectors_out(b):
    t, w = b.t, b.w[0]
    w[0] = jnp.transpose(b.vg[...]).reshape(4, 4, 48, 128)
    row = lax.broadcasted_iota(jnp.int32, (32, 768), 0)
    both = b.pairs[1][0] + b.pairs[1][1]
    places = jnp.where(row == 2 * t.i, both[0:1], 0.0) + jnp.where(row == 2 * t.i + 1, both[1:2], 0.0)
    b.vg[0:32, :] = places
    w[1] = jnp.transpose(b.vg[...]).reshape(4, 4, 48, 128)


def document_terms(b):
    t = b.t
    b.f.third(0)
    b.f.finish(0)
    b.f.arrived((1, 1), b.fz.at[t.o])
    b.f.drain()
    own = 24 * t.dev
    part = 24 * lax.rem(t.dev, 8)

    def rows_of(value, at, size):
        n = value.shape[1]
        b.flip[0:n, :] = jnp.transpose(value.astype(F32))
        return b.flip[pl.ds(pl.multiple_of(at, 8), size), :].astype(BF)

    left = rows_of(b.fz[0, :, :, 0:768].reshape(128, 768), own, 24)
    for q in range(4):
        b.gdp[:, 768 * q : 768 * q + 768] = dot(left, b.fq[0, :, q, :, 0:768].reshape(128, 768))
    left = rows_of(b.fq[0, :, t.z, :, 768:1024].reshape(128, 256), part, 24)
    b.gdo[...] = dot(left, b.fz[0, :, :, 768:1536].reshape(128, 768))
    left = rows_of(b.fz[1, :, :, 0:768].reshape(128, 768), own, 24)
    for q in range(4):
        b.gdu[:, 768 * q : 768 * q + 768] = dot(left, b.fq[1, :, q, :, 0:768].reshape(128, 768))
    active = jnp.concatenate((b.fq[0, :, t.z, :, 1024:1280], b.fq[1, :, t.z, :, 768:1280]), axis=-1)
    left = rows_of(active.reshape(128, 768), 4 * part, 96)
    b.gdd[...] = dot(left, b.fz[1, :, :, 768:1536].reshape(128, 768))


def mega(*arrays):
    vm = pl.BlockSpec(memory_space=pltpu.VMEM)
    an = pl.BlockSpec(memory_space=pl.ANY)
    return pl.pallas_call(
        kernel,
        out_shape=[jax.ShapeDtypeStruct(shape, dt) for _, shape, dt in OUTS],
        in_specs=[vm] * len(INS),
        out_specs=[an, an] + [vm] * (len(OUTS) - 2),
        scratch_shapes=[pltpu.VMEM(shape, dt) for items in SCRATCH.values() for shape, dt in items]
        + [pltpu.SemaphoreType.DMA(shape) for shape in SEMS.values()]
        + [pltpu.SemaphoreType.REGULAR],
        compiler_params=pltpu.CompilerParams(
            collective_id=1, has_side_effects=True, vmem_limit_bytes=65200 * 1024
        ),
    )(*arrays)


def local_fast(tokens, token_counts, *rest):
    weights, cotangent = rest[:17], rest[17]
    batches, segments, length, width = tokens.shape
    device = lax.axis_index("seg") * 2 + lax.axis_index("rep")
    own = lax.dynamic_slice(token_counts, (0, device * segments), (batches, segments)).reshape(-1)
    slots = jnp.arange(length)
    tmask = ((slots[None] < own[:, None]) | (slots[None] == 0)).astype(F32)
    z = lax.div(lax.axis_index("seg"), 4)
    doc = lax.dynamic_slice(
        token_counts, (lax.rem(z, 2), lax.div(z, 2) * DOC_SEGS), (1, DOC_SEGS)
    )
    dmask = (doc > 0).astype(F32)
    rows = weights[0].shape[0]
    vectors = jnp.stack([weights[i] for i in (4, 5, 6, 7, 12, 13, 14, 15)], axis=1)
    small = jnp.concatenate(
        (
            vectors,
            jnp.zeros((rows, 120), BF),
            weights[16],
            jnp.zeros((rows, 96), BF),
        ),
        axis=1,
    ).astype(F32)
    project = jnp.pad(weights[8].reshape(rows, 3, 4, 192), ((0, 0), (0, 0), (0, 0), (0, 64)))
    project = jnp.transpose(project, (0, 2, 1, 3)).reshape(rows, 3072)
    dmain = jnp.concatenate((project, weights[9][:, :384], weights[10], weights[9][:, 384:]), axis=1)
    outs = mega(
        tokens.reshape(-1, width),
        cotangent.reshape(-1, width),
        tmask,
        dmask,
        small,
        *weights[:4],
        dmain,
        weights[11],
    )
    out, gin, gsmall, gsp, gso, gsu, gsd, gdp, gdo, gdu, gdd = outs
    gdp = gdp.reshape(rows, 4, 3, 256)[:, :, :, :192]
    gdp = jnp.transpose(gdp, (0, 2, 1, 3)).reshape(rows, 2304)
    return (
        (out.reshape(tokens.shape), gin.reshape(tokens.shape), gsp, gso, gsu, gsd)
        + tuple(gsmall[:, i] for i in range(4))
        + (gdp, gdo, gdu, gdd)
        + tuple(gsmall[:, i] for i in range(4, 8))
        + (gsmall[:, 128:160],)
    )


def partner_2(value, axis, distance):
    mask = 2**distance
    pairs = [(source, source ^ mask) for source in range(lax.axis_size(axis))]
    return lax.ppermute(value, axis, pairs)


def product(left, right):
    return jnp.dot(left, right, preferred_element_type=jnp.float32)


def left_product(left, right):
    return lax.dot_general(
        left, right, (((0,), (0,)), ((), ())), preferred_element_type=jnp.float32
    )


def right_product(left, right):
    return lax.dot_general(
        left, right, (((1,), (1,)), ((), ())), preferred_element_type=jnp.float32
    )


def gelu_value(value):
    return 0.5 * value * (1.0 + lax.erf(value * root_half))


def gelu_slope(value):
    return (
        0.5 * (1.0 + lax.erf(value * root_half))
        + value * jnp.exp(-0.5 * value * value) * inverse_root_tau
    )


def norm_forward(value, gain, shift):
    centred = value - jnp.mean(value, axis=-1, keepdims=True)
    inverse = lax.rsqrt(jnp.mean(centred * centred, axis=-1, keepdims=True) + epsilon)
    normed = centred * inverse
    return (normed * gain + shift, normed, inverse)


def norm_backward(delta_out, normed, inverse, gain):
    scaled = delta_out * gain
    delta_in = inverse * (
        scaled
        - jnp.mean(scaled, axis=-1, keepdims=True)
        - normed * jnp.mean(scaled * normed, axis=-1, keepdims=True)
    )
    return (delta_in, jnp.sum(delta_out * normed, axis=0), jnp.sum(delta_out, axis=0))


def masked_scores(queries, keys, valid):
    scale = 1.0 / math.sqrt(queries.shape[-1])
    scores = (
        jnp.einsum("bqhe,bkhe->bhqk", queries, keys, preferred_element_type=jnp.float32) * scale
    )
    return jnp.where(valid[:, None], scores, floor_score)


def attend_forward(queries, keys, values, valid):
    scores = masked_scores(queries, keys, valid)
    highest = jnp.max(scores, axis=-1, keepdims=True)
    log_total = highest + jnp.log(jnp.sum(jnp.exp(scores - highest), axis=-1, keepdims=True))
    shares = jnp.exp(scores - log_total).astype(jnp.bfloat16)
    context = jnp.einsum("bhqk,bkhe->bqhe", shares, values, preferred_element_type=jnp.float32)
    return (context.astype(jnp.bfloat16), log_total)


def attend_backward(delta_context, queries, keys, values, valid, log_total):
    scale = 1.0 / math.sqrt(queries.shape[-1])
    shares = jnp.exp(masked_scores(queries, keys, valid) - log_total)
    delta_shares = jnp.einsum(
        "bqhe,bkhe->bhqk", delta_context, values, preferred_element_type=jnp.float32
    )
    delta_values = jnp.einsum(
        "bhqk,bqhe->bkhe",
        shares.astype(jnp.bfloat16),
        delta_context,
        preferred_element_type=jnp.float32,
    )
    inner = jnp.sum(delta_shares * shares, axis=-1, keepdims=True)
    delta_scores = (shares * (delta_shares - inner)).astype(jnp.bfloat16)
    delta_queries = (
        jnp.einsum("bhqk,bkhe->bqhe", delta_scores, keys, preferred_element_type=jnp.float32)
        * scale
    )
    delta_keys = (
        jnp.einsum("bhqk,bqhe->bkhe", delta_scores, queries, preferred_element_type=jnp.float32)
        * scale
    )
    return (delta_queries, delta_keys, delta_values)


def block_forward(inputs, layer, attend):
    (
        project_weight,
        output_weight,
        up_weight,
        down_weight,
        first_gain,
        first_shift,
        second_gain,
        second_shift,
    ) = layer
    inputs_low = inputs.astype(jnp.bfloat16)
    projected = product(inputs_low, project_weight).astype(jnp.bfloat16)
    context, attend_kept = attend(projected)
    mixed = product(context, output_weight)
    first, first_normed, first_inverse = norm_forward(
        inputs + mixed, first_gain.astype(jnp.float32), first_shift.astype(jnp.float32)
    )
    first_low = first.astype(jnp.bfloat16)
    hidden = product(first_low, up_weight)
    active = gelu_value(hidden).astype(jnp.bfloat16)
    second, second_normed, second_inverse = norm_forward(
        first + product(active, down_weight),
        second_gain.astype(jnp.float32),
        second_shift.astype(jnp.float32),
    )
    kept = (
        inputs_low,
        projected,
        context,
        attend_kept,
        first_normed,
        first_inverse,
        first_low,
        hidden,
        active,
        second_normed,
        second_inverse,
    )
    return (second, kept)


def block_backward(delta_out, kept, layer, attend_back):
    (
        project_weight,
        output_weight,
        up_weight,
        down_weight,
        first_gain,
        first_shift,
        second_gain,
        second_shift,
    ) = layer
    (
        inputs_low,
        projected,
        context,
        attend_kept,
        first_normed,
        first_inverse,
        first_low,
        hidden,
        active,
        second_normed,
        second_inverse,
    ) = kept
    delta_second, second_gain_delta, second_shift_delta = norm_backward(
        delta_out, second_normed, second_inverse, second_gain.astype(jnp.float32)
    )
    branch_low = delta_second.astype(jnp.bfloat16)
    delta_down = left_product(active, branch_low)
    delta_hidden = (right_product(branch_low, down_weight) * gelu_slope(hidden)).astype(
        jnp.bfloat16
    )
    delta_up = left_product(first_low, delta_hidden)
    delta_first = delta_second + right_product(delta_hidden, up_weight)
    delta_mixed, first_gain_delta, first_shift_delta = norm_backward(
        delta_first, first_normed, first_inverse, first_gain.astype(jnp.float32)
    )
    mixed_low = delta_mixed.astype(jnp.bfloat16)
    delta_output = left_product(context, mixed_low)
    delta_context = right_product(mixed_low, output_weight).astype(jnp.bfloat16)
    delta_projected = attend_back(delta_context, projected, attend_kept)
    delta_project = left_product(inputs_low, delta_projected)
    delta_inputs = delta_mixed + right_product(delta_projected, project_weight)
    return (
        delta_inputs,
        (
            delta_project,
            delta_output,
            delta_up,
            delta_down,
            first_gain_delta,
            first_shift_delta,
            second_gain_delta,
            second_shift_delta,
        ),
    )


def local(
    tokens,
    token_counts,
    segment_project,
    segment_output,
    segment_up,
    segment_down,
    segment_scale,
    segment_offset,
    segment_gain,
    segment_shift,
    document_project,
    document_output,
    document_up,
    document_down,
    document_scale,
    document_offset,
    document_gain,
    document_shift,
    position,
    cotangent,
):
    batches, segments, length, width = tokens.shape
    heads = HEADS
    head_width = width // heads
    rows_total = segments * length
    index = lax.axis_index(("seg", "rep"))
    first_segment = index * segments
    own_document = first_segment // DOC_SEGS
    positions = jnp.arange(length)
    slots = (first_segment + jnp.arange(segments)) % DOC_SEGS
    picker = (slots[:, None] == jnp.arange(DOC_SEGS)[None, :]).astype(jnp.float32)
    levels = (DOC_SEGS // segments).bit_length() - 1
    gathered_once = (
        lax.all_gather(segment_project, ("seg", "rep"), axis=0, tiled=True),
        lax.all_gather(segment_output, ("seg", "rep"), axis=0, tiled=True),
        lax.all_gather(segment_up, ("seg", "rep"), axis=0, tiled=True),
        lax.all_gather(segment_down, ("seg", "rep"), axis=0, tiled=True),
        lax.all_gather(segment_scale, ("seg", "rep"), axis=0, tiled=True),
        lax.all_gather(segment_offset, ("seg", "rep"), axis=0, tiled=True),
        lax.all_gather(segment_gain, ("seg", "rep"), axis=0, tiled=True),
        lax.all_gather(segment_shift, ("seg", "rep"), axis=0, tiled=True),
        lax.all_gather(document_project, ("seg", "rep"), axis=0, tiled=True),
        lax.all_gather(document_output, ("seg", "rep"), axis=0, tiled=True),
        lax.all_gather(document_up, ("seg", "rep"), axis=0, tiled=True),
        lax.all_gather(document_down, ("seg", "rep"), axis=0, tiled=True),
        lax.all_gather(document_scale, ("seg", "rep"), axis=0, tiled=True),
        lax.all_gather(document_offset, ("seg", "rep"), axis=0, tiled=True),
        lax.all_gather(document_gain, ("seg", "rep"), axis=0, tiled=True),
        lax.all_gather(document_shift, ("seg", "rep"), axis=0, tiled=True),
        lax.all_gather(position, ("seg", "rep"), axis=0, tiled=True),
    )
    outputs = []
    deltas = []
    totals = None
    for batch in range(batches):
        segment_layer = gathered_once[0:8]
        document_layer = gathered_once[8:16]
        table = jnp.transpose(gathered_once[16].astype(jnp.float32))
        counts_row = token_counts[batch]
        local_counts = lax.dynamic_slice_in_dim(counts_row, first_segment, segments)
        token_valid = (positions[None, :] < local_counts[:, None]) | (positions[None, :] == 0)
        segment_valid = token_valid[:, None, :]

        def segment_attend(projected):
            parts = projected.reshape(segments, length, 3, heads, head_width)
            context, log_total = attend_forward(
                parts[:, :, 0], parts[:, :, 1], parts[:, :, 2], segment_valid
            )
            return (context.reshape(rows_total, width), log_total)

        def segment_back(delta_context, projected, log_total):
            parts = projected.reshape(segments, length, 3, heads, head_width)
            delta_queries, delta_keys, delta_values = attend_backward(
                delta_context.reshape(segments, length, heads, head_width),
                parts[:, :, 0],
                parts[:, :, 1],
                parts[:, :, 2],
                segment_valid,
                log_total,
            )
            return (
                jnp.stack((delta_queries, delta_keys, delta_values), axis=2)
                .reshape(rows_total, 3 * width)
                .astype(jnp.bfloat16)
            )

        def document_attend(projected):
            queries = projected[:, :width].reshape(1, segments, heads, head_width)
            pairs = projected[:, width:]
            collected = pairs[None]
            for bit in range(levels):
                partner = partner_2(collected, ("seg", "rep"), bit)
                upper = jnp.right_shift(index, bit) % 2
                collected = jnp.where(
                    upper == 0,
                    jnp.concatenate((collected, partner), axis=0),
                    jnp.concatenate((partner, collected), axis=0),
                )
            collected = collected.reshape(DOC_SEGS, 2 * width)
            key_valid = lax.dynamic_slice_in_dim(counts_row, own_document * DOC_SEGS, DOC_SEGS) > 0
            keys = collected[:, :width].reshape(1, DOC_SEGS, heads, head_width)
            values = collected[:, width:].reshape(1, DOC_SEGS, heads, head_width)
            valid = key_valid[None, None, :]
            context, log_total = attend_forward(queries, keys, values, valid)
            return (context.reshape(segments, width), (collected, valid, log_total))

        def document_back(delta_context, projected, kept_rows):
            collected, valid, log_total = kept_rows
            queries = projected[:, :width].reshape(1, segments, heads, head_width)
            keys = collected[:, :width].reshape(1, DOC_SEGS, heads, head_width)
            values = collected[:, width:].reshape(1, DOC_SEGS, heads, head_width)
            delta_queries, delta_keys, delta_values = attend_backward(
                delta_context.reshape(1, segments, heads, head_width),
                queries,
                keys,
                values,
                valid,
                log_total,
            )
            delta_pairs = jnp.concatenate(
                (delta_keys.reshape(DOC_SEGS, width), delta_values.reshape(DOC_SEGS, width)), axis=1
            )
            folded = delta_pairs.reshape(DOC_SEGS // segments, segments, 2 * width)
            for bit in reversed(range(levels)):
                halves = folded.reshape(2, folded.shape[0] // 2, segments, 2 * width)
                upper = jnp.right_shift(index, bit) % 2
                keep = jnp.where(upper == 0, halves[0], halves[1])
                send = jnp.where(upper == 0, halves[1], halves[0])
                folded = keep + partner_2(send.astype(jnp.bfloat16), ("seg", "rep"), bit).astype(
                    send.dtype
                )
            own_pairs = folded.reshape(segments, 2 * width)
            return jnp.concatenate(
                (delta_queries.reshape(segments, width), own_pairs), axis=1
            ).astype(jnp.bfloat16)

        inputs = tokens[batch].astype(jnp.float32).reshape(rows_total, width)
        segment_rows, segment_kept = block_forward(inputs, segment_layer, segment_attend)
        segment_rows = segment_rows.reshape(segments, length, width)
        lookup = jnp.sum(picker[:, :, None] * table[None, :, :], axis=1)
        summary_rows = segment_rows[:, 0, :] + lookup
        summary_out, document_kept = block_forward(summary_rows, document_layer, document_attend)
        outputs.append(segment_rows.at[:, 0, :].set(summary_out).astype(jnp.bfloat16))
        incoming = cotangent[batch].astype(jnp.float32)
        delta_summary, document_deltas = block_backward(
            incoming[:, 0, :], document_kept, document_layer, document_back
        )
        delta_table = jnp.transpose(jnp.sum(picker[:, :, None] * delta_summary[:, None, :], axis=0))
        delta_rows = incoming.at[:, 0, :].set(delta_summary).reshape(rows_total, width)
        delta_inputs, segment_deltas = block_backward(
            delta_rows, segment_kept, segment_layer, segment_back
        )
        deltas.append(delta_inputs.reshape(segments, length, width))
        current = segment_deltas + document_deltas + (delta_table,)
        totals = (
            current
            if totals is None
            else tuple((left + right for left, right in zip(totals, current)))
        )
    groups = lax.axis_size("seg")
    shaped = tuple(
        (item.reshape((groups, item.shape[0] // groups) + item.shape[1:]) for item in totals)
    )
    received = (
        lax.all_to_all(
            shaped[0].astype(jnp.bfloat16), "seg", split_axis=0, concat_axis=0, tiled=True
        ).astype(jnp.float32),
        lax.all_to_all(
            shaped[1].astype(jnp.bfloat16), "seg", split_axis=0, concat_axis=0, tiled=True
        ).astype(jnp.float32),
        lax.all_to_all(
            shaped[2].astype(jnp.bfloat16), "seg", split_axis=0, concat_axis=0, tiled=True
        ).astype(jnp.float32),
        lax.all_to_all(
            shaped[3].astype(jnp.bfloat16), "seg", split_axis=0, concat_axis=0, tiled=True
        ).astype(jnp.float32),
        lax.all_to_all(
            shaped[4].astype(jnp.bfloat16), "seg", split_axis=0, concat_axis=0, tiled=True
        ).astype(jnp.float32),
        lax.all_to_all(
            shaped[5].astype(jnp.bfloat16), "seg", split_axis=0, concat_axis=0, tiled=True
        ).astype(jnp.float32),
        lax.all_to_all(
            shaped[6].astype(jnp.bfloat16), "seg", split_axis=0, concat_axis=0, tiled=True
        ).astype(jnp.float32),
        lax.all_to_all(
            shaped[7].astype(jnp.bfloat16), "seg", split_axis=0, concat_axis=0, tiled=True
        ).astype(jnp.float32),
        lax.all_to_all(
            shaped[8].astype(jnp.bfloat16), "seg", split_axis=0, concat_axis=0, tiled=True
        ).astype(jnp.float32),
        lax.all_to_all(
            shaped[9].astype(jnp.bfloat16), "seg", split_axis=0, concat_axis=0, tiled=True
        ).astype(jnp.float32),
        lax.all_to_all(
            shaped[10].astype(jnp.bfloat16), "seg", split_axis=0, concat_axis=0, tiled=True
        ).astype(jnp.float32),
        lax.all_to_all(
            shaped[11].astype(jnp.bfloat16), "seg", split_axis=0, concat_axis=0, tiled=True
        ).astype(jnp.float32),
        lax.all_to_all(
            shaped[12].astype(jnp.bfloat16), "seg", split_axis=0, concat_axis=0, tiled=True
        ).astype(jnp.float32),
        lax.all_to_all(
            shaped[13].astype(jnp.bfloat16), "seg", split_axis=0, concat_axis=0, tiled=True
        ).astype(jnp.float32),
        lax.all_to_all(
            shaped[14].astype(jnp.bfloat16), "seg", split_axis=0, concat_axis=0, tiled=True
        ).astype(jnp.float32),
        lax.all_to_all(
            shaped[15].astype(jnp.bfloat16), "seg", split_axis=0, concat_axis=0, tiled=True
        ).astype(jnp.float32),
        lax.all_to_all(
            shaped[16].astype(jnp.bfloat16), "seg", split_axis=0, concat_axis=0, tiled=True
        ).astype(jnp.float32),
    )
    summed = tuple((jnp.sum(item, axis=0) for item in received))
    reduced = (
        lax.psum_scatter(
            summed[0].astype(jnp.bfloat16), "rep", scatter_dimension=0, tiled=True
        ).astype(jnp.float32),
        lax.psum_scatter(
            summed[1].astype(jnp.bfloat16), "rep", scatter_dimension=0, tiled=True
        ).astype(jnp.float32),
        lax.psum_scatter(
            summed[2].astype(jnp.bfloat16), "rep", scatter_dimension=0, tiled=True
        ).astype(jnp.float32),
        lax.psum_scatter(
            summed[3].astype(jnp.bfloat16), "rep", scatter_dimension=0, tiled=True
        ).astype(jnp.float32),
        lax.psum_scatter(
            summed[4].astype(jnp.bfloat16), "rep", scatter_dimension=0, tiled=True
        ).astype(jnp.float32),
        lax.psum_scatter(
            summed[5].astype(jnp.bfloat16), "rep", scatter_dimension=0, tiled=True
        ).astype(jnp.float32),
        lax.psum_scatter(
            summed[6].astype(jnp.bfloat16), "rep", scatter_dimension=0, tiled=True
        ).astype(jnp.float32),
        lax.psum_scatter(
            summed[7].astype(jnp.bfloat16), "rep", scatter_dimension=0, tiled=True
        ).astype(jnp.float32),
        lax.psum_scatter(
            summed[8].astype(jnp.bfloat16), "rep", scatter_dimension=0, tiled=True
        ).astype(jnp.float32),
        lax.psum_scatter(
            summed[9].astype(jnp.bfloat16), "rep", scatter_dimension=0, tiled=True
        ).astype(jnp.float32),
        lax.psum_scatter(
            summed[10].astype(jnp.bfloat16), "rep", scatter_dimension=0, tiled=True
        ).astype(jnp.float32),
        lax.psum_scatter(
            summed[11].astype(jnp.bfloat16), "rep", scatter_dimension=0, tiled=True
        ).astype(jnp.float32),
        lax.psum_scatter(
            summed[12].astype(jnp.bfloat16), "rep", scatter_dimension=0, tiled=True
        ).astype(jnp.float32),
        lax.psum_scatter(
            summed[13].astype(jnp.bfloat16), "rep", scatter_dimension=0, tiled=True
        ).astype(jnp.float32),
        lax.psum_scatter(
            summed[14].astype(jnp.bfloat16), "rep", scatter_dimension=0, tiled=True
        ).astype(jnp.float32),
        lax.psum_scatter(
            summed[15].astype(jnp.bfloat16), "rep", scatter_dimension=0, tiled=True
        ).astype(jnp.float32),
        lax.psum_scatter(
            summed[16].astype(jnp.bfloat16), "rep", scatter_dimension=0, tiled=True
        ).astype(jnp.float32),
    )
    return (jnp.stack(outputs), jnp.stack(deltas)) + tuple(reduced)


def solution(mesh):
    sizes = dict(mesh.shape)
    body = local_fast if (sizes["seg"], sizes["rep"]) == (16, 2) else local
    return jax.shard_map(
        body,
        mesh=mesh,
        in_specs=(
            P(None, ("seg", "rep"), None, None),
            P(),
            P(("seg", "rep"), None),
            P(("seg", "rep"), None),
            P(("seg", "rep"), None),
            P(("seg", "rep"), None),
            P(("seg", "rep")),
            P(("seg", "rep")),
            P(("seg", "rep")),
            P(("seg", "rep")),
            P(("seg", "rep"), None),
            P(("seg", "rep"), None),
            P(("seg", "rep"), None),
            P(("seg", "rep"), None),
            P(("seg", "rep")),
            P(("seg", "rep")),
            P(("seg", "rep")),
            P(("seg", "rep")),
            P(("seg", "rep"), None),
            P(None, ("seg", "rep"), None, None),
        ),
        out_specs=(
            P(None, ("seg", "rep"), None, None),
            P(None, ("seg", "rep"), None, None),
            P(("seg", "rep"), None),
            P(("seg", "rep"), None),
            P(("seg", "rep"), None),
            P(("seg", "rep"), None),
            P(("seg", "rep")),
            P(("seg", "rep")),
            P(("seg", "rep")),
            P(("seg", "rep")),
            P(("seg", "rep"), None),
            P(("seg", "rep"), None),
            P(("seg", "rep"), None),
            P(("seg", "rep"), None),
            P(("seg", "rep")),
            P(("seg", "rep")),
            P(("seg", "rep")),
            P(("seg", "rep")),
            P(("seg", "rep"), None),
        ),
        check_vma=False,
    )
```

```python
import math
import jax
import jax.numpy as jnp
from jax import lax
from jax.experimental import pallas as pl
from jax.experimental.pallas import tpu as pltpu
from jax.sharding import PartitionSpec as P

MESH = pl.DeviceIdType.MESH
F32 = jnp.float32
BF = jnp.bfloat16
HEADS = 12
DOC_SEGS = 32
epsilon = 1e-05
floor_score = -1e30
root_half = 1.0 / math.sqrt(2.0)
inverse_root_tau = 1.0 / math.sqrt(2.0 * math.pi)


class Spot:
    def __init__(self):
        s, c = lax.axis_index("seg"), lax.axis_index("rep")
        z, y, x = lax.div(s, 4), lax.rem(lax.div(s, 2), 2), lax.rem(s, 2)
        self.s, self.c, self.z = s, c, z
        self.o = 1 - c
        y1, x1 = y + c * (1 - 2 * y), x + (1 - c) * (1 - 2 * x)
        y2, x2 = y + (1 - c) * (1 - 2 * y), x + c * (1 - 2 * x)
        self.q = 2 * y + x
        self.q1 = 2 * y1 + x1
        self.q2 = 2 * y2 + x2
        self.q12 = 3 - self.q
        self.sib = (s, 1 - c)
        self.n1 = (4 * z + self.q1, c)
        self.n2 = (4 * z + self.q2, c)
        self.diagonal = (4 * z + self.q12, c)
        self.zz = [lax.rem(z + k, 4) for k in (1, 2, 3)]
        odd, high = lax.rem(z, 2), lax.div(z, 2)
        self.middle = (z == 1) | (z == 2)
        self.end = (z == 0) | (z == 3)
        self.zs = [
            (4 * (1 + odd) + self.q, c),
            (4 * ((1 - odd) * (2 + high) + odd * high) + self.q, c),
        ]
        self.pass_from = jnp.where(z == 1, 2, 0)
        self.tip = (4 * jnp.where(z == 2, 3, 0) + self.q, c)
        self.zn = [(4 * zz + self.q, c) for zz in self.zz]
        self.qq = [lax.rem(self.q + k, 4) for k in (0, 1, 2, 3)]
        self.plane = [(4 * z + qq, c) for qq in self.qq]
        self.half = lax.rem(z, 2)
        self.zo = z + 1 - 2 * self.half
        self.i = 8 * self.half + 2 * self.q + c
        self.dev = 2 * s + c


def remote(src, dst, ssem, rsem, dev):
    return pltpu.make_async_remote_copy(
        src_ref=src, dst_ref=dst, send_sem=ssem, recv_sem=rsem, device_id=dev, device_id_type=MESH
    )


def enter(t):
    bar = pltpu.get_barrier_semaphore()
    everyone = [t.sib, t.n1, t.n2, t.diagonal] + t.zn
    for dev in everyone:
        pl.semaphore_signal(bar, inc=1, device_id=dev, device_id_type=MESH)
    pl.semaphore_wait(bar, len(everyone))


def pass_on(t, sem):
    for dev in (t.sib, t.n1, t.n2, t.diagonal):
        pl.semaphore_signal(sem, inc=1, device_id=dev, device_id_type=MESH)


class Sender:
    def __init__(self, t, ss, rs):
        self.t, self.ss, self.rs, self.pending = t, ss, rs, []

    def send(self, at, src, dst, dev):
        d = remote(src, dst, self.ss.at[at], self.rs.at[at], dev)
        d.start()
        self.pending.append(d)

    def arrived(self, at, ref):
        remote(ref, ref, self.ss.at[at], self.rs.at[at], self.t.sib).wait_recv()

    def send_when(self, cond, at, src, dst, dev):
        d = remote(src, dst, self.ss.at[at], self.rs.at[at], dev)
        pl.when(cond)(d.start)
        self.pending.append((cond, d))

    def drain(self):
        for d in self.pending:
            if isinstance(d, tuple):
                pl.when(d[0])(d[1].wait_send)
            else:
                d.wait_send()
        self.pending = []

    def z_spread(self, at, view):
        t = self.t
        for dev in t.zs:
            self.send(at, view(t.z), view(t.z), dev)

    def z_relay(self, at, at2, view):
        t = self.t
        two = view(pl.ds(t.pass_from, 2))
        d = remote(two, two, self.ss.at[at2], self.rs.at[at2], t.tip)

        @pl.when(t.middle)
        def _():
            self.arrived(at, view(pl.ds(0, 3)))
            d.start()

        self.pending.append((t.middle, d))

    def z_last(self, at, at2, view):
        @pl.when(self.t.end)
        def _():
            self.arrived(at, view(0))
            self.arrived(at2, view(pl.ds(0, 2)))


def off(at, size, step=128):
    return pl.ds(pl.multiple_of(at * size, step), size)


def join_pair(t, shard, got, tmp, dest):
    rd, n2 = got.shape
    wide = tmp.shape[1]
    for j in range(0, n2, wide):
        mine = pl.ds(pl.multiple_of(t.c * n2 + j, 128), wide)
        tmp[off(t.c, rd, 8), :] = shard[:, mine].astype(F32)
        tmp[off(t.o, rd, 8), :] = got[:, j : j + wide].astype(F32)
        dest[:, pl.ds(j, wide)] = tmp[...].astype(dest.dtype)


class Gather(Sender):
    def __init__(self, t, far, shard, w, got, tmp, windows, ss, rs):
        super().__init__(t, ss, rs)
        self.far, self.shard, self.w, self.got, self.tmp, self.windows = far, shard, w, got, tmp, windows

    def pair(self):
        n2 = self.got.shape[1]
        self.send((0, 0), self.far.at[:, off(self.t.o, n2)], self.got, self.t.sib)

    def join(self):
        t = self.t
        self.arrived((0, 0), self.got)
        join_pair(t, self.shard, self.got, self.tmp, self.w.at[t.c, t.z, t.q])

    def pick(self, k, *lead):
        rows, cols = self.windows[k]
        return self.w.at[(self.t.c,) + lead + (pl.ds(*rows), pl.ds(*cols))]

    def line(self, k, q):
        return self.pick(k, slice(None), q)

    def view(self, k):
        return lambda at: self.pick(k, at, self.t.q)

    def spread(self, k):
        self.z_spread((k, 1), self.view(k))

    def relay(self, k):
        self.z_relay((k, 1), (k, 9), self.view(k))

    def first(self, k):
        t = self.t
        self.z_last((k, 1), (k, 9), self.view(k))
        line = self.line(k, t.q)
        self.send((k, 2), line, line, t.n1)
        self.send((k, 4), line, line, t.sib)

    def second(self, k):
        t = self.t
        line, other = self.line(k, t.q), self.line(k, t.q1)
        self.arrived((k, 2), other)
        self.send((k, 3), line, line, t.n2)
        self.send((k, 7), other, other, t.n2)
        self.send((k, 5), other, other, t.sib)

    def third(self, k):
        t = self.t
        for i in (3, 7):
            self.arrived((k, i), self.line(k, t.q))
        for i, q in ((6, t.q2), (8, t.q12)):
            self.send((k, i), self.line(k, q), self.line(k, q), t.sib)

    def finish(self, k):
        for i in (4, 5, 6, 8):
            self.arrived((k, i), self.line(k, self.t.q))


class LineGather(Sender):
    def __init__(self, t, w, windows, ss, rs):
        super().__init__(t, ss, rs)
        self.w, self.windows = w, windows

    def view(self, k):
        cols = self.windows[k]
        return lambda at: self.w.at[self.t.c, at, :, pl.ds(*cols)]

    def spread(self, k):
        self.z_spread((k, 0), self.view(k))

    def relay(self, k):
        self.z_relay((k, 0), (k, 1), self.view(k))

    def first(self, k):
        self.z_last((k, 0), (k, 1), self.view(k))
        line = self.view(k)(slice(None))
        self.send((k, 2), line, line, self.t.sib)

    def finish(self, k):
        self.arrived((k, 2), self.view(k)(slice(None)))


class DocGather(Sender):
    def __init__(self, t, far, shards, stages, gots, tmps, dpu, do, dd, ss, rs, ls):
        super().__init__(t, ss, rs)
        self.far, self.shards, self.stages, self.gots, self.tmps = far, shards, stages, gots, tmps
        self.dpu, self.do, self.dd, self.ls = dpu, do, dd, ls
        main, down = stages
        q = t.qq
        self.views = [(lambda at, k=k: main.at[at, :, off(q[k], 768)]) for k in (1, 2, 3, 0)]
        self.views.append(lambda at: main.at[at, :, pl.ds(3072, 384)])
        self.views += [(lambda at, j=j: down.at[at, pl.ds(96 * j, 96)]) for j in range(2)]

    def pair(self):
        dp, do, du, dd = self.far
        for i, ref in enumerate((dp, do, du)):
            self.send(i, ref, self.gots[i], self.t.sib)
        self.send(3, dd.at[:, off(self.t.o, 384)], self.gots[3], self.t.sib)

    def join(self):
        t = self.t
        dp, do, du, dd = self.shards
        for i in range(4):
            self.arrived(i, self.gots[i])
        main, down = self.stages
        tmp = self.tmps[0]
        mine, other = off(t.c, 24, 8), off(t.o, 24, 8)

        def place(ref, got, a, n, b):
            tmp[mine, 0:n] = ref[:, a : a + n].astype(F32)
            tmp[other, 0:n] = got[:, a : a + n].astype(F32)
            wide = -(-n // 128) * 128
            main[t.z, :, b : b + wide] = tmp[:, 0:wide].astype(BF)

        @pl.when(t.c == 0)
        def _():
            tmp[...] = jnp.zeros(tmp.shape, F32)
            for r in range(4):
                for g in range(3):
                    place(dp, self.gots[0], 768 * g + 192 * r, 192, 768 * r + 256 * g)
            place(do, self.gots[1], 0, 384, 3072)

        @pl.when(t.c == 1)
        def _():
            for r in range(4):
                place(du, self.gots[2], 768 * r, 768, 768 * r)
            place(do, self.gots[1], 384, 384, 3072)

        join_pair(t, dd, self.gots[3], self.tmps[1], down.at[t.z])

    def spread(self, k):
        self.z_spread((4 + k), self.views[k])

    def relay(self, k):
        self.z_relay(4 + k, 11 + k, self.views[k])

    def plane(self, w):
        t = self.t
        main, down = self.stages
        self.z_last(4 + w, 11 + w, self.views[w])
        if w == 0:
            self.local = []
        for k in (1, 2, 3, 0):
            if w < 4 and k != (1, 2, 3, 0)[w]:
                continue
            q = t.qq[k]
            if w < 4:
                src, dst, at = main.at[:, :, off(q, 768)], self.dpu.at[t.c, :, t.q], 18
            elif w == 4:
                src, at = main.at[q, :, pl.ds(3072, 384)], 19
                dst = self.do.at[t.c, pl.ds(pl.multiple_of(48 * t.q, 16), 48)]
            else:
                rows = pl.ds(96 * (w - 5), 96)
                src, dst, at = down.at[q, rows], self.dd.at[t.c, t.q, rows], 15 + w
            if k:
                self.send(at, src, dst, t.plane[k])
            else:
                d = pltpu.make_async_copy(src, dst, self.ls.at[at - 18])
                d.start()
                self.local.append(d)

    def share(self):
        t = self.t
        self.arrived(18, self.dpu.at[t.c, :, pl.ds(0, 3)])
        self.arrived(19, self.do.at[t.c, pl.ds(0, 144)])
        for j in range(2):
            self.arrived(20 + j, self.dd.at[t.c, pl.ds(0, 3), pl.ds(0, 96)])
        for d in self.local:
            d.wait()
        for i, ref in enumerate((self.dpu, self.do, self.dd)):
            view = ref.at[t.c, pl.ds(0, 192)] if i == 1 else ref.at[t.c]
            self.send(22 + i, view, view, t.sib)

    def finish(self, i):
        ref = (self.dpu, self.do, self.dd)[i]
        view = ref.at[self.t.o, pl.ds(0, 192)] if i == 1 else ref.at[self.t.o]
        self.arrived(22 + i, view)


class Reduce(Sender):
    def __init__(self, t, w, rc_, r1, r2, r3, fin, fin2, out, windows, ss, rs):
        super().__init__(t, ss, rs)
        self.w, self.rc, self.r1, self.r2, self.r3 = w, rc_, r1, r2, r3
        self.fin, self.fin2, self.out, self.windows = fin, fin2, out, windows
        self.by_rows = fin2.shape[0] == 96

    def cut(self, ref, k, *lead):
        rows, cols = self.windows[k]
        lead += (slice(None),) * (len(ref.shape) - 2 - len(lead))
        return ref.at[lead + (pl.ds(*rows), pl.ds(*cols))]

    def pair(self, k):
        self.send((k, 0), self.cut(self.w, k, self.t.o), self.cut(self.rc, k), self.t.sib)

    def pair_rows(self, z):
        self.send((z, 0), self.w.at[self.t.o, z], self.rc.at[z], self.t.sib)

    def add(self, k, q, part):
        (r, rn), (a, an) = self.windows[k]
        w, c = self.w, self.t.c

        @pl.loop(0, 4)
        def _(z):
            at = (c, z, q, pl.ds(r, rn), pl.ds(a, an))
            w[at] = (w[at].astype(F32) + part[z, r : r + rn, a : a + an].astype(F32)).astype(w.dtype)

    def first(self, k):
        t = self.t
        if self.by_rows:
            for z in range(4 if k == 0 else 0):
                self.arrived((z, 0), self.rc.at[z])
        else:
            self.arrived((k, 0), self.cut(self.rc, k))
        for i, q in ((0, t.q2), (1, t.q12)):
            self.add(k, q, self.rc.at[:, q])
            self.send(
                (k, 1 + i), self.cut(self.w, k, t.c, slice(None), q), self.cut(self.r1, k, i, slice(None)), t.n2
            )
        for q in (t.q, t.q1):
            self.add(k, q, self.rc.at[:, q])

    def second(self, k):
        t = self.t
        self.arrived((k, 2), self.cut(self.r1, k, 1, slice(None)))
        self.add(k, t.q1, self.r1.at[1])
        self.send((k, 3), self.cut(self.w, k, t.c, slice(None), t.q1), self.cut(self.r2, k, slice(None)), t.n1)
        self.arrived((k, 1), self.cut(self.r1, k, 0, slice(None)))
        self.add(k, t.q, self.r1.at[0])

    def third(self, k):
        t = self.t
        self.arrived((k, 3), self.cut(self.r2, k, slice(None)))
        self.add(k, t.q, self.r2)
        for i in range(3):
            self.send((k, 4), self.cut(self.w, k, t.c, t.zz[i], t.q), self.cut(self.r3, k, 2 - i), t.zn[i])

    def fourth(self, k):
        t = self.t
        (r, rn), (a, an) = self.windows[k]
        self.arrived((k, 4), self.cut(self.r3, k, slice(None)))
        total = self.w[t.c, t.z, t.q, r : r + rn, a : a + an].astype(F32)
        for i in range(3):
            total = total + self.r3[i, r : r + rn, a : a + an].astype(F32)
        self.fin[r : r + rn, a : a + an] = total
        if k == len(self.windows) - 1:
            rd = self.fin.shape[0] // 2
            self.send((0, 5), self.fin.at[off(t.o, rd, 8)], self.fin2, t.sib)

    def fifth(self):
        t = self.t
        rd, n2 = self.fin2.shape
        self.arrived((0, 5), self.fin2)
        self.out[:, off(t.c, n2)] = self.fin[off(t.c, rd, 8), :]
        self.out[:, off(t.o, n2)] = self.fin2[...]


def dot(a, b):
    return jnp.dot(a, b, preferred_element_type=F32)


def dot_rt(a, b):
    return lax.dot_general(a, b, (((1,), (1,)), ((), ())), preferred_element_type=F32)


def dot_lt(a, b):
    return lax.dot_general(a, b, (((0,), (0,)), ((), ())), preferred_element_type=F32)


def normed(v):
    centred = v - jnp.mean(v, axis=-1, keepdims=True)
    inverse = lax.rsqrt(jnp.mean(centred * centred, axis=-1, keepdims=True) + epsilon)
    return centred * inverse, inverse


def norm_back(g, n, inverse, gain):
    v = g * gain
    return inverse * (
        v - jnp.mean(v, axis=-1, keepdims=True) - n * jnp.mean(v * n, axis=-1, keepdims=True)
    )


def gelu_pair(v):
    share = 0.5 * (1.0 + lax.erf(v * root_half))
    return v * share, share + v * jnp.exp(-0.5 * v * v) * inverse_root_tau


SIZES = ((24, 128, F32), (24, 1152, BF), (24, 384, BF), (24, 1536, BF), (96, 384, BF))
WINDOWS = (
    [((0, 48), (0, 128))],
    [((0, 48), (384 * j, 384)) for j in range(3)],
    [((0, 48), (0, 384))],
    [((0, 48), (384 * j, 384)) for j in range(4)],
    [((48 * j, 48), (0, 384)) for j in range(4)],
)
SCRATCH = {
    "got": [((rd, n2), dt) for rd, n2, dt in SIZES]
    + [((24, 2304), BF), ((24, 768), BF), ((24, 3072), BF), ((96, 384), BF)],
    "w": [((2, 4, 4, 2 * rd, n2), dt) for rd, n2, dt in SIZES],
    "fin": [((2 * rd, n2), F32) for rd, n2, dt in SIZES],
    "fin2": [((rd, n2), F32) for rd, n2, dt in SIZES],
    "rc": [((4, 4, 2 * rd, n2), dt) for rd, n2, dt in SIZES if n2 not in (1152, 384) or rd == 96],
    "r1": [((2, 4, 2 * rd, n2), dt) for rd, n2, dt in SIZES],
    "r2": [((4, 2 * rd, n2), dt) for rd, n2, dt in SIZES],
    "r3": [((3, 2 * rd, n2), dt) for rd, n2, dt in SIZES],
    "stage": [((4, 48, 3456), BF), ((4, 192, 384), BF)],
    "dpu": [((2, 4, 4, 48, 768), BF)],
    "do": [((2, 256, 384), BF)],
    "dd": [((2, 4, 192, 384), BF)],
    "vec": [((16, 768), F32)],
    "table": [((16, 2, 768), F32)],
    "pr": [((512, 2304), BF)],
    "ctx": [((512, 768), BF)],
    "sh": [((24, 256, 128), BF)],
    "n1": [((512, 768), BF)],
    "i1": [((512, 1), F32)],
    "n2": [((512, 768), BF)],
    "i2": [((512, 1), F32)],
    "fl": [((512, 768), BF)],
    "act": [((512, 3072), BF)],
    "gp": [((512, 3072), BF)],
    "row": [((512, 768), F32)],
    "low": [((512, 768), BF)],
    "ob": [((512, 768), BF)],
    "hid": [((256, 384), F32)],
    "src": [((2, 2, 768), F32)] * 2,
    "slots": [((16, 2, 768), F32)] * 4,
    "sdr": [((2, 4, 2, 768), F32)],
    "pairs": [((2, 2, 768), F32)] * 2,
    "soo": [((2, 768), F32)],
    "mat": [((32, 768), F32)] * 2,
    "ars": [((3, 32, 768), BF)],
    "gpc": [((64, 3072), BF)],
    "lowc": [((64, 768), BF)],
    "arb": [((3, 3, 32, 768), BF)],
    "fq": [((2, 4, 4, 32, 1280), BF)],
    "fz": [((2, 4, 32, 1536), BF)],
    "vg": [((128, 768), F32)],
    "flip": [((768, 128), F32)],
}
SEMS = {
    "gs": (5, 4, 10),
    "gr": (5, 4, 10),
    "ds": (25,),
    "dr": (25,),
    "ls": (4,),
    "rs": (5, 4, 6),
    "rr": (5, 4, 6),
    "xs": (12,),
    "xr": (12,),
    "fs": (3, 10),
    "fr": (3, 10),
    "es": (3, 3),
    "er": (3, 3),
    "os": (11,),
    "ins": (13,),
}
INS = ("tok", "cot", "tmask", "dmask", "small", "sp", "so", "su", "sd", "dp", "dout", "du", "ddown")
OUTS = (
    ("out", (512, 768), BF),
    ("gin", (512, 768), F32),
    ("gsmall", (24, 256), F32),
    ("gsp", (24, 2304), F32),
    ("gso", (24, 768), F32),
    ("gsu", (24, 3072), F32),
    ("gsd", (96, 768), F32),
    ("gdp", (24, 2304), F32),
    ("gdo", (24, 768), F32),
    ("gdu", (24, 3072), F32),
    ("gdd", (96, 768), F32),
)


class Box:
    def put(self, name, ref):
        at = [out[0] for out in OUTS].index(name)
        d = pltpu.make_async_copy(ref, self.back[name], self.os.at[at])
        d.start()
        self.flying[name] = d

    def ready(self, *names):
        for name in names:
            self.coming[name].wait()


def kernel(*refs):
    b = Box()
    refs = list(refs)

    def take(n):
        got, refs[:n] = refs[:n], []
        return got

    b.far = {name: take(1)[0] for name in INS}
    b.back = {name: take(1)[0] for name, _, _ in OUTS}
    for name in INS:
        setattr(b, name, take(1)[0])
    for name, _, _ in OUTS[2:]:
        setattr(b, name, take(1)[0])
    for name, items in SCRATCH.items():
        got = take(len(items))
        setattr(b, name, got if len(got) > 1 else got[0])
    for name in SEMS:
        setattr(b, name, take(1)[0])
    b.credit, b.met, b.met2 = take(3)
    b.t = Spot()
    run(b)


FACTOR_WINDOWS = [((0, 32), (0, 512)), ((0, 32), (512, 384)), ((0, 32), (896, 384))]
LINE_WINDOWS = [(0, 768), (768, 384), (1152, 384)]


def run(b):
    t = b.t
    b.x = Sender(t, b.xs, b.xr)
    b.flying, b.coming = {}, {}
    for i, name in enumerate(INS):
        d = pltpu.make_async_copy(b.far[name], getattr(b, name), b.ins.at[i])
        d.start()
        b.coming[name] = d
    b.do[...] = jnp.zeros(b.do.shape, BF)
    b.vg[...] = jnp.zeros(b.vg.shape, F32)
    enter(t)
    pass_on(t, b.met)
    shards = (b.small, b.sp, b.so, b.su, b.sd)
    far = [b.far[name] for name in ("small", "sp", "so", "su", "sd")]
    gs = [
        Gather(t, far[i], shards[i], b.w[i], b.got[i], b.fin[i], WINDOWS[i], b.gs.at[i], b.gr.at[i])
        for i in range(5)
    ]
    dg = DocGather(
        t,
        [b.far[name] for name in ("dp", "dout", "du", "ddown")],
        (b.dp, b.dout, b.du, b.ddown),
        b.stage,
        b.got[5:],
        (b.fin[1], b.fin[4]),
        b.dpu,
        b.do,
        b.dd,
        b.ds,
        b.dr,
        b.ls,
    )
    for g in gs:
        g.pair()
    dg.pair()
    b.f = Gather(t, None, None, b.fq, None, None, FACTOR_WINDOWS, b.fs, b.fr)
    b.e = LineGather(t, b.fz, LINE_WINDOWS, b.es, b.er)

    events = [(g, k) for g in gs for k in range(len(g.windows))]
    lines = events + [(dg, k) for k in range(7)]
    clock, spreads, relays = [0], [0], [0]

    def do(name, at, among=events):
        if 0 <= at < len(among):
            getattr(among[at][0], name)(among[at][1])

    def relay(n):
        for _ in range(n):
            do("relay", relays[0], lines)
            relays[0] += 1
            do("spread", spreads[0], lines)
            spreads[0] += 1

    def tick(upto):
        while clock[0] <= upto:
            at = clock[0]
            busy = relays[0] < len(events)
            do("first", at)
            relay(1)
            do("second", at - 2)
            if busy:
                relay(1)
            do("third", at - 4)
            do("finish", at - 5)
            clock[0] += 1

    b.ready("small", "sp")
    gs[0].join()
    gs[1].join()
    for i in range(3):
        do("spread", i, lines)
    spreads[0] = 3
    b.ready("so", "su", "sd")
    for g in gs[2:]:
        g.join()
    pl.semaphore_wait(b.met, 4)
    pass_on(t, b.met2)
    relay(1)
    tick(0)
    b.ready("dp", "dout", "du", "ddown")
    dg.join()
    tick(1)
    pl.semaphore_wait(b.met2, 4)
    b.ready("cot", "tok", "tmask", "dmask")
    send_cotangents(b)
    tick(5)
    vectors_in(b)
    tick(8)
    segment_project(b)
    tick(9)
    for seg in range(4):
        attend(b, seg)
        tick(10 + seg // 2)
    segment_mix(b)
    for j in range(4):
        segment_up(b, j)
        tick(12 + j)
        if j:
            dg.plane(j - 1)
    dg.plane(3)
    tick(16)
    for k in range(4, 7):
        dg.plane(k)
    tick(17)
    send_summaries(b, summary_rows(b))
    steps = document(b)
    segment_down(b, 0)
    dg.share()
    for g in gs:
        g.drain()
    for i in range(3):
        dg.finish(i)
    dg.drain()
    next(steps)
    segment_down(b, 1)
    next(steps)
    second_back(b)
    next(steps)
    hidden_back(b)
    next(steps)
    first_back(b)
    next(steps)
    next(steps, None)
    finish_output(b)
    b.f.spread(2)
    b.e.spread(2)

    small_rc, up_rc, down_rc = b.rc
    rcs = (small_rc, up_rc.at[:, :, :, 0:1152], up_rc.at[:, :, :, 1152:1536], up_rc, down_rc)
    rs = [
        Reduce(
            t,
            b.w[i],
            rcs[i],
            b.r1[i],
            b.r2[i],
            b.r3[i],
            b.fin[i],
            b.fin2[i],
            out,
            WINDOWS[i],
            b.rs.at[i],
            b.rr.at[i],
        )
        for i, out in enumerate((b.gsmall, b.gsp, b.gso, b.gsu, b.gsd))
    ]
    for r, name in zip(rs, ("gsmall", "gsp", "gso", "gsu", "gsd")):
        r.name = name
    rsmall, rproject, routput, rup, rdown = rs
    terms = [(r, k) for r in (rdown, rup, routput, rproject, rsmall) for k in range(len(r.windows))]
    clock[0] = 0

    ends = {id(r): max(i for i, e in enumerate(terms) if e[0] is r) for r in rs}

    def tock(upto):
        while clock[0] <= upto:
            at = clock[0]
            do("first", at, terms)
            do("second", at - 2, terms)
            do("third", at - 4, terms)
            do("fourth", at - 6, terms)
            for r in rs:
                if ends[id(r)] == at - 7:
                    r.fifth()
                    b.put(r.name, r.out)
            clock[0] += 1

    second_back_rows(b)
    hidden_back_rows(b)
    b.f.relay(2)
    b.e.relay(2)
    b.f.second(1)
    b.f.third(0)
    down_terms(b, rdown)
    first_back_rows(b)
    b.f.first(2)
    b.e.first(2)
    b.f.third(1)
    tock(0)
    column_terms(b, rup, b.fl, b.gp)
    tock(1)
    b.f.second(2)
    mixed_back(b)
    tock(2)
    context_back(b)
    tock(3)
    b.f.third(2)
    attend_back(b, 0)
    tock(4)
    attend_back(b, 1)
    tock(5)
    attend_back(b, 2)
    tock(6)
    attend_back(b, 3)
    tock(7)
    pl.semaphore_signal(b.credit, inc=1, device_id=t.sib, device_id_type=MESH)
    pl.semaphore_wait(b.credit, 1)
    column_terms(b, routput, b.ctx, b.low)
    input_back(b)
    column_terms(b, rproject, b.tok, b.pr)
    tock(8)
    vectors_out(b)
    rsmall.pair(0)
    tock(10)
    document_terms(b)
    tock(len(terms) + 6)
    for r in rs:
        r.drain()
    b.x.drain()
    for d in b.flying.values():
        d.wait()


def send_cotangents(b):
    for m in range(2):
        for s in range(2):
            rows = b.cot[pl.ds(128 * (2 * m + s), 16), :].astype(F32)
            b.src[0][m, s : s + 1, :] = rows[0:1]
    send_rows(b, 0)


def send_rows(b, n):
    t, src, slots = b.t, b.src[n], b.slots[n]
    mine = src.at[t.half]
    other = src.at[1 - t.half]
    for k in (1, 2, 3):
        b.x.send(n, mine, slots.at[t.i], t.plane[k])
    for k in (0, 1, 2, 3):
        b.x.send(n, mine, slots.at[t.i], (4 * t.z + t.qq[k], t.o))
        b.x.send(n, other, slots.at[t.i], (4 * t.zo + t.qq[k], t.c))
        b.x.send(n, other, slots.at[t.i], (4 * t.zo + t.qq[k], t.o))
    slots[t.i] = src[t.half]


def take_rows(b, n):
    slots = b.slots[n]
    b.x.arrived(n, slots.at[pl.ds(0, 15)])
    for i in range(16):
        b.mat[n][2 * i : 2 * i + 2, :] = slots[i]
    return b.mat[n][...]


def vectors_in(b):
    small = b.w[0]
    b.vec[...] = jnp.transpose(small[0].reshape(768, 128))[0:16]
    table = jnp.transpose(small[1].reshape(768, 128))[0:32]
    for i in range(16):
        b.table[i] = table[2 * i : 2 * i + 2]


def vec(b, i):
    return b.vec[i : i + 1, :]


def segment_project(b):
    w = b.w[1]

    @pl.loop(0, 6)
    def _(i):
        h, j = lax.div(i, 3), lax.rem(i, 3)
        part = w[h, :, :, :, off(j, 384)].reshape(768, 384)
        b.pr[:, off(i, 384)] = dot(b.tok[...], part).astype(BF)


def lane_masks():
    lane = lax.broadcasted_iota(jnp.int32, (1, 128), 1)
    low = (lane < 64).astype(F32)
    return low.astype(BF), (1.0 - low).astype(BF)


def attend(b, seg):
    low, high = lane_masks()
    keep = b.tmask[seg : seg + 1, :] > 0.0
    rows = pl.ds(128 * seg, 128)

    @pl.loop(0, 6)
    def _(p):
        q2 = b.pr[rows, off(p, 128)]
        k2 = b.pr[rows, off(p + 6, 128)]
        v2 = b.pr[rows, off(p + 12, 128)]
        qs = jnp.concatenate((q2 * low, q2 * high), axis=0)
        scores = jnp.where(keep, dot_rt(qs, k2) * 0.125, floor_score)
        raised = jnp.exp(scores - jnp.max(scores, axis=-1, keepdims=True))
        shares = (raised * (1.0 / jnp.sum(raised, axis=-1, keepdims=True))).astype(BF)
        b.sh[6 * seg + p] = shares
        both = dot(shares, v2)
        lane = lax.broadcasted_iota(jnp.int32, (128, 128), 1)
        b.ctx[rows, off(p, 128)] = jnp.where(lane < 64, both[:128], both[128:]).astype(BF)


def segment_mix(b):
    w = b.w[2]
    for r in range(2):
        rows = pl.ds(256 * r, 256)
        for h in range(2):
            b.row[rows, pl.ds(384 * h, 384)] = dot(b.ctx[rows, :], w[h].reshape(768, 384))
    scale, offset = vec(b, 0), vec(b, 1)

    @pl.loop(0, 16)
    def _(i):
        rows = off(i, 32, 32)
        n, inverse = normed(b.tok[rows, :].astype(F32) + b.row[rows, :])
        first = n * scale + offset
        b.n1[rows, :] = n.astype(BF)
        b.i1[rows, :] = inverse
        b.row[rows, :] = first
        b.fl[rows, :] = first.astype(BF)


def segment_up(b, j):
    w = b.w[3]
    for h, r in ((0, 0), (0, 1), (1, 0), (1, 1)):
        up = w[h, :, :, :, pl.ds(384 * j, 384)].reshape(768, 384)
        b.hid[...] = dot(b.fl[256 * r : 256 * r + 256, :], up)
        cols = pl.ds(1536 * h + 384 * j, 384)

        @pl.loop(0, 8)
        def _(i):
            rows = off(i + 8 * r, 32, 32)
            value, slope = gelu_pair(b.hid[off(i, 32, 32), :])
            b.act[rows, cols] = value.astype(BF)
            b.gp[rows, cols] = slope.astype(BF)


def summary_rows(b):
    w = b.w[4]
    for s in range(4):
        b.gpc[16 * s : 16 * s + 16, :] = b.act[128 * s : 128 * s + 16, :]
    parts = [dot(b.gpc[...], w[h].reshape(3072, 384)) for h in range(2)]
    both = jnp.concatenate(parts, axis=1)
    for s in range(4):
        b.gpc[16 * s : 16 * s + 16, :] = b.gp[128 * s : 128 * s + 16, :]
    rows = []
    for s in range(4):
        n, _ = normed(b.row[128 * s : 128 * s + 8, :] + both[16 * s : 16 * s + 8])
        rows.append((n * vec(b, 2) + vec(b, 3))[0:1])
    return rows


def segment_down(b, r):
    w = b.w[4]
    rows = pl.ds(256 * r, 256)

    @pl.loop(0, 2)
    def _(h):
        b.row[rows, off(h, 384)] += dot(b.act[rows, :], w[h].reshape(3072, 384))

    gain, shift = vec(b, 2), vec(b, 3)

    @pl.loop(8 * r, 8 * r + 8)
    def _(i):
        rows = off(i, 32, 32)
        n, inverse = normed(b.row[rows, :])
        b.n2[rows, :] = n.astype(BF)
        b.i2[rows, :] = inverse
        b.ob[rows, :] = (n * gain + shift).astype(BF)


def send_summaries(b, rows):
    places = b.table[b.t.i]
    for m in range(2):
        for s in range(2):
            b.src[1][m, s : s + 1, :] = rows[2 * m + s] + places[s : s + 1]
    send_rows(b, 1)


def plane_send(b, n, partial):
    b.ars[n] = partial.astype(BF)
    for k in (1, 2, 3):
        b.x.send(2 + n, b.ars.at[n], b.arb.at[n, k - 1], b.t.plane[k])


def plane_take(b, n):
    b.x.arrived(2 + n, b.arb.at[n])
    total = b.ars[n].astype(F32)
    for k in range(3):
        total = total + b.arb[n, k].astype(F32)
    return total


def document(b):
    t = b.t
    dp = b.dpu[0].reshape(768, 768)
    du = b.dpu[1].reshape(768, 768)
    lane = lax.broadcasted_iota(jnp.int32, (1, 256), 1)
    heads = [((lane >= 64 * h) & (lane < 64 * h + 64)).astype(F32).astype(BF) for h in range(3)]
    keep = b.dmask[...] > 0.0
    h_in = take_rows(b, 1)
    h_low = h_in.astype(BF)
    pr = dot(h_low, dp).astype(BF)
    q3, k3, v3 = pr[:, 0:256], pr[:, 256:512], pr[:, 512:768]
    qs = jnp.concatenate([q3 * m for m in heads], axis=0)
    scores = jnp.where(keep, dot_rt(qs, k3) * 0.125, floor_score)
    raised = jnp.exp(scores - jnp.max(scores, axis=-1, keepdims=True))
    shares = raised * (1.0 / jnp.sum(raised, axis=-1, keepdims=True))
    shares_low = shares.astype(BF)
    three = dot(shares_low, v3)
    ctx = sum(three[32 * h : 32 * h + 32] * heads[h].astype(F32) for h in range(3)).astype(BF)
    mixed = jnp.concatenate([dot(ctx, b.do[h]) for h in range(2)], axis=1)
    plane_send(b, 0, mixed)
    yield
    n1, i1 = normed(h_in + plane_take(b, 0))
    first = n1 * vec(b, 4) + vec(b, 5)
    first_low = first.astype(BF)
    active, slope = gelu_pair(dot(first_low, du))
    active = active.astype(BF)
    branch = jnp.concatenate([dot(active, b.dd[h].reshape(768, 384)) for h in range(2)], axis=1)
    plane_send(b, 1, branch)

    @pl.when(t.c == 0)
    def _():
        b.fq[0, t.z, t.q, :, 0:512] = active[:, 0:512]
        b.fz[0, t.z, :, 0:768] = h_low

    @pl.when(t.c == 1)
    def _():
        b.fq[1, t.z, t.q, :, 0:256] = active[:, 512:768]
        b.fq[1, t.z, t.q, :, 256:512] = ctx
        b.fz[1, t.z, :, 0:768] = first_low

    b.f.spread(0)
    b.e.spread(0)
    yield
    n2, i2 = normed(first + plane_take(b, 1))
    out = n2 * vec(b, 6) + vec(b, 7)
    g = take_rows(b, 0)
    delta = norm_back(g, n2, i2, vec(b, 6))
    branch_low = delta.astype(BF)
    back = sum(dot_rt(branch_low[:, 384 * h : 384 * h + 384], b.dd[h].reshape(768, 384)) for h in range(2))
    hidden_delta = (back * slope).astype(BF)
    plane_send(b, 2, dot_rt(hidden_delta, du))
    b.vg[6:7, :] = jnp.sum(g * n2, axis=0, keepdims=True) * 0.125
    b.vg[7:8, :] = jnp.sum(g, axis=0, keepdims=True) * 0.125
    for i in range(16):
        b.slots[2][i] = out[2 * i : 2 * i + 2]
    other_i = 8 * (1 - t.half) + 2 * t.q + t.c
    b.x.send(6, b.slots[2].at[other_i], b.soo, (4 * t.zo + t.q, t.c))

    def halves(ref, at, value):
        for h in range(2):

            @pl.when(t.c == h)
            def _():
                ref[(h,) + at] = value[:, 384 * h : 384 * h + 384]

    halves(b.fq, (t.z, t.q, slice(None), slice(512, 896)), hidden_delta)
    halves(b.fz, (t.z, slice(None), slice(768, 1152)), branch_low)
    b.f.relay(0)
    b.e.relay(0)
    b.f.spread(1)
    b.e.spread(1)
    yield
    first_delta = delta + plane_take(b, 2)
    mixed_delta = norm_back(first_delta, n1, i1, vec(b, 4))
    mixed_low = mixed_delta.astype(BF)
    ctx_delta = sum(dot_rt(mixed_low[:, 384 * h : 384 * h + 384], b.do[h]) for h in range(2)).astype(BF)
    cs = jnp.concatenate([ctx_delta * m for m in heads], axis=0)
    shares_delta = dot_rt(cs, v3)
    inner = jnp.sum(shares_delta * shares, axis=-1, keepdims=True)
    scores_delta = (shares * (shares_delta - inner)).astype(BF)
    dq3 = dot(scores_delta, k3) * 0.125
    dq = sum(dq3[32 * h : 32 * h + 32] * heads[h].astype(F32) for h in range(3))
    dk = dot_lt(scores_delta, qs) * 0.125
    dv = dot_lt(shares_low, cs)
    pd = jnp.concatenate((dq, dk, dv), axis=1).astype(BF)
    h_delta = dot_rt(pd, dp) + 0.25 * mixed_delta
    for i in range(16):
        b.slots[3][i] = h_delta[2 * i : 2 * i + 2]
    for k in (0, 1, 2, 3):
        if k:
            b.x.send(7, b.slots[3].at[8 * t.half + 2 * t.qq[k] + t.c], b.sdr.at[0, k], t.plane[k])
        b.x.send(
            8, b.slots[3].at[8 * (1 - t.half) + 2 * t.qq[k] + t.c], b.sdr.at[1, k], (4 * t.zo + t.qq[k], t.c)
        )
    b.sdr[0, 0] = b.slots[3][t.i]
    b.vg[4:5, :] = jnp.sum(first_delta * n1, axis=0, keepdims=True) * 0.125
    b.vg[5:6, :] = jnp.sum(first_delta, axis=0, keepdims=True) * 0.125
    halves(b.fq, (t.z, t.q, slice(None), slice(896, 1280)), pd)
    halves(b.fz, (t.z, slice(None), slice(1152, 1536)), mixed_low)
    b.f.relay(1)
    b.e.relay(1)
    b.f.first(0)
    b.e.first(0)
    yield
    b.f.second(0)
    b.x.arrived(6, b.soo)
    b.pairs[0][t.half] = b.slots[2][t.i]
    b.pairs[0][1 - t.half] = b.soo[...]
    yield
    b.x.arrived(7, b.sdr.at[0, pl.ds(0, 3)])
    b.x.arrived(8, b.sdr.at[1])
    b.pairs[1][t.half] = b.sdr[0, 0] + b.sdr[0, 1] + b.sdr[0, 2] + b.sdr[0, 3]
    b.pairs[1][1 - t.half] = b.sdr[1, 0] + b.sdr[1, 1] + b.sdr[1, 2] + b.sdr[1, 3]
    b.f.first(1)
    b.e.first(1)


def finish_output(b):
    first_row = lax.broadcasted_iota(jnp.int32, (16, 768), 0) == 0
    for m in range(2):
        for s in range(2):
            rows = pl.ds(128 * (2 * m + s), 16)
            fresh = jnp.where(first_row, b.pairs[0][m, s : s + 1, :], b.ob[rows, :].astype(F32))
            b.ob[rows, :] = fresh.astype(BF)
    b.put("out", b.ob)


def second_back(b):
    gain = vec(b, 2)

    def body(i, carry):
        gains, shifts = carry
        rows = off(i, 16, 16)
        late = (lax.broadcasted_iota(jnp.int32, (16, 768), 0) + 16 * lax.rem(i, 8)) == 0
        g = jnp.where(late, 0.0, b.cot[rows, :].astype(F32))
        n = b.n2[rows, :].astype(F32)
        delta = norm_back(g, n, b.i2[rows, :], gain)
        b.row[rows, :] = delta
        b.low[rows, :] = delta.astype(BF)
        return gains + g * n, shifts + g

    zero = jnp.zeros((16, 768), F32)
    gains, shifts = lax.fori_loop(0, 32, body, (zero, zero))
    b.vg[2:3, :] = jnp.sum(gains, axis=0, keepdims=True)
    b.vg[3:4, :] = jnp.sum(shifts, axis=0, keepdims=True)


def second_back_rows(b):
    gain = vec(b, 2)
    top = lax.broadcasted_iota(jnp.int32, (16, 768), 0) == 0
    gains, shifts = b.vg[2:3, :], b.vg[3:4, :]
    for s in range(4):
        rows = slice(128 * s, 128 * s + 16)
        g = b.pairs[1][s // 2, s % 2 : s % 2 + 1, :]
        n = b.n2[rows, :].astype(F32)
        delta = norm_back(jnp.where(top, g, 0.0), n, b.i2[rows, :], gain)
        b.row[rows, :] = jnp.where(top, delta, b.row[rows, :])
        low = jnp.where(top, delta, b.low[rows, :].astype(F32)).astype(BF)
        b.low[rows, :] = low
        b.lowc[16 * s : 16 * s + 16, :] = low
        gains += g * n[0:1]
        shifts += g
    b.vg[2:3, :] = gains
    b.vg[3:4, :] = shifts


def hidden_back_rows(b):
    w = b.w[4]

    @pl.loop(0, 4)
    def _(z):
        cols = off(z, 768)
        back = dot_rt(b.lowc[:, 0:384], w[0, z].reshape(768, 384)) + dot_rt(
            b.lowc[:, 384:768], w[1, z].reshape(768, 384)
        )
        delta = (back * b.gpc[:, cols].astype(F32)).astype(BF)
        b.gpc[:, cols] = delta
        for s in range(4):
            b.gp[pl.ds(128 * s, 16), cols] = delta[16 * s : 16 * s + 16]


def first_back_rows(b):
    w = b.w[3]
    top = lax.broadcasted_iota(jnp.int32, (16, 768), 0) == 0
    more = dot_rt(b.gpc[:, 0:1536], w[0].reshape(768, 1536)) + dot_rt(
        b.gpc[:, 1536:3072], w[1].reshape(768, 1536)
    )
    for s in range(4):
        rows = slice(128 * s, 128 * s + 16)
        b.row[rows, :] += jnp.where(top, more[16 * s : 16 * s + 16], 0.0)


def hidden_back(b):
    w = b.w[4]

    @pl.loop(0, 4)
    def _(z):
        cols = off(z, 768)
        for r in range(2):
            rows = pl.ds(256 * r, 256)
            back = dot_rt(b.low[rows, 0:384], w[0, z].reshape(768, 384)) + dot_rt(
                b.low[rows, 384:768], w[1, z].reshape(768, 384)
            )
            b.gp[rows, cols] = (back * b.gp[rows, cols].astype(F32)).astype(BF)


def down_terms(b, r):
    t, w = b.t, b.w[4]
    for h in (t.o, t.c):
        for z in range(4):
            part = dot_lt(b.act[:, 768 * z : 768 * z + 768], b.low[:, off(h, 384)])
            w[h, z] = part.astype(BF).reshape(4, 192, 384)
            if h is t.o:
                r.pair_rows(z)


def first_back(b):
    w = b.w[3]

    @pl.loop(0, 2)
    def _(r):
        rows = off(r, 256, 256)
        for h in range(2):
            b.row[rows, :] += dot_rt(b.gp[rows, 1536 * h : 1536 * h + 1536], w[h].reshape(768, 1536))


def mixed_back(b):
    scale = vec(b, 0)

    def body(i, carry):
        scales, offsets = carry
        rows = off(i, 16, 16)
        g = b.row[rows, :]
        n = b.n1[rows, :].astype(F32)
        delta = norm_back(g, n, b.i1[rows, :], scale)
        b.row[rows, :] = delta
        b.low[rows, :] = delta.astype(BF)
        return scales + g * n, offsets + g

    zero = jnp.zeros((16, 768), F32)
    scales, offsets = lax.fori_loop(0, 32, body, (zero, zero))
    b.vg[0:1, :] = jnp.sum(scales, axis=0, keepdims=True)
    b.vg[1:2, :] = jnp.sum(offsets, axis=0, keepdims=True)


def context_back(b):
    w = b.w[2]
    b.flying.pop("out").wait()
    for r in range(2):
        rows = pl.ds(256 * r, 256)
        back = dot_rt(b.low[rows, 0:384], w[0].reshape(768, 384)) + dot_rt(
            b.low[rows, 384:768], w[1].reshape(768, 384)
        )
        b.ob[rows, :] = back.astype(BF)


def attend_back(b, seg):
    low, high = lane_masks()
    rows = pl.ds(128 * seg, 128)

    @pl.loop(0, 6)
    def _(p):
        q2 = b.pr[rows, off(p, 128)]
        k2 = b.pr[rows, off(p + 6, 128)]
        v2 = b.pr[rows, off(p + 12, 128)]
        d2 = b.ob[rows, off(p, 128)]
        qs = jnp.concatenate((q2 * low, q2 * high), axis=0)
        cs = jnp.concatenate((d2 * low, d2 * high), axis=0)
        shares_low = b.sh[6 * seg + p]
        shares = shares_low.astype(F32)
        shares_delta = dot_rt(cs, v2)
        inner = jnp.sum(shares_delta * shares, axis=-1, keepdims=True)
        scores_delta = (shares * (shares_delta - inner)).astype(BF)
        dq = dot(scores_delta, k2) * 0.125
        lane = lax.broadcasted_iota(jnp.int32, (128, 128), 1)
        b.pr[rows, off(p, 128)] = jnp.where(lane < 64, dq[:128], dq[128:]).astype(BF)
        b.pr[rows, off(p + 6, 128)] = (dot_lt(scores_delta, qs) * 0.125).astype(BF)
        b.pr[rows, off(p + 12, 128)] = dot_lt(shares_low, cs).astype(BF)


def input_back(b):
    w = b.w[1]

    @pl.loop(0, 2)
    def _(r):
        rows = off(r, 256, 256)
        for h in range(2):
            b.row[rows, :] += dot_rt(b.pr[rows, 1152 * h : 1152 * h + 1152], w[h].reshape(768, 1152))

    b.put("gin", b.row)


def column_terms(b, r, left, right):
    t, w = b.t, r.w
    n = len(r.windows)
    for h in (t.o, t.c):
        for j in range(n):
            part = dot_lt(left[...], right[:, off(n * h + j, 384)])
            w[h, :, :, :, pl.ds(384 * j, 384)] = part.astype(BF).reshape(4, 4, 48, 384)
            if h is t.o:
                r.pair(j)


def vectors_out(b):
    t, w = b.t, b.w[0]
    w[0] = jnp.transpose(b.vg[...]).reshape(4, 4, 48, 128)
    row = lax.broadcasted_iota(jnp.int32, (32, 768), 0)
    both = b.pairs[1][0] + b.pairs[1][1]
    places = jnp.where(row == 2 * t.i, both[0:1], 0.0) + jnp.where(row == 2 * t.i + 1, both[1:2], 0.0)
    b.vg[0:32, :] = places
    w[1] = jnp.transpose(b.vg[...]).reshape(4, 4, 48, 128)


def document_terms(b):
    t = b.t
    for k in range(3):
        b.f.finish(k)
        b.e.finish(k)
    b.f.drain()
    b.e.drain()
    own = 24 * t.dev
    part = 24 * lax.rem(t.dev, 8)
    fq, fz = b.fq, b.fz

    def rows_of(value, at, size):
        n = value.shape[1]
        b.flip[0:n, :] = jnp.transpose(value.astype(F32))
        return b.flip[pl.ds(pl.multiple_of(at, 8), size), :].astype(BF)

    def line(a):
        both = [fz[h, :, :, a : a + 384].reshape(128, 384) for h in range(2)]
        return jnp.concatenate(both, axis=1)

    def rank(q, a):
        both = [fq[h, :, q, :, a : a + 384].reshape(128, 384) for h in range(2)]
        return jnp.concatenate(both, axis=1)

    left = rows_of(fz[0, :, :, 0:768].reshape(128, 768), own, 24)
    for q in range(4):
        part_q = dot(left, rank(q, 896))
        for g in range(3):
            b.gdp[:, 768 * g + 192 * q : 768 * g + 192 * q + 192] = part_q[:, 256 * g : 256 * g + 192]
    left = rows_of(fq[1, :, t.z, :, 256:512].reshape(128, 256), part, 24)
    b.gdo[...] = dot(left, line(1152))
    left = rows_of(fz[1, :, :, 0:768].reshape(128, 768), own, 24)
    for q in range(4):
        b.gdu[:, 768 * q : 768 * q + 768] = dot(left, rank(q, 512))
    active = jnp.concatenate((fq[0, :, t.z, :, 0:512], fq[1, :, t.z, :, 0:256]), axis=-1)
    left = rows_of(active.reshape(128, 768), 4 * part, 96)
    b.gdd[...] = dot(left, line(768))
    for name in ("gdp", "gdo", "gdu", "gdd"):
        b.put(name, getattr(b, name))


def mega(*arrays):
    an = pl.BlockSpec(memory_space=pl.ANY)
    return pl.pallas_call(
        kernel,
        out_shape=[jax.ShapeDtypeStruct(shape, dt) for _, shape, dt in OUTS],
        in_specs=[an] * len(INS),
        out_specs=[an] * len(OUTS),
        scratch_shapes=[pltpu.VMEM(item.shape, item.dtype) for item in arrays]
        + [pltpu.VMEM(shape, dt) for _, shape, dt in OUTS[2:]]
        + [pltpu.VMEM(shape, dt) for items in SCRATCH.values() for shape, dt in items]
        + [pltpu.SemaphoreType.DMA(shape) for shape in SEMS.values()]
        + [pltpu.SemaphoreType.REGULAR] * 3,
        compiler_params=pltpu.CompilerParams(
            collective_id=1, has_side_effects=True, vmem_limit_bytes=65200 * 1024
        ),
    )(*arrays)


def local_fast(tokens, token_counts, *rest):
    weights, cotangent = rest[:17], rest[17]
    batches, segments, length, width = tokens.shape
    device = lax.axis_index("seg") * 2 + lax.axis_index("rep")
    own = lax.dynamic_slice(token_counts, (0, device * segments), (batches, segments)).reshape(-1)
    slots = jnp.arange(length)
    tmask = ((slots[None] < own[:, None]) | (slots[None] == 0)).astype(F32)
    z = lax.div(lax.axis_index("seg"), 4)
    doc = lax.dynamic_slice(
        token_counts, (lax.rem(z, 2), lax.div(z, 2) * DOC_SEGS), (1, DOC_SEGS)
    )
    dmask = (doc > 0).astype(F32)
    rows = weights[0].shape[0]
    lane = jnp.arange(256)[None]
    small = jnp.pad(weights[16], ((0, 0), (128, 96)))
    for at, i in enumerate((4, 5, 6, 7, 12, 13, 14, 15)):
        small = jnp.where(lane == at, weights[i][:, None], small)
    small = small.astype(F32)
    outs = mega(
        tokens.reshape(-1, width),
        cotangent.reshape(-1, width),
        tmask,
        dmask,
        small,
        *weights[:4],
        *weights[8:12],
    )
    out, gin, gsmall, gsp, gso, gsu, gsd, gdp, gdo, gdu, gdd = outs
    return (
        (out.reshape(tokens.shape), gin.reshape(tokens.shape), gsp, gso, gsu, gsd)
        + tuple(gsmall[:, i] for i in range(4))
        + (gdp, gdo, gdu, gdd)
        + tuple(gsmall[:, i] for i in range(4, 8))
        + (gsmall[:, 128:160],)
    )


def partner_2(value, axis, distance):
    mask = 2**distance
    pairs = [(source, source ^ mask) for source in range(lax.axis_size(axis))]
    return lax.ppermute(value, axis, pairs)


def product(left, right):
    return jnp.dot(left, right, preferred_element_type=jnp.float32)


def left_product(left, right):
    return lax.dot_general(
        left, right, (((0,), (0,)), ((), ())), preferred_element_type=jnp.float32
    )


def right_product(left, right):
    return lax.dot_general(
        left, right, (((1,), (1,)), ((), ())), preferred_element_type=jnp.float32
    )


def gelu_value(value):
    return 0.5 * value * (1.0 + lax.erf(value * root_half))


def gelu_slope(value):
    return (
        0.5 * (1.0 + lax.erf(value * root_half))
        + value * jnp.exp(-0.5 * value * value) * inverse_root_tau
    )


def norm_forward(value, gain, shift):
    centred = value - jnp.mean(value, axis=-1, keepdims=True)
    inverse = lax.rsqrt(jnp.mean(centred * centred, axis=-1, keepdims=True) + epsilon)
    normed = centred * inverse
    return (normed * gain + shift, normed, inverse)


def norm_backward(delta_out, normed, inverse, gain):
    scaled = delta_out * gain
    delta_in = inverse * (
        scaled
        - jnp.mean(scaled, axis=-1, keepdims=True)
        - normed * jnp.mean(scaled * normed, axis=-1, keepdims=True)
    )
    return (delta_in, jnp.sum(delta_out * normed, axis=0), jnp.sum(delta_out, axis=0))


def masked_scores(queries, keys, valid):
    scale = 1.0 / math.sqrt(queries.shape[-1])
    scores = (
        jnp.einsum("bqhe,bkhe->bhqk", queries, keys, preferred_element_type=jnp.float32) * scale
    )
    return jnp.where(valid[:, None], scores, floor_score)


def attend_forward(queries, keys, values, valid):
    scores = masked_scores(queries, keys, valid)
    highest = jnp.max(scores, axis=-1, keepdims=True)
    log_total = highest + jnp.log(jnp.sum(jnp.exp(scores - highest), axis=-1, keepdims=True))
    shares = jnp.exp(scores - log_total).astype(jnp.bfloat16)
    context = jnp.einsum("bhqk,bkhe->bqhe", shares, values, preferred_element_type=jnp.float32)
    return (context.astype(jnp.bfloat16), log_total)


def attend_backward(delta_context, queries, keys, values, valid, log_total):
    scale = 1.0 / math.sqrt(queries.shape[-1])
    shares = jnp.exp(masked_scores(queries, keys, valid) - log_total)
    delta_shares = jnp.einsum(
        "bqhe,bkhe->bhqk", delta_context, values, preferred_element_type=jnp.float32
    )
    delta_values = jnp.einsum(
        "bhqk,bqhe->bkhe",
        shares.astype(jnp.bfloat16),
        delta_context,
        preferred_element_type=jnp.float32,
    )
    inner = jnp.sum(delta_shares * shares, axis=-1, keepdims=True)
    delta_scores = (shares * (delta_shares - inner)).astype(jnp.bfloat16)
    delta_queries = (
        jnp.einsum("bhqk,bkhe->bqhe", delta_scores, keys, preferred_element_type=jnp.float32)
        * scale
    )
    delta_keys = (
        jnp.einsum("bhqk,bqhe->bkhe", delta_scores, queries, preferred_element_type=jnp.float32)
        * scale
    )
    return (delta_queries, delta_keys, delta_values)


def block_forward(inputs, layer, attend):
    (
        project_weight,
        output_weight,
        up_weight,
        down_weight,
        first_gain,
        first_shift,
        second_gain,
        second_shift,
    ) = layer
    inputs_low = inputs.astype(jnp.bfloat16)
    projected = product(inputs_low, project_weight).astype(jnp.bfloat16)
    context, attend_kept = attend(projected)
    mixed = product(context, output_weight)
    first, first_normed, first_inverse = norm_forward(
        inputs + mixed, first_gain.astype(jnp.float32), first_shift.astype(jnp.float32)
    )
    first_low = first.astype(jnp.bfloat16)
    hidden = product(first_low, up_weight)
    active = gelu_value(hidden).astype(jnp.bfloat16)
    second, second_normed, second_inverse = norm_forward(
        first + product(active, down_weight),
        second_gain.astype(jnp.float32),
        second_shift.astype(jnp.float32),
    )
    kept = (
        inputs_low,
        projected,
        context,
        attend_kept,
        first_normed,
        first_inverse,
        first_low,
        hidden,
        active,
        second_normed,
        second_inverse,
    )
    return (second, kept)


def block_backward(delta_out, kept, layer, attend_back):
    (
        project_weight,
        output_weight,
        up_weight,
        down_weight,
        first_gain,
        first_shift,
        second_gain,
        second_shift,
    ) = layer
    (
        inputs_low,
        projected,
        context,
        attend_kept,
        first_normed,
        first_inverse,
        first_low,
        hidden,
        active,
        second_normed,
        second_inverse,
    ) = kept
    delta_second, second_gain_delta, second_shift_delta = norm_backward(
        delta_out, second_normed, second_inverse, second_gain.astype(jnp.float32)
    )
    branch_low = delta_second.astype(jnp.bfloat16)
    delta_down = left_product(active, branch_low)
    delta_hidden = (right_product(branch_low, down_weight) * gelu_slope(hidden)).astype(
        jnp.bfloat16
    )
    delta_up = left_product(first_low, delta_hidden)
    delta_first = delta_second + right_product(delta_hidden, up_weight)
    delta_mixed, first_gain_delta, first_shift_delta = norm_backward(
        delta_first, first_normed, first_inverse, first_gain.astype(jnp.float32)
    )
    mixed_low = delta_mixed.astype(jnp.bfloat16)
    delta_output = left_product(context, mixed_low)
    delta_context = right_product(mixed_low, output_weight).astype(jnp.bfloat16)
    delta_projected = attend_back(delta_context, projected, attend_kept)
    delta_project = left_product(inputs_low, delta_projected)
    delta_inputs = delta_mixed + right_product(delta_projected, project_weight)
    return (
        delta_inputs,
        (
            delta_project,
            delta_output,
            delta_up,
            delta_down,
            first_gain_delta,
            first_shift_delta,
            second_gain_delta,
            second_shift_delta,
        ),
    )


def local(
    tokens,
    token_counts,
    segment_project,
    segment_output,
    segment_up,
    segment_down,
    segment_scale,
    segment_offset,
    segment_gain,
    segment_shift,
    document_project,
    document_output,
    document_up,
    document_down,
    document_scale,
    document_offset,
    document_gain,
    document_shift,
    position,
    cotangent,
):
    batches, segments, length, width = tokens.shape
    heads = HEADS
    head_width = width // heads
    rows_total = segments * length
    index = lax.axis_index(("seg", "rep"))
    first_segment = index * segments
    own_document = first_segment // DOC_SEGS
    positions = jnp.arange(length)
    slots = (first_segment + jnp.arange(segments)) % DOC_SEGS
    picker = (slots[:, None] == jnp.arange(DOC_SEGS)[None, :]).astype(jnp.float32)
    levels = (DOC_SEGS // segments).bit_length() - 1
    gathered_once = (
        lax.all_gather(segment_project, ("seg", "rep"), axis=0, tiled=True),
        lax.all_gather(segment_output, ("seg", "rep"), axis=0, tiled=True),
        lax.all_gather(segment_up, ("seg", "rep"), axis=0, tiled=True),
        lax.all_gather(segment_down, ("seg", "rep"), axis=0, tiled=True),
        lax.all_gather(segment_scale, ("seg", "rep"), axis=0, tiled=True),
        lax.all_gather(segment_offset, ("seg", "rep"), axis=0, tiled=True),
        lax.all_gather(segment_gain, ("seg", "rep"), axis=0, tiled=True),
        lax.all_gather(segment_shift, ("seg", "rep"), axis=0, tiled=True),
        lax.all_gather(document_project, ("seg", "rep"), axis=0, tiled=True),
        lax.all_gather(document_output, ("seg", "rep"), axis=0, tiled=True),
        lax.all_gather(document_up, ("seg", "rep"), axis=0, tiled=True),
        lax.all_gather(document_down, ("seg", "rep"), axis=0, tiled=True),
        lax.all_gather(document_scale, ("seg", "rep"), axis=0, tiled=True),
        lax.all_gather(document_offset, ("seg", "rep"), axis=0, tiled=True),
        lax.all_gather(document_gain, ("seg", "rep"), axis=0, tiled=True),
        lax.all_gather(document_shift, ("seg", "rep"), axis=0, tiled=True),
        lax.all_gather(position, ("seg", "rep"), axis=0, tiled=True),
    )
    outputs = []
    deltas = []
    totals = None
    for batch in range(batches):
        segment_layer = gathered_once[0:8]
        document_layer = gathered_once[8:16]
        table = jnp.transpose(gathered_once[16].astype(jnp.float32))
        counts_row = token_counts[batch]
        local_counts = lax.dynamic_slice_in_dim(counts_row, first_segment, segments)
        token_valid = (positions[None, :] < local_counts[:, None]) | (positions[None, :] == 0)
        segment_valid = token_valid[:, None, :]

        def segment_attend(projected):
            parts = projected.reshape(segments, length, 3, heads, head_width)
            context, log_total = attend_forward(
                parts[:, :, 0], parts[:, :, 1], parts[:, :, 2], segment_valid
            )
            return (context.reshape(rows_total, width), log_total)

        def segment_back(delta_context, projected, log_total):
            parts = projected.reshape(segments, length, 3, heads, head_width)
            delta_queries, delta_keys, delta_values = attend_backward(
                delta_context.reshape(segments, length, heads, head_width),
                parts[:, :, 0],
                parts[:, :, 1],
                parts[:, :, 2],
                segment_valid,
                log_total,
            )
            return (
                jnp.stack((delta_queries, delta_keys, delta_values), axis=2)
                .reshape(rows_total, 3 * width)
                .astype(jnp.bfloat16)
            )

        def document_attend(projected):
            queries = projected[:, :width].reshape(1, segments, heads, head_width)
            pairs = projected[:, width:]
            collected = pairs[None]
            for bit in range(levels):
                partner = partner_2(collected, ("seg", "rep"), bit)
                upper = jnp.right_shift(index, bit) % 2
                collected = jnp.where(
                    upper == 0,
                    jnp.concatenate((collected, partner), axis=0),
                    jnp.concatenate((partner, collected), axis=0),
                )
            collected = collected.reshape(DOC_SEGS, 2 * width)
            key_valid = lax.dynamic_slice_in_dim(counts_row, own_document * DOC_SEGS, DOC_SEGS) > 0
            keys = collected[:, :width].reshape(1, DOC_SEGS, heads, head_width)
            values = collected[:, width:].reshape(1, DOC_SEGS, heads, head_width)
            valid = key_valid[None, None, :]
            context, log_total = attend_forward(queries, keys, values, valid)
            return (context.reshape(segments, width), (collected, valid, log_total))

        def document_back(delta_context, projected, kept_rows):
            collected, valid, log_total = kept_rows
            queries = projected[:, :width].reshape(1, segments, heads, head_width)
            keys = collected[:, :width].reshape(1, DOC_SEGS, heads, head_width)
            values = collected[:, width:].reshape(1, DOC_SEGS, heads, head_width)
            delta_queries, delta_keys, delta_values = attend_backward(
                delta_context.reshape(1, segments, heads, head_width),
                queries,
                keys,
                values,
                valid,
                log_total,
            )
            delta_pairs = jnp.concatenate(
                (delta_keys.reshape(DOC_SEGS, width), delta_values.reshape(DOC_SEGS, width)), axis=1
            )
            folded = delta_pairs.reshape(DOC_SEGS // segments, segments, 2 * width)
            for bit in reversed(range(levels)):
                halves = folded.reshape(2, folded.shape[0] // 2, segments, 2 * width)
                upper = jnp.right_shift(index, bit) % 2
                keep = jnp.where(upper == 0, halves[0], halves[1])
                send = jnp.where(upper == 0, halves[1], halves[0])
                folded = keep + partner_2(send.astype(jnp.bfloat16), ("seg", "rep"), bit).astype(
                    send.dtype
                )
            own_pairs = folded.reshape(segments, 2 * width)
            return jnp.concatenate(
                (delta_queries.reshape(segments, width), own_pairs), axis=1
            ).astype(jnp.bfloat16)

        inputs = tokens[batch].astype(jnp.float32).reshape(rows_total, width)
        segment_rows, segment_kept = block_forward(inputs, segment_layer, segment_attend)
        segment_rows = segment_rows.reshape(segments, length, width)
        lookup = jnp.sum(picker[:, :, None] * table[None, :, :], axis=1)
        summary_rows = segment_rows[:, 0, :] + lookup
        summary_out, document_kept = block_forward(summary_rows, document_layer, document_attend)
        outputs.append(segment_rows.at[:, 0, :].set(summary_out).astype(jnp.bfloat16))
        incoming = cotangent[batch].astype(jnp.float32)
        delta_summary, document_deltas = block_backward(
            incoming[:, 0, :], document_kept, document_layer, document_back
        )
        delta_table = jnp.transpose(jnp.sum(picker[:, :, None] * delta_summary[:, None, :], axis=0))
        delta_rows = incoming.at[:, 0, :].set(delta_summary).reshape(rows_total, width)
        delta_inputs, segment_deltas = block_backward(
            delta_rows, segment_kept, segment_layer, segment_back
        )
        deltas.append(delta_inputs.reshape(segments, length, width))
        current = segment_deltas + document_deltas + (delta_table,)
        totals = (
            current
            if totals is None
            else tuple((left + right for left, right in zip(totals, current)))
        )
    groups = lax.axis_size("seg")
    shaped = tuple(
        (item.reshape((groups, item.shape[0] // groups) + item.shape[1:]) for item in totals)
    )
    received = (
        lax.all_to_all(
            shaped[0].astype(jnp.bfloat16), "seg", split_axis=0, concat_axis=0, tiled=True
        ).astype(jnp.float32),
        lax.all_to_all(
            shaped[1].astype(jnp.bfloat16), "seg", split_axis=0, concat_axis=0, tiled=True
        ).astype(jnp.float32),
        lax.all_to_all(
            shaped[2].astype(jnp.bfloat16), "seg", split_axis=0, concat_axis=0, tiled=True
        ).astype(jnp.float32),
        lax.all_to_all(
            shaped[3].astype(jnp.bfloat16), "seg", split_axis=0, concat_axis=0, tiled=True
        ).astype(jnp.float32),
        lax.all_to_all(
            shaped[4].astype(jnp.bfloat16), "seg", split_axis=0, concat_axis=0, tiled=True
        ).astype(jnp.float32),
        lax.all_to_all(
            shaped[5].astype(jnp.bfloat16), "seg", split_axis=0, concat_axis=0, tiled=True
        ).astype(jnp.float32),
        lax.all_to_all(
            shaped[6].astype(jnp.bfloat16), "seg", split_axis=0, concat_axis=0, tiled=True
        ).astype(jnp.float32),
        lax.all_to_all(
            shaped[7].astype(jnp.bfloat16), "seg", split_axis=0, concat_axis=0, tiled=True
        ).astype(jnp.float32),
        lax.all_to_all(
            shaped[8].astype(jnp.bfloat16), "seg", split_axis=0, concat_axis=0, tiled=True
        ).astype(jnp.float32),
        lax.all_to_all(
            shaped[9].astype(jnp.bfloat16), "seg", split_axis=0, concat_axis=0, tiled=True
        ).astype(jnp.float32),
        lax.all_to_all(
            shaped[10].astype(jnp.bfloat16), "seg", split_axis=0, concat_axis=0, tiled=True
        ).astype(jnp.float32),
        lax.all_to_all(
            shaped[11].astype(jnp.bfloat16), "seg", split_axis=0, concat_axis=0, tiled=True
        ).astype(jnp.float32),
        lax.all_to_all(
            shaped[12].astype(jnp.bfloat16), "seg", split_axis=0, concat_axis=0, tiled=True
        ).astype(jnp.float32),
        lax.all_to_all(
            shaped[13].astype(jnp.bfloat16), "seg", split_axis=0, concat_axis=0, tiled=True
        ).astype(jnp.float32),
        lax.all_to_all(
            shaped[14].astype(jnp.bfloat16), "seg", split_axis=0, concat_axis=0, tiled=True
        ).astype(jnp.float32),
        lax.all_to_all(
            shaped[15].astype(jnp.bfloat16), "seg", split_axis=0, concat_axis=0, tiled=True
        ).astype(jnp.float32),
        lax.all_to_all(
            shaped[16].astype(jnp.bfloat16), "seg", split_axis=0, concat_axis=0, tiled=True
        ).astype(jnp.float32),
    )
    summed = tuple((jnp.sum(item, axis=0) for item in received))
    reduced = (
        lax.psum_scatter(
            summed[0].astype(jnp.bfloat16), "rep", scatter_dimension=0, tiled=True
        ).astype(jnp.float32),
        lax.psum_scatter(
            summed[1].astype(jnp.bfloat16), "rep", scatter_dimension=0, tiled=True
        ).astype(jnp.float32),
        lax.psum_scatter(
            summed[2].astype(jnp.bfloat16), "rep", scatter_dimension=0, tiled=True
        ).astype(jnp.float32),
        lax.psum_scatter(
            summed[3].astype(jnp.bfloat16), "rep", scatter_dimension=0, tiled=True
        ).astype(jnp.float32),
        lax.psum_scatter(
            summed[4].astype(jnp.bfloat16), "rep", scatter_dimension=0, tiled=True
        ).astype(jnp.float32),
        lax.psum_scatter(
            summed[5].astype(jnp.bfloat16), "rep", scatter_dimension=0, tiled=True
        ).astype(jnp.float32),
        lax.psum_scatter(
            summed[6].astype(jnp.bfloat16), "rep", scatter_dimension=0, tiled=True
        ).astype(jnp.float32),
        lax.psum_scatter(
            summed[7].astype(jnp.bfloat16), "rep", scatter_dimension=0, tiled=True
        ).astype(jnp.float32),
        lax.psum_scatter(
            summed[8].astype(jnp.bfloat16), "rep", scatter_dimension=0, tiled=True
        ).astype(jnp.float32),
        lax.psum_scatter(
            summed[9].astype(jnp.bfloat16), "rep", scatter_dimension=0, tiled=True
        ).astype(jnp.float32),
        lax.psum_scatter(
            summed[10].astype(jnp.bfloat16), "rep", scatter_dimension=0, tiled=True
        ).astype(jnp.float32),
        lax.psum_scatter(
            summed[11].astype(jnp.bfloat16), "rep", scatter_dimension=0, tiled=True
        ).astype(jnp.float32),
        lax.psum_scatter(
            summed[12].astype(jnp.bfloat16), "rep", scatter_dimension=0, tiled=True
        ).astype(jnp.float32),
        lax.psum_scatter(
            summed[13].astype(jnp.bfloat16), "rep", scatter_dimension=0, tiled=True
        ).astype(jnp.float32),
        lax.psum_scatter(
            summed[14].astype(jnp.bfloat16), "rep", scatter_dimension=0, tiled=True
        ).astype(jnp.float32),
        lax.psum_scatter(
            summed[15].astype(jnp.bfloat16), "rep", scatter_dimension=0, tiled=True
        ).astype(jnp.float32),
        lax.psum_scatter(
            summed[16].astype(jnp.bfloat16), "rep", scatter_dimension=0, tiled=True
        ).astype(jnp.float32),
    )
    return (jnp.stack(outputs), jnp.stack(deltas)) + tuple(reduced)


def solution(mesh):
    sizes = dict(mesh.shape)
    body = local_fast if (sizes["seg"], sizes["rep"]) == (16, 2) else local
    return jax.shard_map(
        body,
        mesh=mesh,
        in_specs=(
            P(None, ("seg", "rep"), None, None),
            P(),
            P(("seg", "rep"), None),
            P(("seg", "rep"), None),
            P(("seg", "rep"), None),
            P(("seg", "rep"), None),
            P(("seg", "rep")),
            P(("seg", "rep")),
            P(("seg", "rep")),
            P(("seg", "rep")),
            P(("seg", "rep"), None),
            P(("seg", "rep"), None),
            P(("seg", "rep"), None),
            P(("seg", "rep"), None),
            P(("seg", "rep")),
            P(("seg", "rep")),
            P(("seg", "rep")),
            P(("seg", "rep")),
            P(("seg", "rep"), None),
            P(None, ("seg", "rep"), None, None),
        ),
        out_specs=(
            P(None, ("seg", "rep"), None, None),
            P(None, ("seg", "rep"), None, None),
            P(("seg", "rep"), None),
            P(("seg", "rep"), None),
            P(("seg", "rep"), None),
            P(("seg", "rep"), None),
            P(("seg", "rep")),
            P(("seg", "rep")),
            P(("seg", "rep")),
            P(("seg", "rep")),
            P(("seg", "rep"), None),
            P(("seg", "rep"), None),
            P(("seg", "rep"), None),
            P(("seg", "rep"), None),
            P(("seg", "rep")),
            P(("seg", "rep")),
            P(("seg", "rep")),
            P(("seg", "rep")),
            P(("seg", "rep"), None),
        ),
        check_vma=False,
    )
```

```python
import math
import jax
import jax.numpy as jnp
from jax import lax
from jax.experimental import pallas as pl
from jax.experimental.pallas import tpu as pltpu
from jax.sharding import PartitionSpec as P

MESH = pl.DeviceIdType.MESH
F32 = jnp.float32
BF = jnp.bfloat16
HEADS = 12
DOC_SEGS = 32
epsilon = 1e-05
floor_score = -1e30
root_half = 1.0 / math.sqrt(2.0)
inverse_root_tau = 1.0 / math.sqrt(2.0 * math.pi)


class Spot:
    def __init__(self):
        s, c = lax.axis_index("seg"), lax.axis_index("rep")
        z, y, x = lax.div(s, 4), lax.rem(lax.div(s, 2), 2), lax.rem(s, 2)
        self.s, self.c, self.z = s, c, z
        self.o = 1 - c
        y1, x1 = y + c * (1 - 2 * y), x + (1 - c) * (1 - 2 * x)
        y2, x2 = y + (1 - c) * (1 - 2 * y), x + c * (1 - 2 * x)
        self.q = 2 * y + x
        self.q1 = 2 * y1 + x1
        self.q2 = 2 * y2 + x2
        self.q12 = 3 - self.q
        self.sib = (s, 1 - c)
        self.n1 = (4 * z + self.q1, c)
        self.n2 = (4 * z + self.q2, c)
        self.diagonal = (4 * z + self.q12, c)
        self.zz = [lax.rem(z + k, 4) for k in (1, 2, 3)]
        odd, high = lax.rem(z, 2), lax.div(z, 2)
        self.middle = (z == 1) | (z == 2)
        self.end = (z == 0) | (z == 3)
        self.zs = [
            (4 * (1 + odd) + self.q, c),
            (4 * ((1 - odd) * (2 + high) + odd * high) + self.q, c),
        ]
        self.pass_from = jnp.where(z == 1, 2, 0)
        self.tip = (4 * jnp.where(z == 2, 3, 0) + self.q, c)
        self.zn = [(4 * zz + self.q, c) for zz in self.zz]
        self.qq = [lax.rem(self.q + k, 4) for k in (0, 1, 2, 3)]
        self.plane = [(4 * z + qq, c) for qq in self.qq]
        self.half = lax.rem(z, 2)
        self.zo = z + 1 - 2 * self.half
        self.i = 8 * self.half + 2 * self.q + c
        self.dev = 2 * s + c


def remote(src, dst, ssem, rsem, dev):
    return pltpu.make_async_remote_copy(
        src_ref=src, dst_ref=dst, send_sem=ssem, recv_sem=rsem, device_id=dev, device_id_type=MESH
    )


def enter(t):
    bar = pltpu.get_barrier_semaphore()
    everyone = [t.sib, t.n1, t.n2, t.diagonal] + t.zn
    for dev in everyone:
        pl.semaphore_signal(bar, inc=1, device_id=dev, device_id_type=MESH)
    pl.semaphore_wait(bar, len(everyone))


def pass_on(t, sem):
    for dev in (t.sib, t.n1, t.n2, t.diagonal):
        pl.semaphore_signal(sem, inc=1, device_id=dev, device_id_type=MESH)


class Sender:
    def __init__(self, t, ss, rs):
        self.t, self.ss, self.rs, self.pending = t, ss, rs, []

    def send(self, at, src, dst, dev):
        d = remote(src, dst, self.ss, self.rs.at[at], dev)
        d.start()
        self.pending.append(d)

    def arrived(self, at, ref):
        remote(ref, ref, self.ss, self.rs.at[at], self.t.sib).wait_recv()

    def drain(self):
        for d in self.pending:
            if isinstance(d, tuple):
                pl.when(d[0])(d[1].wait_send)
            else:
                d.wait_send()
        self.pending = []

    def z_spread(self, at, view):
        t = self.t
        for dev in t.zs:
            self.send(at, view(t.z), view(t.z), dev)

    def z_relay(self, at, at2, view):
        t = self.t
        two = view(pl.ds(t.pass_from, 2))
        d = remote(two, two, self.ss, self.rs.at[at2], t.tip)

        @pl.when(t.middle)
        def _():
            self.arrived(at, view(pl.ds(0, 3)))
            d.start()

        self.pending.append((t.middle, d))

    def z_last(self, at, at2, view):
        @pl.when(self.t.end)
        def _():
            self.arrived(at, view(0))
            self.arrived(at2, view(pl.ds(0, 2)))


def off(at, size, step=128):
    return pl.ds(pl.multiple_of(at * size, step), size)


def join_pair(t, shard, got, tmp, dest):
    rd, n2 = got.shape
    wide = tmp.shape[1]
    for j in range(0, n2, wide):
        mine = pl.ds(pl.multiple_of(t.c * n2 + j, 128), wide)
        tmp[off(t.c, rd, 8), :] = shard[:, mine].astype(F32)
        tmp[off(t.o, rd, 8), :] = got[:, j : j + wide].astype(F32)
        dest[:, pl.ds(j, wide)] = tmp[...].astype(dest.dtype)


class Gather(Sender):
    def __init__(self, t, far, shard, w, got, tmp, windows, ss, rs):
        super().__init__(t, ss, rs)
        self.far, self.shard, self.w, self.got, self.tmp, self.windows = far, shard, w, got, tmp, windows

    def pair(self):
        n2 = self.got.shape[1]
        self.send(5 * len(self.windows), self.far.at[:, off(self.t.o, n2)], self.got, self.t.sib)

    def join(self):
        t = self.t
        self.arrived(5 * len(self.windows), self.got)
        join_pair(t, self.shard, self.got, self.tmp, self.w.at[t.c, t.z, t.q])

    def pick(self, k, *lead):
        rows, cols = self.windows[k]
        return self.w.at[(self.t.c,) + lead + (pl.ds(*rows), pl.ds(*cols))]

    def line(self, k, q):
        return self.pick(k, slice(None), q)

    def view(self, k):
        return lambda at: self.pick(k, at, self.t.q)

    def spread(self, k):
        self.z_spread(5 * k, self.view(k))

    def relay(self, k):
        self.z_relay(5 * k, 5 * k + 1, self.view(k))

    def first(self, k):
        t = self.t
        self.z_last(5 * k, 5 * k + 1, self.view(k))
        line = self.line(k, t.q)
        self.send(5 * k + 2, line, line, t.n1)
        self.send(5 * k + 4, line, line, t.sib)

    def second(self, k):
        t = self.t
        line, other = self.line(k, t.q), self.line(k, t.q1)
        self.arrived(5 * k + 2, other)
        self.send(5 * k + 3, line, line, t.n2)
        self.send(5 * k + 3, other, other, t.n2)
        self.send(5 * k + 4, other, other, t.sib)

    def third(self, k):
        t = self.t
        self.arrived(5 * k + 3, self.pick(k, slice(None), pl.ds(0, 2)))
        for q in (t.q2, t.q12):
            self.send(5 * k + 4, self.line(k, q), self.line(k, q), t.sib)

    def finish(self, k):
        self.arrived(5 * k + 4, self.pick(k, slice(None), slice(None)))


class LineGather(Sender):
    def __init__(self, t, w, windows, ss, rs):
        super().__init__(t, ss, rs)
        self.w, self.windows = w, windows

    def view(self, k):
        cols = self.windows[k]
        return lambda at: self.w.at[self.t.c, at, :, pl.ds(*cols)]

    def spread(self, k):
        self.z_spread(3 * k, self.view(k))

    def relay(self, k):
        self.z_relay(3 * k, 3 * k + 1, self.view(k))

    def first(self, k):
        self.z_last(3 * k, 3 * k + 1, self.view(k))
        line = self.view(k)(slice(None))
        self.send(3 * k + 2, line, line, self.t.sib)

    def finish(self, k):
        self.arrived(3 * k + 2, self.view(k)(slice(None)))


class DocGather(Sender):
    def __init__(self, t, far, shards, stages, gots, tmps, dpu, do, dd, ss, rs, ls):
        super().__init__(t, ss, rs)
        self.far, self.shards, self.stages, self.gots, self.tmps = far, shards, stages, gots, tmps
        self.dpu, self.do, self.dd, self.ls = dpu, do, dd, ls
        main, down = stages
        q = t.qq
        self.views = [(lambda at, k=k: main.at[at, :, off(q[k], 768)]) for k in (1, 2, 3, 0)]
        self.views.append(lambda at: main.at[at, :, pl.ds(3072, 384)])
        self.views += [(lambda at, j=j: down.at[at, pl.ds(96 * j, 96)]) for j in range(2)]

    def pair(self):
        dp, do, du, dd = self.far
        for i, ref in enumerate((dp, do, du)):
            self.send(i, ref, self.gots[i], self.t.sib)
        self.send(3, dd.at[:, off(self.t.o, 384)], self.gots[3], self.t.sib)

    def join(self):
        t = self.t
        dp, do, du, dd = self.shards
        for i in range(4):
            self.arrived(i, self.gots[i])
        main, down = self.stages
        tmp = self.tmps[0]
        mine, other = off(t.c, 24, 8), off(t.o, 24, 8)

        def place(ref, got, a, n, b):
            tmp[mine, 0:n] = ref[:, a : a + n].astype(F32)
            tmp[other, 0:n] = got[:, a : a + n].astype(F32)
            wide = -(-n // 128) * 128
            main[t.z, :, b : b + wide] = tmp[:, 0:wide].astype(BF)

        @pl.when(t.c == 0)
        def _():
            tmp[...] = jnp.zeros(tmp.shape, F32)
            for r in range(4):
                for g in range(3):
                    place(dp, self.gots[0], 768 * g + 192 * r, 192, 768 * r + 256 * g)
            place(do, self.gots[1], 0, 384, 3072)

        @pl.when(t.c == 1)
        def _():
            for r in range(4):
                place(du, self.gots[2], 768 * r, 768, 768 * r)
            place(do, self.gots[1], 384, 384, 3072)

        join_pair(t, dd, self.gots[3], self.tmps[1], down.at[t.z])

    def spread(self, k):
        self.z_spread((4 + k), self.views[k])

    def relay(self, k):
        self.z_relay(4 + k, 11 + k, self.views[k])

    def plane(self, w):
        t = self.t
        main, down = self.stages
        self.z_last(4 + w, 11 + w, self.views[w])
        if w == 0:
            self.local = []
        for k in (1, 2, 3, 0):
            if w < 4 and k != (1, 2, 3, 0)[w]:
                continue
            q = t.qq[k]
            if w < 4:
                src, dst, at = main.at[:, :, off(q, 768)], self.dpu.at[t.c, :, t.q], 18
            elif w == 4:
                src, at = main.at[q, :, pl.ds(3072, 384)], 19
                dst = self.do.at[t.c, pl.ds(pl.multiple_of(48 * t.q, 16), 48)]
            else:
                rows = pl.ds(96 * (w - 5), 96)
                src, dst, at = down.at[q, rows], self.dd.at[t.c, t.q, rows], 15 + w
            if k:
                self.send(at, src, dst, t.plane[k])
            else:
                d = pltpu.make_async_copy(src, dst, self.ls.at[at - 18])
                d.start()
                self.local.append(d)

    def share(self):
        t = self.t
        self.arrived(18, self.dpu.at[t.c, :, pl.ds(0, 3)])
        self.arrived(19, self.do.at[t.c, pl.ds(0, 144)])
        for j in range(2):
            self.arrived(20 + j, self.dd.at[t.c, pl.ds(0, 3), pl.ds(0, 96)])
        for d in self.local:
            d.wait()
        for i, ref in enumerate((self.dpu, self.do, self.dd)):
            view = ref.at[t.c, pl.ds(0, 192)] if i == 1 else ref.at[t.c]
            self.send(22 + i, view, view, t.sib)

    def finish(self, i):
        ref = (self.dpu, self.do, self.dd)[i]
        view = ref.at[self.t.o, pl.ds(0, 192)] if i == 1 else ref.at[self.t.o]
        self.arrived(22 + i, view)


class Reduce(Sender):
    def __init__(self, t, w, rc_, r1, r2, r3, fin, fin2, out, windows, ss, rs):
        super().__init__(t, ss, rs)
        self.w, self.rc, self.r1, self.r2, self.r3 = w, rc_, r1, r2, r3
        self.fin, self.fin2, self.out, self.windows = fin, fin2, out, windows
        self.by_rows = fin2.shape[0] == 96

    def cut(self, ref, k, *lead):
        rows, cols = self.windows[k]
        lead += (slice(None),) * (len(ref.shape) - 2 - len(lead))
        return ref.at[lead + (pl.ds(*rows), pl.ds(*cols))]

    def pair(self, k):
        self.send(5 * k, self.cut(self.w, k, self.t.o), self.cut(self.rc, k), self.t.sib)

    def pair_rows(self, z):
        self.send(5 * z, self.w.at[self.t.o, z], self.rc.at[z], self.t.sib)

    def add(self, k, q, part):
        (r, rn), (a, an) = self.windows[k]
        w, c = self.w, self.t.c

        @pl.loop(0, 4)
        def _(z):
            at = (c, z, q, pl.ds(r, rn), pl.ds(a, an))
            w[at] = (w[at].astype(F32) + part[z, r : r + rn, a : a + an].astype(F32)).astype(w.dtype)

    def first(self, k):
        t = self.t
        if self.by_rows:
            for z in range(4 if k == 0 else 0):
                self.arrived(5 * z, self.rc.at[z])
        else:
            self.arrived(5 * k, self.cut(self.rc, k))
        for i, q in ((0, t.q2), (1, t.q12)):
            self.add(k, q, self.rc.at[:, q])
            self.send(
                5 * k + 1 + i, self.cut(self.w, k, t.c, slice(None), q), self.cut(self.r1, k, i, slice(None)), t.n2
            )
        for q in (t.q, t.q1):
            self.add(k, q, self.rc.at[:, q])

    def second(self, k):
        t = self.t
        self.arrived(5 * k + 2, self.cut(self.r1, k, 1, slice(None)))
        self.add(k, t.q1, self.r1.at[1])
        self.send(5 * k + 3, self.cut(self.w, k, t.c, slice(None), t.q1), self.cut(self.r2, k, slice(None)), t.n1)
        self.arrived(5 * k + 1, self.cut(self.r1, k, 0, slice(None)))
        self.add(k, t.q, self.r1.at[0])

    def third(self, k):
        t = self.t
        self.arrived(5 * k + 3, self.cut(self.r2, k, slice(None)))
        self.add(k, t.q, self.r2)
        for i in range(3):
            self.send(5 * k + 4, self.cut(self.w, k, t.c, t.zz[i], t.q), self.cut(self.r3, k, 2 - i), t.zn[i])

    def fourth(self, k):
        t = self.t
        (r, rn), (a, an) = self.windows[k]
        self.arrived(5 * k + 4, self.cut(self.r3, k, slice(None)))
        total = self.w[t.c, t.z, t.q, r : r + rn, a : a + an].astype(F32)
        for i in range(3):
            total = total + self.r3[i, r : r + rn, a : a + an].astype(F32)
        self.fin[r : r + rn, a : a + an] = total
        if k == len(self.windows) - 1:
            rd = self.fin.shape[0] // 2
            self.send(5 * len(self.windows), self.fin.at[off(t.o, rd, 8)], self.fin2, t.sib)

    def fifth(self):
        t = self.t
        rd, n2 = self.fin2.shape
        self.arrived(5 * len(self.windows), self.fin2)
        self.out[:, off(t.c, n2)] = self.fin[off(t.c, rd, 8), :]
        self.out[:, off(t.o, n2)] = self.fin2[...]


def dot(a, b):
    return jnp.dot(a, b, preferred_element_type=F32)


def dot_rt(a, b):
    return lax.dot_general(a, b, (((1,), (1,)), ((), ())), preferred_element_type=F32)


def dot_lt(a, b):
    return lax.dot_general(a, b, (((0,), (0,)), ((), ())), preferred_element_type=F32)


def normed(v):
    centred = v - jnp.mean(v, axis=-1, keepdims=True)
    inverse = lax.rsqrt(jnp.mean(centred * centred, axis=-1, keepdims=True) + epsilon)
    return centred * inverse, inverse


def norm_back(g, n, inverse, gain):
    v = g * gain
    return inverse * (
        v - jnp.mean(v, axis=-1, keepdims=True) - n * jnp.mean(v * n, axis=-1, keepdims=True)
    )


def gelu_pair(v):
    share = 0.5 * (1.0 + lax.erf(v * root_half))
    return v * share, share + v * jnp.exp(-0.5 * v * v) * inverse_root_tau


SIZES = ((24, 128, F32), (24, 1152, BF), (24, 384, BF), (24, 1536, BF), (96, 384, BF))
WINDOWS = (
    [((0, 48), (0, 128))],
    [((0, 48), (384 * j, 384)) for j in range(3)],
    [((0, 48), (0, 384))],
    [((0, 48), (384 * j, 384)) for j in range(4)],
    [((48 * j, 48), (0, 384)) for j in range(4)],
)
SCRATCH = {
    "got": [((rd, n2), dt) for rd, n2, dt in SIZES]
    + [((24, 2304), BF), ((24, 768), BF), ((24, 3072), BF), ((96, 384), BF)],
    "w": [((2, 4, 4, 2 * rd, n2), dt) for rd, n2, dt in SIZES],
    "fin": [((2 * rd, n2), F32) for rd, n2, dt in SIZES],
    "fin2": [((rd, n2), F32) for rd, n2, dt in SIZES],
    "rc": [((4, 4, 2 * rd, n2), dt) for rd, n2, dt in SIZES if n2 not in (1152, 384) or rd == 96],
    "r1": [((2, 4, 2 * rd, n2), dt) for rd, n2, dt in SIZES],
    "r2": [((4, 2 * rd, n2), dt) for rd, n2, dt in SIZES],
    "r3": [((3, 2 * rd, n2), dt) for rd, n2, dt in SIZES],
    "stage": [((4, 48, 3456), BF), ((4, 192, 384), BF)],
    "dpu": [((2, 4, 4, 48, 768), BF)],
    "do": [((2, 256, 384), BF)],
    "dd": [((2, 4, 192, 384), BF)],
    "tmask": [((4, 128), F32)],
    "dmask": [((1, 32), F32)],
    "vec": [((16, 768), F32)],
    "table": [((16, 2, 768), F32)],
    "pr": [((512, 2304), BF)],
    "ctx": [((512, 768), BF)],
    "sh": [((24, 256, 128), BF)],
    "n1": [((512, 768), BF)],
    "i1": [((512, 1), F32)],
    "n2": [((512, 768), BF)],
    "i2": [((512, 1), F32)],
    "fl": [((512, 768), BF)],
    "act": [((512, 3072), BF)],
    "gp": [((512, 3072), BF)],
    "row": [((512, 768), F32)],
    "low": [((512, 768), BF)],
    "ob": [((512, 768), BF)],
    "hid": [((256, 384), F32)],
    "src": [((2, 2, 768), F32)] * 2,
    "slots": [((16, 2, 768), F32)] * 4,
    "sdr": [((2, 4, 2, 768), F32)],
    "pairs": [((2, 2, 768), F32)] * 2,
    "soo": [((2, 768), F32)],
    "mat": [((32, 768), F32)] * 2,
    "ars": [((3, 32, 768), BF)],
    "gpc": [((64, 3072), BF)],
    "lowc": [((64, 768), BF)],
    "arb": [((3, 3, 32, 768), BF)],
    "fq": [((2, 4, 4, 32, 1280), BF)],
    "fz": [((2, 4, 32, 1536), BF)],
    "vg": [((128, 768), F32)],
    "flip": [((768, 128), F32)],
}
SEMS = {
    "gr0": (6,),
    "gr1": (16,),
    "gr2": (6,),
    "gr3": (21,),
    "gr4": (21,),
    "dr": (25,),
    "ls": (4,),
    "rr0": (6,),
    "rr1": (16,),
    "rr2": (6,),
    "rr3": (21,),
    "rr4": (21,),
    "xr": (9,),
    "fr": (15,),
    "er": (9,),
    "ss": (14,),
    "os": (11,),
    "ins": (12,),
}
INS = ("tok", "cot", "counts", "small", "sp", "so", "su", "sd", "dp", "dout", "du", "ddown")
OUTS = (
    ("out", (512, 768), BF),
    ("gin", (512, 768), F32),
    ("gsmall", (24, 256), F32),
    ("gsp", (24, 2304), F32),
    ("gso", (24, 768), F32),
    ("gsu", (24, 3072), F32),
    ("gsd", (96, 768), F32),
    ("gdp", (24, 2304), F32),
    ("gdo", (24, 768), F32),
    ("gdu", (24, 3072), F32),
    ("gdd", (96, 768), F32),
)


class Box:
    def put(self, name, ref):
        at = [out[0] for out in OUTS].index(name)
        d = pltpu.make_async_copy(ref, self.back[name], self.os.at[at])
        d.start()
        self.flying[name] = d

    def ready(self, *names):
        for name in names:
            self.coming[name].wait()


def kernel(*refs):
    b = Box()
    refs = list(refs)

    def take(n):
        got, refs[:n] = refs[:n], []
        return got

    b.far = {name: take(1)[0] for name in INS}
    b.back = {name: take(1)[0] for name, _, _ in OUTS}
    for name in INS:
        setattr(b, name, take(1)[0])
    for name, _, _ in OUTS[2:]:
        setattr(b, name, take(1)[0])
    for name, items in SCRATCH.items():
        got = take(len(items))
        setattr(b, name, got if len(got) > 1 else got[0])
    for name in SEMS:
        setattr(b, name, take(1)[0])
    b.credit, b.met, b.met2 = take(3)
    b.t = Spot()
    run(b)


FACTOR_WINDOWS = [((0, 32), (0, 512)), ((0, 32), (512, 384)), ((0, 32), (896, 384))]
LINE_WINDOWS = [(0, 768), (768, 384), (1152, 384)]


def run(b):
    t = b.t
    b.x = Sender(t, b.ss.at[0], b.xr)
    b.flying, b.coming = {}, {}
    for i, name in enumerate(INS):
        d = pltpu.make_async_copy(b.far[name], getattr(b, name), b.ins.at[i])
        d.start()
        b.coming[name] = d
    b.do[...] = jnp.zeros(b.do.shape, BF)
    b.vg[...] = jnp.zeros(b.vg.shape, F32)
    enter(t)
    pass_on(t, b.met)
    shards = (b.small, b.sp, b.so, b.su, b.sd)
    far = [b.far[name] for name in ("small", "sp", "so", "su", "sd")]
    gs = [
        Gather(t, far[i], shards[i], b.w[i], b.got[i], b.fin[i], WINDOWS[i], b.ss.at[1 + i], getattr(b, f"gr{i}"))
        for i in range(5)
    ]
    dg = DocGather(
        t,
        [b.far[name] for name in ("dp", "dout", "du", "ddown")],
        (b.dp, b.dout, b.du, b.ddown),
        b.stage,
        b.got[5:],
        (b.fin[1], b.fin[4]),
        b.dpu,
        b.do,
        b.dd,
        b.ss.at[6],
        b.dr,
        b.ls,
    )
    for g in gs:
        g.pair()
    dg.pair()
    b.f = Gather(t, None, None, b.fq, None, None, FACTOR_WINDOWS, b.ss.at[7], b.fr)
    b.e = LineGather(t, b.fz, LINE_WINDOWS, b.ss.at[8], b.er)

    events = [(g, k) for g in gs for k in range(len(g.windows))]
    lines = events + [(dg, k) for k in range(7)]
    clock, spreads, relays = [0], [0], [0]

    def do(name, at, among=events):
        if 0 <= at < len(among):
            getattr(among[at][0], name)(among[at][1])

    def relay(n):
        for _ in range(n):
            do("relay", relays[0], lines)
            relays[0] += 1
            do("spread", spreads[0], lines)
            spreads[0] += 1

    def tick(upto):
        while clock[0] <= upto:
            at = clock[0]
            busy = relays[0] < len(events)
            do("first", at)
            relay(1)
            do("second", at - 2)
            if busy:
                relay(1)
            do("third", at - 4)
            do("finish", at - 5)
            clock[0] += 1

    b.ready("small", "sp")
    gs[0].join()
    gs[1].join()
    for i in range(3):
        do("spread", i, lines)
    spreads[0] = 3
    b.ready("so", "su", "sd")
    for g in gs[2:]:
        g.join()
    pl.semaphore_wait(b.met, 4)
    pass_on(t, b.met2)
    relay(1)
    tick(0)
    b.ready("dp", "dout", "du", "ddown")
    dg.join()
    tick(1)
    pl.semaphore_wait(b.met2, 4)
    b.ready("cot", "tok", "counts")
    masks_in(b)
    send_cotangents(b)
    tick(5)
    vectors_in(b)
    tick(8)
    segment_project(b)
    tick(9)
    for seg in range(4):
        attend(b, seg)
        tick(10 + seg // 2)
    segment_mix(b)
    for j in range(4):
        segment_up(b, j)
        if j < 3:
            tick(12 + j)
    for k in range(4):
        dg.plane(k)
    tick(15)
    tick(16)
    for k in range(4, 7):
        dg.plane(k)
    tick(17)
    send_summaries(b, summary_rows(b))
    steps = document(b)
    segment_down(b, 0)
    segment_down(b, 1)
    dg.share()
    for g in gs:
        g.drain()
    for i in range(3):
        dg.finish(i)
    dg.drain()
    next(steps)
    second_back(b)
    next(steps)
    hidden_back(b)
    next(steps)
    first_back(b)
    next(steps)
    next(steps)
    next(steps, None)
    finish_output(b)
    b.f.spread(2)
    b.e.spread(2)

    small_rc, up_rc, down_rc = b.rc
    rcs = (small_rc, up_rc.at[:, :, :, 0:1152], up_rc.at[:, :, :, 1152:1536], up_rc, down_rc)
    rs = [
        Reduce(
            t,
            b.w[i],
            rcs[i],
            b.r1[i],
            b.r2[i],
            b.r3[i],
            b.fin[i],
            b.fin2[i],
            out,
            WINDOWS[i],
            b.ss.at[9 + i],
            getattr(b, f"rr{i}"),
        )
        for i, out in enumerate((b.gsmall, b.gsp, b.gso, b.gsu, b.gsd))
    ]
    for r, name in zip(rs, ("gsmall", "gsp", "gso", "gsu", "gsd")):
        r.name = name
    rsmall, rproject, routput, rup, rdown = rs
    terms = [(r, k) for r in (rdown, rup, routput, rproject, rsmall) for k in range(len(r.windows))]
    clock[0] = 0

    ends = {id(r): max(i for i, e in enumerate(terms) if e[0] is r) for r in rs}

    def tock(upto):
        while clock[0] <= upto:
            at = clock[0]
            do("first", at, terms)
            do("second", at - 2, terms)
            do("third", at - 4, terms)
            do("fourth", at - 6, terms)
            for r in rs:
                if ends[id(r)] == at - 7:
                    r.fifth()
                    b.put(r.name, r.out)
            clock[0] += 1

    second_back_rows(b)
    hidden_back_rows(b)
    b.f.relay(2)
    b.e.relay(2)
    b.f.second(1)
    b.f.third(0)
    down_terms(b, rdown)
    first_back_rows(b)
    b.f.first(2)
    b.e.first(2)
    b.f.third(1)
    tock(0)
    column_terms(b, rup, b.fl, b.gp)
    tock(1)
    b.f.second(2)
    mixed_back(b)
    tock(2)
    context_back(b)
    tock(3)
    b.f.third(2)
    attend_back(b, 0)
    tock(4)
    attend_back(b, 1)
    tock(5)
    attend_back(b, 2)
    tock(6)
    attend_back(b, 3)
    tock(7)
    pl.semaphore_signal(b.credit, inc=1, device_id=t.sib, device_id_type=MESH)
    pl.semaphore_wait(b.credit, 1)
    column_terms(b, routput, b.ctx, b.low)
    input_back(b)
    column_terms(b, rproject, b.tok, b.pr)
    tock(8)
    vectors_out(b)
    rsmall.pair(0)
    tock(10)
    document_terms(b)
    tock(len(terms) + 6)
    for r in rs:
        r.drain()
    b.x.drain()
    for d in b.flying.values():
        d.wait()


def send_cotangents(b):
    for m in range(2):
        for s in range(2):
            rows = b.cot[pl.ds(128 * (2 * m + s), 16), :].astype(F32)
            b.src[0][m, s : s + 1, :] = rows[0:1]
    send_rows(b, 0)


def send_rows(b, n):
    t, src, slots = b.t, b.src[n], b.slots[n]
    mine = src.at[t.half]
    other = src.at[1 - t.half]
    for k in (1, 2, 3):
        b.x.send(n, mine, slots.at[t.i], t.plane[k])
    for k in (0, 1, 2, 3):
        b.x.send(n, mine, slots.at[t.i], (4 * t.z + t.qq[k], t.o))
        b.x.send(n, other, slots.at[t.i], (4 * t.zo + t.qq[k], t.c))
        b.x.send(n, other, slots.at[t.i], (4 * t.zo + t.qq[k], t.o))
    slots[t.i] = src[t.half]


def take_rows(b, n):
    slots = b.slots[n]
    b.x.arrived(n, slots.at[pl.ds(0, 15)])
    for i in range(16):
        b.mat[n][2 * i : 2 * i + 2, :] = slots[i]
    return b.mat[n][...]


def vectors_in(b):
    small = b.w[0]
    b.vec[...] = jnp.transpose(small[0].reshape(768, 128))[0:16]
    table = jnp.transpose(small[1].reshape(768, 128))[0:32]
    for i in range(16):
        b.table[i] = table[2 * i : 2 * i + 2]


def masks_in(b):
    t = b.t
    rows = [b.counts[m : m + 1, :].astype(F32) for m in range(2)]
    lane = lax.broadcasted_iota(jnp.int32, (1, 64), 1)
    slot = lax.broadcasted_iota(jnp.int32, (1, 128), 1)
    for m in range(2):
        for s in range(2):
            own = jnp.sum(jnp.where(lane == 2 * t.dev + s, rows[m], 0.0), axis=1, keepdims=True)
            keep = (slot.astype(F32) < own) | (slot == 0)
            b.tmask[2 * m + s : 2 * m + s + 1, :] = jnp.where(keep, 1.0, 0.0)
    row = jnp.where(t.half == 0, rows[0], rows[1])
    row = jnp.where(lax.div(t.z, 2) == 0, row[:, 0:32], row[:, 32:64])
    b.dmask[...] = jnp.where(row > 0.0, 1.0, 0.0)


def vec(b, i):
    return b.vec[i : i + 1, :]


def segment_project(b):
    w = b.w[1]

    @pl.loop(0, 6)
    def _(i):
        h, j = lax.div(i, 3), lax.rem(i, 3)
        part = w[h, :, :, :, off(j, 384)].reshape(768, 384)
        b.pr[:, off(i, 384)] = dot(b.tok[...], part).astype(BF)


def lane_masks():
    lane = lax.broadcasted_iota(jnp.int32, (1, 128), 1)
    low = (lane < 64).astype(F32)
    return low.astype(BF), (1.0 - low).astype(BF)


def attend(b, seg):
    low, high = lane_masks()
    keep = b.tmask[seg : seg + 1, :] > 0.0
    rows = pl.ds(128 * seg, 128)

    @pl.loop(0, 6)
    def _(p):
        q2 = b.pr[rows, off(p, 128)]
        k2 = b.pr[rows, off(p + 6, 128)]
        v2 = b.pr[rows, off(p + 12, 128)]
        qs = jnp.concatenate((q2 * low, q2 * high), axis=0)
        scores = jnp.where(keep, dot_rt(qs, k2) * 0.125, floor_score)
        raised = jnp.exp(scores - jnp.max(scores, axis=-1, keepdims=True))
        shares = (raised * (1.0 / jnp.sum(raised, axis=-1, keepdims=True))).astype(BF)
        b.sh[6 * seg + p] = shares
        both = dot(shares, v2)
        lane = lax.broadcasted_iota(jnp.int32, (128, 128), 1)
        b.ctx[rows, off(p, 128)] = jnp.where(lane < 64, both[:128], both[128:]).astype(BF)


def segment_mix(b):
    w = b.w[2]
    for r in range(2):
        rows = pl.ds(256 * r, 256)
        for h in range(2):
            b.row[rows, pl.ds(384 * h, 384)] = dot(b.ctx[rows, :], w[h].reshape(768, 384))
    scale, offset = vec(b, 0), vec(b, 1)

    @pl.loop(0, 16)
    def _(i):
        rows = off(i, 32, 32)
        n, inverse = normed(b.tok[rows, :].astype(F32) + b.row[rows, :])
        first = n * scale + offset
        b.n1[rows, :] = n.astype(BF)
        b.i1[rows, :] = inverse
        b.row[rows, :] = first
        b.fl[rows, :] = first.astype(BF)


def segment_up(b, j):
    w = b.w[3]
    for h, r in ((0, 0), (0, 1), (1, 0), (1, 1)):
        up = w[h, :, :, :, pl.ds(384 * j, 384)].reshape(768, 384)
        b.hid[...] = dot(b.fl[256 * r : 256 * r + 256, :], up)
        cols = pl.ds(1536 * h + 384 * j, 384)

        @pl.loop(0, 8)
        def _(i):
            rows = off(i + 8 * r, 32, 32)
            value, slope = gelu_pair(b.hid[off(i, 32, 32), :])
            b.act[rows, cols] = value.astype(BF)
            b.gp[rows, cols] = slope.astype(BF)


def summary_rows(b):
    w = b.w[4]
    for s in range(4):
        b.gpc[16 * s : 16 * s + 16, :] = b.act[128 * s : 128 * s + 16, :]
    parts = [dot(b.gpc[...], w[h].reshape(3072, 384)) for h in range(2)]
    both = jnp.concatenate(parts, axis=1)
    for s in range(4):
        b.gpc[16 * s : 16 * s + 16, :] = b.gp[128 * s : 128 * s + 16, :]
    rows = []
    for s in range(4):
        n, _ = normed(b.row[128 * s : 128 * s + 8, :] + both[16 * s : 16 * s + 8])
        rows.append((n * vec(b, 2) + vec(b, 3))[0:1])
    return rows


def segment_down(b, r):
    w = b.w[4]
    rows = pl.ds(256 * r, 256)

    @pl.loop(0, 2)
    def _(h):
        b.row[rows, off(h, 384)] += dot(b.act[rows, :], w[h].reshape(3072, 384))

    gain, shift = vec(b, 2), vec(b, 3)

    @pl.loop(8 * r, 8 * r + 8)
    def _(i):
        rows = off(i, 32, 32)
        n, inverse = normed(b.row[rows, :])
        b.n2[rows, :] = n.astype(BF)
        b.i2[rows, :] = inverse
        b.ob[rows, :] = (n * gain + shift).astype(BF)


def send_summaries(b, rows):
    places = b.table[b.t.i]
    for m in range(2):
        for s in range(2):
            b.src[1][m, s : s + 1, :] = rows[2 * m + s] + places[s : s + 1]
    send_rows(b, 1)


def plane_send(b, n, partial):
    b.ars[n] = partial.astype(BF)
    for k in (1, 2, 3):
        b.x.send(2 + n, b.ars.at[n], b.arb.at[n, k - 1], b.t.plane[k])


def plane_take(b, n):
    b.x.arrived(2 + n, b.arb.at[n])
    total = b.ars[n].astype(F32)
    for k in range(3):
        total = total + b.arb[n, k].astype(F32)
    return total


def document(b):
    t = b.t
    dp = b.dpu[0].reshape(768, 768)
    du = b.dpu[1].reshape(768, 768)
    lane = lax.broadcasted_iota(jnp.int32, (1, 256), 1)
    heads = [((lane >= 64 * h) & (lane < 64 * h + 64)).astype(F32).astype(BF) for h in range(3)]
    keep = b.dmask[...] > 0.0
    h_in = take_rows(b, 1)
    h_low = h_in.astype(BF)
    pr = dot(h_low, dp).astype(BF)
    q3, k3, v3 = pr[:, 0:256], pr[:, 256:512], pr[:, 512:768]
    qs = jnp.concatenate([q3 * m for m in heads], axis=0)
    scores = jnp.where(keep, dot_rt(qs, k3) * 0.125, floor_score)
    raised = jnp.exp(scores - jnp.max(scores, axis=-1, keepdims=True))
    shares = raised * (1.0 / jnp.sum(raised, axis=-1, keepdims=True))
    shares_low = shares.astype(BF)
    three = dot(shares_low, v3)
    ctx = sum(three[32 * h : 32 * h + 32] * heads[h].astype(F32) for h in range(3)).astype(BF)
    mixed = jnp.concatenate([dot(ctx, b.do[h]) for h in range(2)], axis=1)
    plane_send(b, 0, mixed)
    yield
    n1, i1 = normed(h_in + plane_take(b, 0))
    first = n1 * vec(b, 4) + vec(b, 5)
    first_low = first.astype(BF)
    active, slope = gelu_pair(dot(first_low, du))
    active = active.astype(BF)
    branch = jnp.concatenate([dot(active, b.dd[h].reshape(768, 384)) for h in range(2)], axis=1)
    plane_send(b, 1, branch)

    @pl.when(t.c == 0)
    def _():
        b.fq[0, t.z, t.q, :, 0:512] = active[:, 0:512]
        b.fz[0, t.z, :, 0:768] = h_low

    @pl.when(t.c == 1)
    def _():
        b.fq[1, t.z, t.q, :, 0:256] = active[:, 512:768]
        b.fq[1, t.z, t.q, :, 256:512] = ctx
        b.fz[1, t.z, :, 0:768] = first_low

    b.f.spread(0)
    b.e.spread(0)
    yield
    n2, i2 = normed(first + plane_take(b, 1))
    out = n2 * vec(b, 6) + vec(b, 7)
    g = take_rows(b, 0)
    delta = norm_back(g, n2, i2, vec(b, 6))
    branch_low = delta.astype(BF)
    back = sum(dot_rt(branch_low[:, 384 * h : 384 * h + 384], b.dd[h].reshape(768, 384)) for h in range(2))
    hidden_delta = (back * slope).astype(BF)
    plane_send(b, 2, dot_rt(hidden_delta, du))
    b.vg[6:7, :] = jnp.sum(g * n2, axis=0, keepdims=True) * 0.125
    b.vg[7:8, :] = jnp.sum(g, axis=0, keepdims=True) * 0.125
    for i in range(16):
        b.slots[2][i] = out[2 * i : 2 * i + 2]
    other_i = 8 * (1 - t.half) + 2 * t.q + t.c
    b.x.send(6, b.slots[2].at[other_i], b.soo, (4 * t.zo + t.q, t.c))

    def halves(ref, at, value):
        for h in range(2):

            @pl.when(t.c == h)
            def _():
                ref[(h,) + at] = value[:, 384 * h : 384 * h + 384]

    halves(b.fq, (t.z, t.q, slice(None), slice(512, 896)), hidden_delta)
    halves(b.fz, (t.z, slice(None), slice(768, 1152)), branch_low)
    b.f.relay(0)
    b.e.relay(0)
    b.f.spread(1)
    b.e.spread(1)
    yield
    first_delta = delta + plane_take(b, 2)
    mixed_delta = norm_back(first_delta, n1, i1, vec(b, 4))
    mixed_low = mixed_delta.astype(BF)
    ctx_delta = sum(dot_rt(mixed_low[:, 384 * h : 384 * h + 384], b.do[h]) for h in range(2)).astype(BF)
    cs = jnp.concatenate([ctx_delta * m for m in heads], axis=0)
    shares_delta = dot_rt(cs, v3)
    inner = jnp.sum(shares_delta * shares, axis=-1, keepdims=True)
    scores_delta = (shares * (shares_delta - inner)).astype(BF)
    dq3 = dot(scores_delta, k3) * 0.125
    dq = sum(dq3[32 * h : 32 * h + 32] * heads[h].astype(F32) for h in range(3))
    dk = dot_lt(scores_delta, qs) * 0.125
    dv = dot_lt(shares_low, cs)
    pd = jnp.concatenate((dq, dk, dv), axis=1).astype(BF)
    h_delta = dot_rt(pd, dp) + 0.25 * mixed_delta
    for i in range(16):
        b.slots[3][i] = h_delta[2 * i : 2 * i + 2]
    for k in (0, 1, 2, 3):
        if k:
            b.x.send(7, b.slots[3].at[8 * t.half + 2 * t.qq[k] + t.c], b.sdr.at[0, k], t.plane[k])
        b.x.send(
            8, b.slots[3].at[8 * (1 - t.half) + 2 * t.qq[k] + t.c], b.sdr.at[1, k], (4 * t.zo + t.qq[k], t.c)
        )
    b.sdr[0, 0] = b.slots[3][t.i]
    b.vg[4:5, :] = jnp.sum(first_delta * n1, axis=0, keepdims=True) * 0.125
    b.vg[5:6, :] = jnp.sum(first_delta, axis=0, keepdims=True) * 0.125
    halves(b.fq, (t.z, t.q, slice(None), slice(896, 1280)), pd)
    halves(b.fz, (t.z, slice(None), slice(1152, 1536)), mixed_low)
    b.f.relay(1)
    b.e.relay(1)
    b.f.first(0)
    b.e.first(0)
    yield
    b.f.second(0)
    b.x.arrived(6, b.soo)
    b.pairs[0][t.half] = b.slots[2][t.i]
    b.pairs[0][1 - t.half] = b.soo[...]
    yield
    b.x.arrived(7, b.sdr.at[0, pl.ds(0, 3)])
    b.x.arrived(8, b.sdr.at[1])
    b.pairs[1][t.half] = b.sdr[0, 0] + b.sdr[0, 1] + b.sdr[0, 2] + b.sdr[0, 3]
    b.pairs[1][1 - t.half] = b.sdr[1, 0] + b.sdr[1, 1] + b.sdr[1, 2] + b.sdr[1, 3]
    b.f.first(1)
    b.e.first(1)


def finish_output(b):
    first_row = lax.broadcasted_iota(jnp.int32, (16, 768), 0) == 0
    for m in range(2):
        for s in range(2):
            rows = pl.ds(128 * (2 * m + s), 16)
            fresh = jnp.where(first_row, b.pairs[0][m, s : s + 1, :], b.ob[rows, :].astype(F32))
            b.ob[rows, :] = fresh.astype(BF)
    b.put("out", b.ob)


def second_back(b):
    gain = vec(b, 2)

    def body(i, carry):
        gains, shifts = carry
        rows = off(i, 16, 16)
        late = (lax.broadcasted_iota(jnp.int32, (16, 768), 0) + 16 * lax.rem(i, 8)) == 0
        g = jnp.where(late, 0.0, b.cot[rows, :].astype(F32))
        n = b.n2[rows, :].astype(F32)
        delta = norm_back(g, n, b.i2[rows, :], gain)
        b.row[rows, :] = delta
        b.low[rows, :] = delta.astype(BF)
        return gains + g * n, shifts + g

    zero = jnp.zeros((16, 768), F32)
    gains, shifts = lax.fori_loop(0, 32, body, (zero, zero))
    b.vg[2:3, :] = jnp.sum(gains, axis=0, keepdims=True)
    b.vg[3:4, :] = jnp.sum(shifts, axis=0, keepdims=True)


def second_back_rows(b):
    gain = vec(b, 2)
    top = lax.broadcasted_iota(jnp.int32, (16, 768), 0) == 0
    gains, shifts = b.vg[2:3, :], b.vg[3:4, :]
    for s in range(4):
        rows = slice(128 * s, 128 * s + 16)
        g = b.pairs[1][s // 2, s % 2 : s % 2 + 1, :]
        n = b.n2[rows, :].astype(F32)
        delta = norm_back(jnp.where(top, g, 0.0), n, b.i2[rows, :], gain)
        b.row[rows, :] = jnp.where(top, delta, b.row[rows, :])
        low = jnp.where(top, delta, b.low[rows, :].astype(F32)).astype(BF)
        b.low[rows, :] = low
        b.lowc[16 * s : 16 * s + 16, :] = low
        gains += g * n[0:1]
        shifts += g
    b.vg[2:3, :] = gains
    b.vg[3:4, :] = shifts


def hidden_back_rows(b):
    w = b.w[4]

    @pl.loop(0, 4)
    def _(z):
        cols = off(z, 768)
        back = dot_rt(b.lowc[:, 0:384], w[0, z].reshape(768, 384)) + dot_rt(
            b.lowc[:, 384:768], w[1, z].reshape(768, 384)
        )
        delta = (back * b.gpc[:, cols].astype(F32)).astype(BF)
        b.gpc[:, cols] = delta
        for s in range(4):
            b.gp[pl.ds(128 * s, 16), cols] = delta[16 * s : 16 * s + 16]


def first_back_rows(b):
    w = b.w[3]
    top = lax.broadcasted_iota(jnp.int32, (16, 768), 0) == 0
    more = dot_rt(b.gpc[:, 0:1536], w[0].reshape(768, 1536)) + dot_rt(
        b.gpc[:, 1536:3072], w[1].reshape(768, 1536)
    )
    for s in range(4):
        rows = slice(128 * s, 128 * s + 16)
        b.row[rows, :] += jnp.where(top, more[16 * s : 16 * s + 16], 0.0)


def hidden_back(b):
    w = b.w[4]

    @pl.loop(0, 4)
    def _(z):
        cols = off(z, 768)
        for r in range(2):
            rows = pl.ds(256 * r, 256)
            back = dot_rt(b.low[rows, 0:384], w[0, z].reshape(768, 384)) + dot_rt(
                b.low[rows, 384:768], w[1, z].reshape(768, 384)
            )
            b.gp[rows, cols] = (back * b.gp[rows, cols].astype(F32)).astype(BF)


def down_terms(b, r):
    t, w = b.t, b.w[4]
    for h in (t.o, t.c):
        for z in range(4):
            part = dot_lt(b.act[:, 768 * z : 768 * z + 768], b.low[:, off(h, 384)])
            w[h, z] = part.astype(BF).reshape(4, 192, 384)
            if h is t.o:
                r.pair_rows(z)


def first_back(b):
    w = b.w[3]

    @pl.loop(0, 2)
    def _(r):
        rows = off(r, 256, 256)
        for h in range(2):
            b.row[rows, :] += dot_rt(b.gp[rows, 1536 * h : 1536 * h + 1536], w[h].reshape(768, 1536))


def mixed_back(b):
    scale = vec(b, 0)

    def body(i, carry):
        scales, offsets = carry
        rows = off(i, 16, 16)
        g = b.row[rows, :]
        n = b.n1[rows, :].astype(F32)
        delta = norm_back(g, n, b.i1[rows, :], scale)
        b.row[rows, :] = delta
        b.low[rows, :] = delta.astype(BF)
        return scales + g * n, offsets + g

    zero = jnp.zeros((16, 768), F32)
    scales, offsets = lax.fori_loop(0, 32, body, (zero, zero))
    b.vg[0:1, :] = jnp.sum(scales, axis=0, keepdims=True)
    b.vg[1:2, :] = jnp.sum(offsets, axis=0, keepdims=True)


def context_back(b):
    w = b.w[2]
    b.flying.pop("out").wait()
    for r in range(2):
        rows = pl.ds(256 * r, 256)
        back = dot_rt(b.low[rows, 0:384], w[0].reshape(768, 384)) + dot_rt(
            b.low[rows, 384:768], w[1].reshape(768, 384)
        )
        b.ob[rows, :] = back.astype(BF)


def attend_back(b, seg):
    low, high = lane_masks()
    rows = pl.ds(128 * seg, 128)

    @pl.loop(0, 6)
    def _(p):
        q2 = b.pr[rows, off(p, 128)]
        k2 = b.pr[rows, off(p + 6, 128)]
        v2 = b.pr[rows, off(p + 12, 128)]
        d2 = b.ob[rows, off(p, 128)]
        qs = jnp.concatenate((q2 * low, q2 * high), axis=0)
        cs = jnp.concatenate((d2 * low, d2 * high), axis=0)
        shares_low = b.sh[6 * seg + p]
        shares = shares_low.astype(F32)
        shares_delta = dot_rt(cs, v2)
        inner = jnp.sum(shares_delta * shares, axis=-1, keepdims=True)
        scores_delta = (shares * (shares_delta - inner)).astype(BF)
        dq = dot(scores_delta, k2) * 0.125
        lane = lax.broadcasted_iota(jnp.int32, (128, 128), 1)
        b.pr[rows, off(p, 128)] = jnp.where(lane < 64, dq[:128], dq[128:]).astype(BF)
        b.pr[rows, off(p + 6, 128)] = (dot_lt(scores_delta, qs) * 0.125).astype(BF)
        b.pr[rows, off(p + 12, 128)] = dot_lt(shares_low, cs).astype(BF)


def input_back(b):
    w = b.w[1]

    @pl.loop(0, 2)
    def _(r):
        rows = off(r, 256, 256)
        for h in range(2):
            b.row[rows, :] += dot_rt(b.pr[rows, 1152 * h : 1152 * h + 1152], w[h].reshape(768, 1152))

    b.put("gin", b.row)


def column_terms(b, r, left, right):
    t, w = b.t, r.w
    n = len(r.windows)
    for h in (t.o, t.c):
        for j in range(n):
            part = dot_lt(left[...], right[:, off(n * h + j, 384)])
            w[h, :, :, :, pl.ds(384 * j, 384)] = part.astype(BF).reshape(4, 4, 48, 384)
            if h is t.o:
                r.pair(j)


def vectors_out(b):
    t, w = b.t, b.w[0]
    w[0] = jnp.transpose(b.vg[...]).reshape(4, 4, 48, 128)
    row = lax.broadcasted_iota(jnp.int32, (32, 768), 0)
    both = b.pairs[1][0] + b.pairs[1][1]
    places = jnp.where(row == 2 * t.i, both[0:1], 0.0) + jnp.where(row == 2 * t.i + 1, both[1:2], 0.0)
    b.vg[0:32, :] = places
    w[1] = jnp.transpose(b.vg[...]).reshape(4, 4, 48, 128)


def document_terms(b):
    t = b.t
    for k in range(3):
        b.f.finish(k)
        b.e.finish(k)
    b.f.drain()
    b.e.drain()
    own = 24 * t.dev
    part = 24 * lax.rem(t.dev, 8)
    fq, fz = b.fq, b.fz

    def rows_of(value, at, size):
        n = value.shape[1]
        b.flip[0:n, :] = jnp.transpose(value.astype(F32))
        return b.flip[pl.ds(pl.multiple_of(at, 8), size), :].astype(BF)

    def line(a):
        both = [fz[h, :, :, a : a + 384].reshape(128, 384) for h in range(2)]
        return jnp.concatenate(both, axis=1)

    def rank(q, a):
        both = [fq[h, :, q, :, a : a + 384].reshape(128, 384) for h in range(2)]
        return jnp.concatenate(both, axis=1)

    left = rows_of(fz[0, :, :, 0:768].reshape(128, 768), own, 24)
    for q in range(4):
        part_q = dot(left, rank(q, 896))
        for g in range(3):
            b.gdp[:, 768 * g + 192 * q : 768 * g + 192 * q + 192] = part_q[:, 256 * g : 256 * g + 192]
    left = rows_of(fq[1, :, t.z, :, 256:512].reshape(128, 256), part, 24)
    b.gdo[...] = dot(left, line(1152))
    left = rows_of(fz[1, :, :, 0:768].reshape(128, 768), own, 24)
    for q in range(4):
        b.gdu[:, 768 * q : 768 * q + 768] = dot(left, rank(q, 512))
    active = jnp.concatenate((fq[0, :, t.z, :, 0:512], fq[1, :, t.z, :, 0:256]), axis=-1)
    left = rows_of(active.reshape(128, 768), 4 * part, 96)
    b.gdd[...] = dot(left, line(768))
    for name in ("gdp", "gdo", "gdu", "gdd"):
        b.put(name, getattr(b, name))


def mega(*arrays):
    an = pl.BlockSpec(memory_space=pl.ANY)
    return pl.pallas_call(
        kernel,
        out_shape=[jax.ShapeDtypeStruct(shape, dt) for _, shape, dt in OUTS],
        in_specs=[an] * len(INS),
        out_specs=[an] * len(OUTS),
        scratch_shapes=[pltpu.VMEM(item.shape, item.dtype) for item in arrays]
        + [pltpu.VMEM(shape, dt) for _, shape, dt in OUTS[2:]]
        + [pltpu.VMEM(shape, dt) for items in SCRATCH.values() for shape, dt in items]
        + [pltpu.SemaphoreType.DMA(shape) for shape in SEMS.values()]
        + [pltpu.SemaphoreType.REGULAR] * 3,
        compiler_params=pltpu.CompilerParams(
            collective_id=1, has_side_effects=True, vmem_limit_bytes=65200 * 1024
        ),
    )(*arrays)


def hand_on_kernel(*refs):
    n = (len(refs) - 2) // 3
    src, dst, mid = refs[:n], refs[n : 2 * n], refs[2 * n : 3 * n]
    ins = [pltpu.make_async_copy(src[i], mid[i], refs[-2].at[i]) for i in range(n)]
    outs = [pltpu.make_async_copy(mid[i], dst[i], refs[-1].at[i]) for i in range(n)]
    for d in ins:
        d.start()
    for i in range(n):
        ins[i].wait()
        outs[i].start()
    for d in outs:
        d.wait()


def hand_on(*arrays):
    an = pl.BlockSpec(memory_space=pl.ANY)
    n = len(arrays)
    return pl.pallas_call(
        hand_on_kernel,
        out_shape=[jax.ShapeDtypeStruct(item.shape, item.dtype) for item in arrays],
        in_specs=[an] * n,
        out_specs=[an] * n,
        scratch_shapes=[pltpu.VMEM(item.shape, item.dtype) for item in arrays]
        + [pltpu.SemaphoreType.DMA((n,))] * 2,
        compiler_params=pltpu.CompilerParams(vmem_limit_bytes=63 * 2**20),
    )(*arrays)


def local_fast(tokens, token_counts, *rest):
    weights, cotangent = rest[:17], rest[17]
    width = tokens.shape[-1]
    rows = weights[0].shape[0]
    lane = jnp.arange(256)[None]
    small = jnp.pad(weights[16], ((0, 0), (128, 96)))
    for at, i in enumerate((4, 5, 6, 7, 12, 13, 14, 15)):
        small = jnp.where(lane == at, weights[i][:, None], small)
    small = small.astype(F32)
    outs = mega(
        tokens.reshape(-1, width),
        cotangent.reshape(-1, width),
        token_counts,
        small,
        *weights[:4],
        *weights[8:12],
    )
    gsmall = outs[2]
    out, gin, gsp, gso, gsu, gsd, gdp, gdo, gdu, gdd = hand_on(*outs[:2], *outs[3:])
    return (
        (out.reshape(tokens.shape), gin.reshape(tokens.shape), gsp, gso, gsu, gsd)
        + tuple(gsmall[:, i] for i in range(4))
        + (gdp, gdo, gdu, gdd)
        + tuple(gsmall[:, i] for i in range(4, 8))
        + (gsmall[:, 128:160],)
    )


def partner_2(value, axis, distance):
    mask = 2**distance
    pairs = [(source, source ^ mask) for source in range(lax.axis_size(axis))]
    return lax.ppermute(value, axis, pairs)


def product(left, right):
    return jnp.dot(left, right, preferred_element_type=jnp.float32)


def left_product(left, right):
    return lax.dot_general(
        left, right, (((0,), (0,)), ((), ())), preferred_element_type=jnp.float32
    )


def right_product(left, right):
    return lax.dot_general(
        left, right, (((1,), (1,)), ((), ())), preferred_element_type=jnp.float32
    )


def gelu_value(value):
    return 0.5 * value * (1.0 + lax.erf(value * root_half))


def gelu_slope(value):
    return (
        0.5 * (1.0 + lax.erf(value * root_half))
        + value * jnp.exp(-0.5 * value * value) * inverse_root_tau
    )


def norm_forward(value, gain, shift):
    centred = value - jnp.mean(value, axis=-1, keepdims=True)
    inverse = lax.rsqrt(jnp.mean(centred * centred, axis=-1, keepdims=True) + epsilon)
    normed = centred * inverse
    return (normed * gain + shift, normed, inverse)


def norm_backward(delta_out, normed, inverse, gain):
    scaled = delta_out * gain
    delta_in = inverse * (
        scaled
        - jnp.mean(scaled, axis=-1, keepdims=True)
        - normed * jnp.mean(scaled * normed, axis=-1, keepdims=True)
    )
    return (delta_in, jnp.sum(delta_out * normed, axis=0), jnp.sum(delta_out, axis=0))


def masked_scores(queries, keys, valid):
    scale = 1.0 / math.sqrt(queries.shape[-1])
    scores = (
        jnp.einsum("bqhe,bkhe->bhqk", queries, keys, preferred_element_type=jnp.float32) * scale
    )
    return jnp.where(valid[:, None], scores, floor_score)


def attend_forward(queries, keys, values, valid):
    scores = masked_scores(queries, keys, valid)
    highest = jnp.max(scores, axis=-1, keepdims=True)
    log_total = highest + jnp.log(jnp.sum(jnp.exp(scores - highest), axis=-1, keepdims=True))
    shares = jnp.exp(scores - log_total).astype(jnp.bfloat16)
    context = jnp.einsum("bhqk,bkhe->bqhe", shares, values, preferred_element_type=jnp.float32)
    return (context.astype(jnp.bfloat16), log_total)


def attend_backward(delta_context, queries, keys, values, valid, log_total):
    scale = 1.0 / math.sqrt(queries.shape[-1])
    shares = jnp.exp(masked_scores(queries, keys, valid) - log_total)
    delta_shares = jnp.einsum(
        "bqhe,bkhe->bhqk", delta_context, values, preferred_element_type=jnp.float32
    )
    delta_values = jnp.einsum(
        "bhqk,bqhe->bkhe",
        shares.astype(jnp.bfloat16),
        delta_context,
        preferred_element_type=jnp.float32,
    )
    inner = jnp.sum(delta_shares * shares, axis=-1, keepdims=True)
    delta_scores = (shares * (delta_shares - inner)).astype(jnp.bfloat16)
    delta_queries = (
        jnp.einsum("bhqk,bkhe->bqhe", delta_scores, keys, preferred_element_type=jnp.float32)
        * scale
    )
    delta_keys = (
        jnp.einsum("bhqk,bqhe->bkhe", delta_scores, queries, preferred_element_type=jnp.float32)
        * scale
    )
    return (delta_queries, delta_keys, delta_values)


def block_forward(inputs, layer, attend):
    (
        project_weight,
        output_weight,
        up_weight,
        down_weight,
        first_gain,
        first_shift,
        second_gain,
        second_shift,
    ) = layer
    inputs_low = inputs.astype(jnp.bfloat16)
    projected = product(inputs_low, project_weight).astype(jnp.bfloat16)
    context, attend_kept = attend(projected)
    mixed = product(context, output_weight)
    first, first_normed, first_inverse = norm_forward(
        inputs + mixed, first_gain.astype(jnp.float32), first_shift.astype(jnp.float32)
    )
    first_low = first.astype(jnp.bfloat16)
    hidden = product(first_low, up_weight)
    active = gelu_value(hidden).astype(jnp.bfloat16)
    second, second_normed, second_inverse = norm_forward(
        first + product(active, down_weight),
        second_gain.astype(jnp.float32),
        second_shift.astype(jnp.float32),
    )
    kept = (
        inputs_low,
        projected,
        context,
        attend_kept,
        first_normed,
        first_inverse,
        first_low,
        hidden,
        active,
        second_normed,
        second_inverse,
    )
    return (second, kept)


def block_backward(delta_out, kept, layer, attend_back):
    (
        project_weight,
        output_weight,
        up_weight,
        down_weight,
        first_gain,
        first_shift,
        second_gain,
        second_shift,
    ) = layer
    (
        inputs_low,
        projected,
        context,
        attend_kept,
        first_normed,
        first_inverse,
        first_low,
        hidden,
        active,
        second_normed,
        second_inverse,
    ) = kept
    delta_second, second_gain_delta, second_shift_delta = norm_backward(
        delta_out, second_normed, second_inverse, second_gain.astype(jnp.float32)
    )
    branch_low = delta_second.astype(jnp.bfloat16)
    delta_down = left_product(active, branch_low)
    delta_hidden = (right_product(branch_low, down_weight) * gelu_slope(hidden)).astype(
        jnp.bfloat16
    )
    delta_up = left_product(first_low, delta_hidden)
    delta_first = delta_second + right_product(delta_hidden, up_weight)
    delta_mixed, first_gain_delta, first_shift_delta = norm_backward(
        delta_first, first_normed, first_inverse, first_gain.astype(jnp.float32)
    )
    mixed_low = delta_mixed.astype(jnp.bfloat16)
    delta_output = left_product(context, mixed_low)
    delta_context = right_product(mixed_low, output_weight).astype(jnp.bfloat16)
    delta_projected = attend_back(delta_context, projected, attend_kept)
    delta_project = left_product(inputs_low, delta_projected)
    delta_inputs = delta_mixed + right_product(delta_projected, project_weight)
    return (
        delta_inputs,
        (
            delta_project,
            delta_output,
            delta_up,
            delta_down,
            first_gain_delta,
            first_shift_delta,
            second_gain_delta,
            second_shift_delta,
        ),
    )


def local(
    tokens,
    token_counts,
    segment_project,
    segment_output,
    segment_up,
    segment_down,
    segment_scale,
    segment_offset,
    segment_gain,
    segment_shift,
    document_project,
    document_output,
    document_up,
    document_down,
    document_scale,
    document_offset,
    document_gain,
    document_shift,
    position,
    cotangent,
):
    batches, segments, length, width = tokens.shape
    heads = HEADS
    head_width = width // heads
    rows_total = segments * length
    index = lax.axis_index(("seg", "rep"))
    first_segment = index * segments
    own_document = first_segment // DOC_SEGS
    positions = jnp.arange(length)
    slots = (first_segment + jnp.arange(segments)) % DOC_SEGS
    picker = (slots[:, None] == jnp.arange(DOC_SEGS)[None, :]).astype(jnp.float32)
    levels = (DOC_SEGS // segments).bit_length() - 1
    gathered_once = (
        lax.all_gather(segment_project, ("seg", "rep"), axis=0, tiled=True),
        lax.all_gather(segment_output, ("seg", "rep"), axis=0, tiled=True),
        lax.all_gather(segment_up, ("seg", "rep"), axis=0, tiled=True),
        lax.all_gather(segment_down, ("seg", "rep"), axis=0, tiled=True),
        lax.all_gather(segment_scale, ("seg", "rep"), axis=0, tiled=True),
        lax.all_gather(segment_offset, ("seg", "rep"), axis=0, tiled=True),
        lax.all_gather(segment_gain, ("seg", "rep"), axis=0, tiled=True),
        lax.all_gather(segment_shift, ("seg", "rep"), axis=0, tiled=True),
        lax.all_gather(document_project, ("seg", "rep"), axis=0, tiled=True),
        lax.all_gather(document_output, ("seg", "rep"), axis=0, tiled=True),
        lax.all_gather(document_up, ("seg", "rep"), axis=0, tiled=True),
        lax.all_gather(document_down, ("seg", "rep"), axis=0, tiled=True),
        lax.all_gather(document_scale, ("seg", "rep"), axis=0, tiled=True),
        lax.all_gather(document_offset, ("seg", "rep"), axis=0, tiled=True),
        lax.all_gather(document_gain, ("seg", "rep"), axis=0, tiled=True),
        lax.all_gather(document_shift, ("seg", "rep"), axis=0, tiled=True),
        lax.all_gather(position, ("seg", "rep"), axis=0, tiled=True),
    )
    outputs = []
    deltas = []
    totals = None
    for batch in range(batches):
        segment_layer = gathered_once[0:8]
        document_layer = gathered_once[8:16]
        table = jnp.transpose(gathered_once[16].astype(jnp.float32))
        counts_row = token_counts[batch]
        local_counts = lax.dynamic_slice_in_dim(counts_row, first_segment, segments)
        token_valid = (positions[None, :] < local_counts[:, None]) | (positions[None, :] == 0)
        segment_valid = token_valid[:, None, :]

        def segment_attend(projected):
            parts = projected.reshape(segments, length, 3, heads, head_width)
            context, log_total = attend_forward(
                parts[:, :, 0], parts[:, :, 1], parts[:, :, 2], segment_valid
            )
            return (context.reshape(rows_total, width), log_total)

        def segment_back(delta_context, projected, log_total):
            parts = projected.reshape(segments, length, 3, heads, head_width)
            delta_queries, delta_keys, delta_values = attend_backward(
                delta_context.reshape(segments, length, heads, head_width),
                parts[:, :, 0],
                parts[:, :, 1],
                parts[:, :, 2],
                segment_valid,
                log_total,
            )
            return (
                jnp.stack((delta_queries, delta_keys, delta_values), axis=2)
                .reshape(rows_total, 3 * width)
                .astype(jnp.bfloat16)
            )

        def document_attend(projected):
            queries = projected[:, :width].reshape(1, segments, heads, head_width)
            pairs = projected[:, width:]
            collected = pairs[None]
            for bit in range(levels):
                partner = partner_2(collected, ("seg", "rep"), bit)
                upper = jnp.right_shift(index, bit) % 2
                collected = jnp.where(
                    upper == 0,
                    jnp.concatenate((collected, partner), axis=0),
                    jnp.concatenate((partner, collected), axis=0),
                )
            collected = collected.reshape(DOC_SEGS, 2 * width)
            key_valid = lax.dynamic_slice_in_dim(counts_row, own_document * DOC_SEGS, DOC_SEGS) > 0
            keys = collected[:, :width].reshape(1, DOC_SEGS, heads, head_width)
            values = collected[:, width:].reshape(1, DOC_SEGS, heads, head_width)
            valid = key_valid[None, None, :]
            context, log_total = attend_forward(queries, keys, values, valid)
            return (context.reshape(segments, width), (collected, valid, log_total))

        def document_back(delta_context, projected, kept_rows):
            collected, valid, log_total = kept_rows
            queries = projected[:, :width].reshape(1, segments, heads, head_width)
            keys = collected[:, :width].reshape(1, DOC_SEGS, heads, head_width)
            values = collected[:, width:].reshape(1, DOC_SEGS, heads, head_width)
            delta_queries, delta_keys, delta_values = attend_backward(
                delta_context.reshape(1, segments, heads, head_width),
                queries,
                keys,
                values,
                valid,
                log_total,
            )
            delta_pairs = jnp.concatenate(
                (delta_keys.reshape(DOC_SEGS, width), delta_values.reshape(DOC_SEGS, width)), axis=1
            )
            folded = delta_pairs.reshape(DOC_SEGS // segments, segments, 2 * width)
            for bit in reversed(range(levels)):
                halves = folded.reshape(2, folded.shape[0] // 2, segments, 2 * width)
                upper = jnp.right_shift(index, bit) % 2
                keep = jnp.where(upper == 0, halves[0], halves[1])
                send = jnp.where(upper == 0, halves[1], halves[0])
                folded = keep + partner_2(send.astype(jnp.bfloat16), ("seg", "rep"), bit).astype(
                    send.dtype
                )
            own_pairs = folded.reshape(segments, 2 * width)
            return jnp.concatenate(
                (delta_queries.reshape(segments, width), own_pairs), axis=1
            ).astype(jnp.bfloat16)

        inputs = tokens[batch].astype(jnp.float32).reshape(rows_total, width)
        segment_rows, segment_kept = block_forward(inputs, segment_layer, segment_attend)
        segment_rows = segment_rows.reshape(segments, length, width)
        lookup = jnp.sum(picker[:, :, None] * table[None, :, :], axis=1)
        summary_rows = segment_rows[:, 0, :] + lookup
        summary_out, document_kept = block_forward(summary_rows, document_layer, document_attend)
        outputs.append(segment_rows.at[:, 0, :].set(summary_out).astype(jnp.bfloat16))
        incoming = cotangent[batch].astype(jnp.float32)
        delta_summary, document_deltas = block_backward(
            incoming[:, 0, :], document_kept, document_layer, document_back
        )
        delta_table = jnp.transpose(jnp.sum(picker[:, :, None] * delta_summary[:, None, :], axis=0))
        delta_rows = incoming.at[:, 0, :].set(delta_summary).reshape(rows_total, width)
        delta_inputs, segment_deltas = block_backward(
            delta_rows, segment_kept, segment_layer, segment_back
        )
        deltas.append(delta_inputs.reshape(segments, length, width))
        current = segment_deltas + document_deltas + (delta_table,)
        totals = (
            current
            if totals is None
            else tuple((left + right for left, right in zip(totals, current)))
        )
    groups = lax.axis_size("seg")
    shaped = tuple(
        (item.reshape((groups, item.shape[0] // groups) + item.shape[1:]) for item in totals)
    )
    received = (
        lax.all_to_all(
            shaped[0].astype(jnp.bfloat16), "seg", split_axis=0, concat_axis=0, tiled=True
        ).astype(jnp.float32),
        lax.all_to_all(
            shaped[1].astype(jnp.bfloat16), "seg", split_axis=0, concat_axis=0, tiled=True
        ).astype(jnp.float32),
        lax.all_to_all(
            shaped[2].astype(jnp.bfloat16), "seg", split_axis=0, concat_axis=0, tiled=True
        ).astype(jnp.float32),
        lax.all_to_all(
            shaped[3].astype(jnp.bfloat16), "seg", split_axis=0, concat_axis=0, tiled=True
        ).astype(jnp.float32),
        lax.all_to_all(
            shaped[4].astype(jnp.bfloat16), "seg", split_axis=0, concat_axis=0, tiled=True
        ).astype(jnp.float32),
        lax.all_to_all(
            shaped[5].astype(jnp.bfloat16), "seg", split_axis=0, concat_axis=0, tiled=True
        ).astype(jnp.float32),
        lax.all_to_all(
            shaped[6].astype(jnp.bfloat16), "seg", split_axis=0, concat_axis=0, tiled=True
        ).astype(jnp.float32),
        lax.all_to_all(
            shaped[7].astype(jnp.bfloat16), "seg", split_axis=0, concat_axis=0, tiled=True
        ).astype(jnp.float32),
        lax.all_to_all(
            shaped[8].astype(jnp.bfloat16), "seg", split_axis=0, concat_axis=0, tiled=True
        ).astype(jnp.float32),
        lax.all_to_all(
            shaped[9].astype(jnp.bfloat16), "seg", split_axis=0, concat_axis=0, tiled=True
        ).astype(jnp.float32),
        lax.all_to_all(
            shaped[10].astype(jnp.bfloat16), "seg", split_axis=0, concat_axis=0, tiled=True
        ).astype(jnp.float32),
        lax.all_to_all(
            shaped[11].astype(jnp.bfloat16), "seg", split_axis=0, concat_axis=0, tiled=True
        ).astype(jnp.float32),
        lax.all_to_all(
            shaped[12].astype(jnp.bfloat16), "seg", split_axis=0, concat_axis=0, tiled=True
        ).astype(jnp.float32),
        lax.all_to_all(
            shaped[13].astype(jnp.bfloat16), "seg", split_axis=0, concat_axis=0, tiled=True
        ).astype(jnp.float32),
        lax.all_to_all(
            shaped[14].astype(jnp.bfloat16), "seg", split_axis=0, concat_axis=0, tiled=True
        ).astype(jnp.float32),
        lax.all_to_all(
            shaped[15].astype(jnp.bfloat16), "seg", split_axis=0, concat_axis=0, tiled=True
        ).astype(jnp.float32),
        lax.all_to_all(
            shaped[16].astype(jnp.bfloat16), "seg", split_axis=0, concat_axis=0, tiled=True
        ).astype(jnp.float32),
    )
    summed = tuple((jnp.sum(item, axis=0) for item in received))
    reduced = (
        lax.psum_scatter(
            summed[0].astype(jnp.bfloat16), "rep", scatter_dimension=0, tiled=True
        ).astype(jnp.float32),
        lax.psum_scatter(
            summed[1].astype(jnp.bfloat16), "rep", scatter_dimension=0, tiled=True
        ).astype(jnp.float32),
        lax.psum_scatter(
            summed[2].astype(jnp.bfloat16), "rep", scatter_dimension=0, tiled=True
        ).astype(jnp.float32),
        lax.psum_scatter(
            summed[3].astype(jnp.bfloat16), "rep", scatter_dimension=0, tiled=True
        ).astype(jnp.float32),
        lax.psum_scatter(
            summed[4].astype(jnp.bfloat16), "rep", scatter_dimension=0, tiled=True
        ).astype(jnp.float32),
        lax.psum_scatter(
            summed[5].astype(jnp.bfloat16), "rep", scatter_dimension=0, tiled=True
        ).astype(jnp.float32),
        lax.psum_scatter(
            summed[6].astype(jnp.bfloat16), "rep", scatter_dimension=0, tiled=True
        ).astype(jnp.float32),
        lax.psum_scatter(
            summed[7].astype(jnp.bfloat16), "rep", scatter_dimension=0, tiled=True
        ).astype(jnp.float32),
        lax.psum_scatter(
            summed[8].astype(jnp.bfloat16), "rep", scatter_dimension=0, tiled=True
        ).astype(jnp.float32),
        lax.psum_scatter(
            summed[9].astype(jnp.bfloat16), "rep", scatter_dimension=0, tiled=True
        ).astype(jnp.float32),
        lax.psum_scatter(
            summed[10].astype(jnp.bfloat16), "rep", scatter_dimension=0, tiled=True
        ).astype(jnp.float32),
        lax.psum_scatter(
            summed[11].astype(jnp.bfloat16), "rep", scatter_dimension=0, tiled=True
        ).astype(jnp.float32),
        lax.psum_scatter(
            summed[12].astype(jnp.bfloat16), "rep", scatter_dimension=0, tiled=True
        ).astype(jnp.float32),
        lax.psum_scatter(
            summed[13].astype(jnp.bfloat16), "rep", scatter_dimension=0, tiled=True
        ).astype(jnp.float32),
        lax.psum_scatter(
            summed[14].astype(jnp.bfloat16), "rep", scatter_dimension=0, tiled=True
        ).astype(jnp.float32),
        lax.psum_scatter(
            summed[15].astype(jnp.bfloat16), "rep", scatter_dimension=0, tiled=True
        ).astype(jnp.float32),
        lax.psum_scatter(
            summed[16].astype(jnp.bfloat16), "rep", scatter_dimension=0, tiled=True
        ).astype(jnp.float32),
    )
    return (jnp.stack(outputs), jnp.stack(deltas)) + tuple(reduced)


def solution(mesh):
    sizes = dict(mesh.shape)
    body = local_fast if (sizes["seg"], sizes["rep"]) == (16, 2) else local
    return jax.shard_map(
        body,
        mesh=mesh,
        in_specs=(
            P(None, ("seg", "rep"), None, None),
            P(),
            P(("seg", "rep"), None),
            P(("seg", "rep"), None),
            P(("seg", "rep"), None),
            P(("seg", "rep"), None),
            P(("seg", "rep")),
            P(("seg", "rep")),
            P(("seg", "rep")),
            P(("seg", "rep")),
            P(("seg", "rep"), None),
            P(("seg", "rep"), None),
            P(("seg", "rep"), None),
            P(("seg", "rep"), None),
            P(("seg", "rep")),
            P(("seg", "rep")),
            P(("seg", "rep")),
            P(("seg", "rep")),
            P(("seg", "rep"), None),
            P(None, ("seg", "rep"), None, None),
        ),
        out_specs=(
            P(None, ("seg", "rep"), None, None),
            P(None, ("seg", "rep"), None, None),
            P(("seg", "rep"), None),
            P(("seg", "rep"), None),
            P(("seg", "rep"), None),
            P(("seg", "rep"), None),
            P(("seg", "rep")),
            P(("seg", "rep")),
            P(("seg", "rep")),
            P(("seg", "rep")),
            P(("seg", "rep"), None),
            P(("seg", "rep"), None),
            P(("seg", "rep"), None),
            P(("seg", "rep"), None),
            P(("seg", "rep")),
            P(("seg", "rep")),
            P(("seg", "rep")),
            P(("seg", "rep")),
            P(("seg", "rep"), None),
        ),
        check_vma=False,
    )
```

```python
import math
import jax
import jax.numpy as jnp
from jax import lax
from jax.experimental import pallas as pl
from jax.experimental.pallas import tpu as pltpu
from jax.sharding import PartitionSpec as P

MESH = pl.DeviceIdType.MESH
F32 = jnp.float32
BF = jnp.bfloat16
HEADS = 12
DOC_SEGS = 32
epsilon = 1e-05
floor_score = -1e30
root_half = 1.0 / math.sqrt(2.0)
inverse_root_tau = 1.0 / math.sqrt(2.0 * math.pi)


class Spot:
    def __init__(self):
        s, c = lax.axis_index("seg"), lax.axis_index("rep")
        z, y, x = lax.div(s, 4), lax.rem(lax.div(s, 2), 2), lax.rem(s, 2)
        self.s, self.c, self.z = s, c, z
        self.o = 1 - c
        y1, x1 = y + c * (1 - 2 * y), x + (1 - c) * (1 - 2 * x)
        y2, x2 = y + (1 - c) * (1 - 2 * y), x + c * (1 - 2 * x)
        self.q = 2 * y + x
        self.q1 = 2 * y1 + x1
        self.q2 = 2 * y2 + x2
        self.q12 = 3 - self.q
        self.sib = (s, 1 - c)
        self.n1 = (4 * z + self.q1, c)
        self.n2 = (4 * z + self.q2, c)
        self.diagonal = (4 * z + self.q12, c)
        self.zz = [lax.rem(z + k, 4) for k in (1, 2, 3)]
        odd, high = lax.rem(z, 2), lax.div(z, 2)
        self.middle = (z == 1) | (z == 2)
        self.end = (z == 0) | (z == 3)
        self.zs = [
            (4 * (1 + odd) + self.q, c),
            (4 * ((1 - odd) * (2 + high) + odd * high) + self.q, c),
        ]
        self.pass_from = jnp.where(z == 1, 2, 0)
        self.tip = (4 * jnp.where(z == 2, 3, 0) + self.q, c)
        self.zn = [(4 * zz + self.q, c) for zz in self.zz]
        self.qq = [lax.rem(self.q + k, 4) for k in (0, 1, 2, 3)]
        self.plane = [(4 * z + qq, c) for qq in self.qq]
        self.half = lax.rem(z, 2)
        self.zo = z + 1 - 2 * self.half
        self.i = 8 * self.half + 2 * self.q + c
        self.dev = 2 * s + c


def remote(src, dst, ssem, rsem, dev):
    return pltpu.make_async_remote_copy(
        src_ref=src, dst_ref=dst, send_sem=ssem, recv_sem=rsem, device_id=dev, device_id_type=MESH
    )


def enter(t):
    bar = pltpu.get_barrier_semaphore()
    everyone = [t.sib, t.n1, t.n2, t.diagonal] + t.zn
    for dev in everyone:
        pl.semaphore_signal(bar, inc=1, device_id=dev, device_id_type=MESH)
    pl.semaphore_wait(bar, len(everyone))


def pass_on(t, sem):
    for dev in (t.sib, t.n1, t.n2, t.diagonal):
        pl.semaphore_signal(sem, inc=1, device_id=dev, device_id_type=MESH)


class Sender:
    def __init__(self, t, ss, rs):
        self.t, self.ss, self.rs, self.pending = t, ss, rs, []

    def send(self, at, src, dst, dev):
        d = remote(src, dst, self.ss, self.rs.at[at], dev)
        d.start()
        self.pending.append(d)

    def arrived(self, at, ref):
        remote(ref, ref, self.ss, self.rs.at[at], self.t.sib).wait_recv()

    def drain(self):
        for d in self.pending:
            if isinstance(d, tuple):
                pl.when(d[0])(d[1].wait_send)
            else:
                d.wait_send()
        self.pending = []

    def z_spread(self, at, view):
        t = self.t
        for dev in t.zs:
            self.send(at, view(t.z), view(t.z), dev)

    def z_relay(self, at, at2, view):
        t = self.t
        two = view(pl.ds(t.pass_from, 2))
        d = remote(two, two, self.ss, self.rs.at[at2], t.tip)

        @pl.when(t.middle)
        def _():
            self.arrived(at, view(pl.ds(0, 3)))
            d.start()

        self.pending.append((t.middle, d))

    def z_last(self, at, at2, view):
        @pl.when(self.t.end)
        def _():
            self.arrived(at, view(0))
            self.arrived(at2, view(pl.ds(0, 2)))


def off(at, size, step=128):
    return pl.ds(pl.multiple_of(at * size, step), size)


def join_pair(t, shard, got, tmp, dest):
    rd, n2 = got.shape
    wide = tmp.shape[1]
    for j in range(0, n2, wide):
        mine = pl.ds(pl.multiple_of(t.c * n2 + j, 128), wide)
        tmp[off(t.c, rd, 8), :] = shard[:, mine].astype(F32)
        tmp[off(t.o, rd, 8), :] = got[:, j : j + wide].astype(F32)
        dest[:, pl.ds(j, wide)] = tmp[...].astype(dest.dtype)


class Gather(Sender):
    def __init__(self, t, far, shard, w, got, tmp, windows, ss, rs):
        super().__init__(t, ss, rs)
        self.far, self.shard, self.w, self.got, self.tmp, self.windows = far, shard, w, got, tmp, windows

    def pair(self):
        n2 = self.got.shape[1]
        self.send(5 * len(self.windows), self.far.at[:, off(self.t.o, n2)], self.got, self.t.sib)

    def join(self):
        t = self.t
        self.arrived(5 * len(self.windows), self.got)
        join_pair(t, self.shard, self.got, self.tmp, self.w.at[t.c, t.z, t.q])

    def pick(self, k, *lead):
        rows, cols = self.windows[k]
        return self.w.at[(self.t.c,) + lead + (pl.ds(*rows), pl.ds(*cols))]

    def line(self, k, q):
        return self.pick(k, slice(None), q)

    def view(self, k):
        return lambda at: self.pick(k, at, self.t.q)

    def spread(self, k):
        self.z_spread(5 * k, self.view(k))

    def relay(self, k):
        self.z_relay(5 * k, 5 * k + 1, self.view(k))

    def first(self, k):
        t = self.t
        self.z_last(5 * k, 5 * k + 1, self.view(k))
        line = self.line(k, t.q)
        self.send(5 * k + 2, line, line, t.n1)
        self.send(5 * k + 4, line, line, t.sib)

    def second(self, k):
        t = self.t
        line, other = self.line(k, t.q), self.line(k, t.q1)
        self.arrived(5 * k + 2, other)
        self.send(5 * k + 3, line, line, t.n2)
        self.send(5 * k + 3, other, other, t.n2)
        self.send(5 * k + 4, other, other, t.sib)

    def third(self, k):
        t = self.t
        self.arrived(5 * k + 3, self.pick(k, slice(None), pl.ds(0, 2)))
        for q in (t.q2, t.q12):
            self.send(5 * k + 4, self.line(k, q), self.line(k, q), t.sib)

    def finish(self, k):
        self.arrived(5 * k + 4, self.pick(k, slice(None), slice(None)))


class LineGather(Sender):
    def __init__(self, t, w, windows, ss, rs):
        super().__init__(t, ss, rs)
        self.w, self.windows = w, windows

    def view(self, k):
        cols = self.windows[k]
        return lambda at: self.w.at[self.t.c, at, :, pl.ds(*cols)]

    def spread(self, k):
        self.z_spread(3 * k, self.view(k))

    def relay(self, k):
        self.z_relay(3 * k, 3 * k + 1, self.view(k))

    def first(self, k):
        self.z_last(3 * k, 3 * k + 1, self.view(k))
        line = self.view(k)(slice(None))
        self.send(3 * k + 2, line, line, self.t.sib)

    def finish(self, k):
        self.arrived(3 * k + 2, self.view(k)(slice(None)))


class DocGather(Sender):
    def __init__(self, t, far, shards, stages, gots, tmps, dpu, do, dd, ss, rs, ls):
        super().__init__(t, ss, rs)
        self.far, self.shards, self.stages, self.gots, self.tmps = far, shards, stages, gots, tmps
        self.dpu, self.do, self.dd, self.ls = dpu, do, dd, ls
        main, down = stages
        self.views = [(lambda at, k=k: dpu.at[t.c, at, k]) for k in range(4)]
        self.views.append(lambda at: main.at[at, :, pl.ds(3072, 384)])
        self.views += [(lambda at, j=j: down.at[at, pl.ds(96 * j, 96)]) for j in range(2)]

    def pair(self):
        dp, do, du, dd = self.far
        for i, ref in enumerate((dp, do, du)):
            self.send(i, ref, self.gots[i], self.t.sib)
        self.send(3, dd.at[:, off(self.t.o, 384)], self.gots[3], self.t.sib)

    def join(self):
        t = self.t
        dp, do, du, dd = self.shards
        for i in range(4):
            self.arrived(i, self.gots[i])
        main, down = self.stages
        tmp = self.tmps[0]
        mine, other = off(t.c, 24, 8), off(t.o, 24, 8)

        def place(ref, got, a, n, b):
            tmp[mine, 0:n] = ref[:, a : a + n].astype(F32)
            tmp[other, 0:n] = got[:, a : a + n].astype(F32)
            wide = -(-n // 128) * 128
            main[t.z, :, b : b + wide] = tmp[:, 0:wide].astype(BF)

        @pl.when(t.c == 0)
        def _():
            tmp[...] = jnp.zeros(tmp.shape, F32)
            for r in range(4):
                for g in range(3):
                    place(dp, self.gots[0], 768 * g + 192 * r, 192, 768 * r + 256 * g)
            place(do, self.gots[1], 0, 384, 3072)

        @pl.when(t.c == 1)
        def _():
            for r in range(4):
                place(du, self.gots[2], 768 * r, 768, 768 * r)
            place(do, self.gots[1], 384, 384, 3072)

        join_pair(t, dd, self.gots[3], self.tmps[1], down.at[t.z])

    def ranks(self):
        t = self.t
        main = self.stages[0]
        for k in (1, 2, 3):
            self.send(18, main.at[t.z, :, off(t.qq[k], 768)], self.dpu.at[t.c, t.z, t.q], t.plane[k])
        d = pltpu.make_async_copy(main.at[t.z, :, off(t.q, 768)], self.dpu.at[t.c, t.z, t.q], self.ls.at[0])
        d.start()
        self.local = [d]

    def spread(self, k):
        t = self.t
        if k == 0:
            self.arrived(18, self.dpu.at[t.c, t.z, pl.ds(0, 3)])
            self.local.pop().wait()
        self.z_spread(4 + k, self.views[k])

    def relay(self, k):
        self.z_relay(4 + k, 11 + k, self.views[k])

    def plane(self, w):
        t = self.t
        main, down = self.stages
        self.z_last(4 + w, 11 + w, self.views[w])
        if w < 4:
            return
        for k in (1, 2, 3, 0):
            q = t.qq[k]
            if w == 4:
                src, at = main.at[q, :, pl.ds(3072, 384)], 19
                dst = self.do.at[t.c, pl.ds(pl.multiple_of(48 * t.q, 16), 48)]
            else:
                rows = pl.ds(96 * (w - 5), 96)
                src, dst, at = down.at[q, rows], self.dd.at[t.c, t.q, rows], 15 + w
            if k:
                self.send(at, src, dst, t.plane[k])
            else:
                d = pltpu.make_async_copy(src, dst, self.ls.at[at - 18])
                d.start()
                self.local.append(d)

    def share(self):
        t = self.t
        self.arrived(19, self.do.at[t.c, pl.ds(0, 144)])
        for j in range(2):
            self.arrived(20 + j, self.dd.at[t.c, pl.ds(0, 3), pl.ds(0, 96)])
        for d in self.local:
            d.wait()
        for i, ref in enumerate((self.dpu, self.do, self.dd)):
            view = ref.at[t.c, pl.ds(0, 192)] if i == 1 else ref.at[t.c]
            self.send(22 + i, view, view, t.sib)

    def finish(self, i):
        ref = (self.dpu, self.do, self.dd)[i]
        view = ref.at[self.t.o, pl.ds(0, 192)] if i == 1 else ref.at[self.t.o]
        self.arrived(22 + i, view)


class Reduce(Sender):
    def __init__(self, t, w, rc_, r1, r2, r3, fin, fin2, out, windows, ss, rs):
        super().__init__(t, ss, rs)
        self.w, self.rc, self.r1, self.r2, self.r3 = w, rc_, r1, r2, r3
        self.fin, self.fin2, self.out, self.windows = fin, fin2, out, windows
        self.by_rows = fin2.shape[0] == 96

    def cut(self, ref, k, *lead):
        rows, cols = self.windows[k]
        lead += (slice(None),) * (len(ref.shape) - 2 - len(lead))
        return ref.at[lead + (pl.ds(*rows), pl.ds(*cols))]

    def pair(self, k):
        self.send(5 * k, self.cut(self.w, k, self.t.o), self.cut(self.rc, k), self.t.sib)

    def pair_rows(self, z):
        self.send(5 * z, self.w.at[self.t.o, z], self.rc.at[z], self.t.sib)

    def add(self, k, q, part):
        (r, rn), (a, an) = self.windows[k]
        w, c = self.w, self.t.c

        @pl.loop(0, 4)
        def _(z):
            at = (c, z, q, pl.ds(r, rn), pl.ds(a, an))
            w[at] = (w[at].astype(F32) + part[z, r : r + rn, a : a + an].astype(F32)).astype(w.dtype)

    def first(self, k):
        t = self.t
        if self.by_rows:
            for z in range(4 if k == 0 else 0):
                self.arrived(5 * z, self.rc.at[z])
        else:
            self.arrived(5 * k, self.cut(self.rc, k))
        for i, q in ((0, t.q2), (1, t.q12)):
            self.add(k, q, self.rc.at[:, q])
            self.send(
                5 * k + 1 + i, self.cut(self.w, k, t.c, slice(None), q), self.cut(self.r1, k, i, slice(None)), t.n2
            )
        for q in (t.q, t.q1):
            self.add(k, q, self.rc.at[:, q])

    def second(self, k):
        t = self.t
        self.arrived(5 * k + 2, self.cut(self.r1, k, 1, slice(None)))
        self.add(k, t.q1, self.r1.at[1])
        self.send(5 * k + 3, self.cut(self.w, k, t.c, slice(None), t.q1), self.cut(self.r2, k, slice(None)), t.n1)
        self.arrived(5 * k + 1, self.cut(self.r1, k, 0, slice(None)))
        self.add(k, t.q, self.r1.at[0])

    def third(self, k):
        t = self.t
        self.arrived(5 * k + 3, self.cut(self.r2, k, slice(None)))
        self.add(k, t.q, self.r2)
        for i in range(3):
            self.send(5 * k + 4, self.cut(self.w, k, t.c, t.zz[i], t.q), self.cut(self.r3, k, 2 - i), t.zn[i])

    def fourth(self, k):
        t = self.t
        (r, rn), (a, an) = self.windows[k]
        self.arrived(5 * k + 4, self.cut(self.r3, k, slice(None)))
        total = self.w[t.c, t.z, t.q, r : r + rn, a : a + an].astype(F32)
        for i in range(3):
            total = total + self.r3[i, r : r + rn, a : a + an].astype(F32)
        self.fin[r : r + rn, a : a + an] = total
        if k == len(self.windows) - 1:
            rd = self.fin.shape[0] // 2
            self.send(5 * len(self.windows), self.fin.at[off(t.o, rd, 8)], self.fin2, t.sib)

    def fifth(self):
        t = self.t
        rd, n2 = self.fin2.shape
        self.arrived(5 * len(self.windows), self.fin2)
        self.out[:, off(t.c, n2)] = self.fin[off(t.c, rd, 8), :]
        self.out[:, off(t.o, n2)] = self.fin2[...]


def dot(a, b):
    return jnp.dot(a, b, preferred_element_type=F32)


def dot_rt(a, b):
    return lax.dot_general(a, b, (((1,), (1,)), ((), ())), preferred_element_type=F32)


def dot_lt(a, b):
    return lax.dot_general(a, b, (((0,), (0,)), ((), ())), preferred_element_type=F32)


def normed(v):
    centred = v - jnp.mean(v, axis=-1, keepdims=True)
    inverse = lax.rsqrt(jnp.mean(centred * centred, axis=-1, keepdims=True) + epsilon)
    return centred * inverse, inverse


def norm_back(g, n, inverse, gain):
    v = g * gain
    return inverse * (
        v - jnp.mean(v, axis=-1, keepdims=True) - n * jnp.mean(v * n, axis=-1, keepdims=True)
    )


def gelu_pair(v):
    share = 0.5 * (1.0 + lax.erf(v * root_half))
    return v * share, share + v * jnp.exp(-0.5 * v * v) * inverse_root_tau


SIZES = ((24, 128, F32), (24, 1152, BF), (24, 384, BF), (24, 1536, BF), (96, 384, BF))
WINDOWS = (
    [((0, 48), (0, 128))],
    [((0, 48), (384 * j, 384)) for j in range(3)],
    [((0, 48), (0, 384))],
    [((0, 48), (384 * j, 384)) for j in range(4)],
    [((48 * j, 48), (0, 384)) for j in range(4)],
)
SCRATCH = {
    "got": [((rd, n2), dt) for rd, n2, dt in SIZES]
    + [((24, 2304), BF), ((24, 768), BF), ((24, 3072), BF), ((96, 384), BF)],
    "w": [((2, 4, 4, 2 * rd, n2), dt) for rd, n2, dt in SIZES],
    "fin": [((2 * rd, n2), F32) for rd, n2, dt in SIZES],
    "fin2": [((rd, n2), F32) for rd, n2, dt in SIZES],
    "rc": [((4, 4, 2 * rd, n2), dt) for rd, n2, dt in SIZES if n2 not in (1152, 384) or rd == 96],
    "r1": [((2, 4, 2 * rd, n2), dt) for rd, n2, dt in SIZES],
    "r2": [((4, 2 * rd, n2), dt) for rd, n2, dt in SIZES],
    "r3": [((3, 2 * rd, n2), dt) for rd, n2, dt in SIZES],
    "stage": [((4, 48, 3456), BF), ((4, 192, 384), BF)],
    "dpu": [((2, 4, 4, 48, 768), BF)],
    "do": [((2, 256, 384), BF)],
    "dd": [((2, 4, 192, 384), BF)],
    "tmask": [((4, 128), F32)],
    "dmask": [((1, 32), F32)],
    "vec": [((16, 768), F32)],
    "table": [((16, 2, 768), F32)],
    "pr": [((512, 2304), BF)],
    "ctx": [((512, 768), BF)],
    "sh": [((24, 256, 128), BF)],
    "n1": [((512, 768), BF)],
    "i1": [((512, 1), F32)],
    "n2": [((512, 768), BF)],
    "i2": [((512, 1), F32)],
    "fl": [((512, 768), BF)],
    "act": [((512, 3072), BF)],
    "gp": [((512, 3072), BF)],
    "row": [((512, 768), F32)],
    "low": [((512, 768), BF)],
    "ob": [((512, 768), BF)],
    "hid": [((256, 384), F32)],
    "src": [((2, 2, 768), F32)] * 2,
    "slots": [((16, 2, 768), F32)] * 4,
    "sdr": [((2, 4, 2, 768), F32)],
    "pairs": [((2, 2, 768), F32)] * 2,
    "soo": [((2, 768), F32)],
    "mat": [((32, 768), F32)] * 2,
    "ars": [((3, 32, 768), BF)],
    "gpc": [((64, 3072), BF)],
    "lowc": [((64, 768), BF)],
    "arb": [((3, 3, 32, 768), BF)],
    "fq": [((2, 4, 4, 32, 1280), BF)],
    "fz": [((2, 4, 32, 1536), BF)],
    "vg": [((128, 768), F32)],
    "flip": [((768, 128), F32)],
}
SEMS = {
    "gr0": (6,),
    "gr1": (16,),
    "gr2": (6,),
    "gr3": (21,),
    "gr4": (21,),
    "dr": (25,),
    "ls": (4,),
    "rr0": (6,),
    "rr1": (16,),
    "rr2": (6,),
    "rr3": (21,),
    "rr4": (21,),
    "xr": (9,),
    "fr": (15,),
    "er": (9,),
    "ss": (14,),
    "os": (11,),
    "ins": (12,),
}
INS = ("tok", "cot", "counts", "small", "sp", "so", "su", "sd", "dp", "dout", "du", "ddown")
OUTS = (
    ("out", (512, 768), BF),
    ("gin", (512, 768), F32),
    ("gsmall", (24, 256), F32),
    ("gsp", (24, 2304), F32),
    ("gso", (24, 768), F32),
    ("gsu", (24, 3072), F32),
    ("gsd", (96, 768), F32),
    ("gdp", (24, 2304), F32),
    ("gdo", (24, 768), F32),
    ("gdu", (24, 3072), F32),
    ("gdd", (96, 768), F32),
)


class Box:
    def put(self, name, ref):
        at = [out[0] for out in OUTS].index(name)
        d = pltpu.make_async_copy(ref, self.back[name], self.os.at[at])
        d.start()
        self.flying[name] = d

    def ready(self, *names):
        for name in names:
            self.coming[name].wait()


def kernel(*refs):
    b = Box()
    refs = list(refs)

    def take(n):
        got, refs[:n] = refs[:n], []
        return got

    b.far = {name: take(1)[0] for name in INS}
    b.back = {name: take(1)[0] for name, _, _ in OUTS}
    for name in INS:
        setattr(b, name, take(1)[0])
    for name, _, _ in OUTS[2:]:
        setattr(b, name, take(1)[0])
    for name, items in SCRATCH.items():
        got = take(len(items))
        setattr(b, name, got if len(got) > 1 else got[0])
    for name in SEMS:
        setattr(b, name, take(1)[0])
    b.credit, b.met, b.met2 = take(3)
    b.t = Spot()
    run(b)


FACTOR_WINDOWS = [((0, 32), (0, 512)), ((0, 32), (512, 384)), ((0, 32), (896, 384))]
LINE_WINDOWS = [(0, 768), (768, 384), (1152, 384)]


def run(b):
    t = b.t
    b.x = Sender(t, b.ss.at[0], b.xr)
    b.flying, b.coming = {}, {}
    for i, name in enumerate(INS):
        d = pltpu.make_async_copy(b.far[name], getattr(b, name), b.ins.at[i])
        d.start()
        b.coming[name] = d
    b.do[...] = jnp.zeros(b.do.shape, BF)
    b.vg[...] = jnp.zeros(b.vg.shape, F32)
    enter(t)
    pass_on(t, b.met)
    shards = (b.small, b.sp, b.so, b.su, b.sd)
    far = [b.far[name] for name in ("small", "sp", "so", "su", "sd")]
    gs = [
        Gather(t, far[i], shards[i], b.w[i], b.got[i], b.fin[i], WINDOWS[i], b.ss.at[1 + i], getattr(b, f"gr{i}"))
        for i in range(5)
    ]
    dg = DocGather(
        t,
        [b.far[name] for name in ("dp", "dout", "du", "ddown")],
        (b.dp, b.dout, b.du, b.ddown),
        b.stage,
        b.got[5:],
        (b.fin[1], b.fin[4]),
        b.dpu,
        b.do,
        b.dd,
        b.ss.at[6],
        b.dr,
        b.ls,
    )
    for g in gs:
        g.pair()
    dg.pair()
    b.f = Gather(t, None, None, b.fq, None, None, FACTOR_WINDOWS, b.ss.at[7], b.fr)
    b.e = LineGather(t, b.fz, LINE_WINDOWS, b.ss.at[8], b.er)

    events = [(g, k) for g in gs for k in range(len(g.windows))]
    lines = events + [(dg, k) for k in range(7)]
    clock, spreads, relays = [0], [0], [0]

    def do(name, at, among=events):
        if 0 <= at < len(among):
            getattr(among[at][0], name)(among[at][1])

    def relay(n):
        for _ in range(n):
            do("relay", relays[0], lines)
            relays[0] += 1
            do("spread", spreads[0], lines)
            spreads[0] += 1

    def tick(upto):
        while clock[0] <= upto:
            at = clock[0]
            busy = relays[0] < len(events)
            do("first", at)
            relay(1)
            do("second", at - 2)
            if busy:
                relay(1)
            do("third", at - 4)
            do("finish", at - 5)
            clock[0] += 1

    b.ready("small", "sp")
    gs[0].join()
    gs[1].join()
    for i in range(3):
        do("spread", i, lines)
    spreads[0] = 3
    b.ready("so", "su", "sd")
    for g in gs[2:]:
        g.join()
    pl.semaphore_wait(b.met, 4)
    pass_on(t, b.met2)
    relay(1)
    tick(0)
    b.ready("dp", "dout", "du", "ddown")
    dg.join()
    dg.ranks()
    tick(1)
    pl.semaphore_wait(b.met2, 4)
    b.ready("cot", "tok", "counts")
    masks_in(b)
    send_cotangents(b)
    tick(5)
    vectors_in(b)
    tick(8)
    segment_project(b)
    tick(9)
    for seg in range(4):
        attend(b, seg)
        tick(10 + seg // 2)
    segment_mix(b)
    for j in range(4):
        segment_up(b, j)
        if j < 3:
            tick(12 + j)
    for k in range(7):
        dg.plane(k)
    tick(17)
    send_summaries(b, summary_rows(b))
    steps = document(b)
    segment_down(b)
    dg.share()
    for g in gs:
        g.drain()
    for i in range(3):
        dg.finish(i)
    dg.drain()
    next(steps)
    second_back(b)
    next(steps)
    hidden_back(b)
    next(steps)
    first_back(b)
    next(steps)
    next(steps)
    next(steps, None)
    finish_output(b)
    b.f.spread(2)
    b.e.spread(2)

    small_rc, up_rc, down_rc = b.rc
    rcs = (small_rc, up_rc.at[:, :, :, 0:1152], up_rc.at[:, :, :, 1152:1536], up_rc, down_rc)
    rs = [
        Reduce(
            t,
            b.w[i],
            rcs[i],
            b.r1[i],
            b.r2[i],
            b.r3[i],
            b.fin[i],
            b.fin2[i],
            out,
            WINDOWS[i],
            b.ss.at[9 + i],
            getattr(b, f"rr{i}"),
        )
        for i, out in enumerate((b.gsmall, b.gsp, b.gso, b.gsu, b.gsd))
    ]
    for r, name in zip(rs, ("gsmall", "gsp", "gso", "gsu", "gsd")):
        r.name = name
    rsmall, rproject, routput, rup, rdown = rs
    terms = [(r, k) for r in (rdown, rup, routput, rproject, rsmall) for k in range(len(r.windows))]
    clock[0] = 0

    ends = {id(r): max(i for i, e in enumerate(terms) if e[0] is r) for r in rs}

    def tock(upto):
        while clock[0] <= upto:
            at = clock[0]
            do("first", at, terms)
            do("second", at - 2, terms)
            do("third", at - 4, terms)
            do("fourth", at - 6, terms)
            for r in rs:
                if ends[id(r)] == at - 7:
                    r.fifth()
                    b.put(r.name, r.out)
            clock[0] += 1

    second_back_rows(b)
    hidden_back_rows(b)
    b.f.relay(2)
    b.e.relay(2)
    b.f.second(1)
    b.f.third(0)
    down_terms(b, rdown)
    first_back_rows(b)
    b.f.first(2)
    b.e.first(2)
    b.f.third(1)
    tock(0)
    column_terms(b, rup, b.fl, b.gp)
    tock(1)
    b.f.second(2)
    mixed_back(b)
    tock(2)
    context_back(b)
    tock(3)
    b.f.third(2)
    attend_back(b, 0)
    tock(4)
    attend_back(b, 1)
    tock(5)
    attend_back(b, 2)
    tock(6)
    attend_back(b, 3)
    tock(7)
    pl.semaphore_signal(b.credit, inc=1, device_id=t.sib, device_id_type=MESH)
    pl.semaphore_wait(b.credit, 1)
    column_terms(b, routput, b.ctx, b.low)
    input_back(b)
    column_terms(b, rproject, b.tok, b.pr)
    tock(8)
    vectors_out(b)
    rsmall.pair(0)
    tock(10)
    document_terms(b)
    tock(len(terms) + 6)
    for r in rs:
        r.drain()
    b.x.drain()
    for d in b.flying.values():
        d.wait()


def send_cotangents(b):
    for m in range(2):
        for s in range(2):
            rows = b.cot[pl.ds(128 * (2 * m + s), 16), :].astype(F32)
            b.src[0][m, s : s + 1, :] = rows[0:1]
    send_rows(b, 0)


def send_rows(b, n):
    t, src, slots = b.t, b.src[n], b.slots[n]
    mine = src.at[t.half]
    other = src.at[1 - t.half]
    for k in (1, 2, 3):
        b.x.send(n, mine, slots.at[t.i], t.plane[k])
    for k in (0, 1, 2, 3):
        b.x.send(n, mine, slots.at[t.i], (4 * t.z + t.qq[k], t.o))
        b.x.send(n, other, slots.at[t.i], (4 * t.zo + t.qq[k], t.c))
        b.x.send(n, other, slots.at[t.i], (4 * t.zo + t.qq[k], t.o))
    slots[t.i] = src[t.half]


def take_rows(b, n):
    slots = b.slots[n]
    b.x.arrived(n, slots.at[pl.ds(0, 15)])
    for i in range(16):
        b.mat[n][2 * i : 2 * i + 2, :] = slots[i]
    return b.mat[n][...]


def vectors_in(b):
    small = b.w[0]
    b.vec[...] = jnp.transpose(small[0].reshape(768, 128))[0:16]
    table = jnp.transpose(small[1].reshape(768, 128))[0:32]
    for i in range(16):
        b.table[i] = table[2 * i : 2 * i + 2]


def masks_in(b):
    t = b.t
    rows = [b.counts[m : m + 1, :].astype(F32) for m in range(2)]
    lane = lax.broadcasted_iota(jnp.int32, (1, 64), 1)
    slot = lax.broadcasted_iota(jnp.int32, (1, 128), 1)
    for m in range(2):
        for s in range(2):
            own = jnp.sum(jnp.where(lane == 2 * t.dev + s, rows[m], 0.0), axis=1, keepdims=True)
            keep = (slot.astype(F32) < own) | (slot == 0)
            b.tmask[2 * m + s : 2 * m + s + 1, :] = jnp.where(keep, 1.0, 0.0)
    row = jnp.where(t.half == 0, rows[0], rows[1])
    row = jnp.where(lax.div(t.z, 2) == 0, row[:, 0:32], row[:, 32:64])
    b.dmask[...] = jnp.where(row > 0.0, 1.0, 0.0)


def vec(b, i):
    return b.vec[i : i + 1, :]


def segment_project(b):
    w = b.w[1]

    @pl.loop(0, 6)
    def _(i):
        h, j = lax.div(i, 3), lax.rem(i, 3)
        part = w[h, :, :, :, off(j, 384)].reshape(768, 384)
        b.pr[:, off(i, 384)] = dot(b.tok[...], part).astype(BF)


def lane_masks():
    lane = lax.broadcasted_iota(jnp.int32, (1, 128), 1)
    low = (lane < 64).astype(F32)
    return low.astype(BF), (1.0 - low).astype(BF)


def attend(b, seg):
    low, high = lane_masks()
    keep = b.tmask[seg : seg + 1, :] > 0.0
    rows = pl.ds(128 * seg, 128)

    lane = lax.broadcasted_iota(jnp.int32, (128, 128), 1)

    @pl.loop(0, 3)
    def _(i):
        pairs = (2 * i, 2 * i + 1)
        loaded = [[b.pr[rows, off(p + 6 * g, 128)] for g in range(3)] for p in pairs]
        stacked = [jnp.concatenate((q2 * low, q2 * high), axis=0) for q2, _, _ in loaded]
        scores = [
            jnp.where(keep, dot_rt(qs, k2) * 0.125, floor_score)
            for qs, (_, k2, _) in zip(stacked, loaded)
        ]
        raised = [jnp.exp(v - jnp.max(v, axis=-1, keepdims=True)) for v in scores]
        shares = [(v * (1.0 / jnp.sum(v, axis=-1, keepdims=True))).astype(BF) for v in raised]
        both = [dot(v, v2) for v, (_, _, v2) in zip(shares, loaded)]
        for p, share, two in zip(pairs, shares, both):
            b.sh[6 * seg + p] = share
            b.ctx[rows, off(p, 128)] = jnp.where(lane < 64, two[:128], two[128:]).astype(BF)


def segment_mix(b):
    w = b.w[2]
    for r in range(2):
        rows = pl.ds(256 * r, 256)
        for h in range(2):
            b.row[rows, pl.ds(384 * h, 384)] = dot(b.ctx[rows, :], w[h].reshape(768, 384))
    scale, offset = vec(b, 0), vec(b, 1)

    @pl.loop(0, 16)
    def _(i):
        rows = off(i, 32, 32)
        n, inverse = normed(b.tok[rows, :].astype(F32) + b.row[rows, :])
        first = n * scale + offset
        b.n1[rows, :] = n.astype(BF)
        b.i1[rows, :] = inverse
        b.row[rows, :] = first
        b.fl[rows, :] = first.astype(BF)


def segment_up(b, j):
    w = b.w[3]
    for h, r in ((0, 0), (0, 1), (1, 0), (1, 1)):
        up = w[h, :, :, :, pl.ds(384 * j, 384)].reshape(768, 384)
        b.hid[...] = dot(b.fl[256 * r : 256 * r + 256, :], up)
        cols = pl.ds(1536 * h + 384 * j, 384)

        @pl.loop(0, 8)
        def _(i):
            rows = off(i + 8 * r, 32, 32)
            value, slope = gelu_pair(b.hid[off(i, 32, 32), :])
            b.act[rows, cols] = value.astype(BF)
            b.gp[rows, cols] = slope.astype(BF)


def summary_rows(b):
    w = b.w[4]
    for s in range(4):
        b.gpc[16 * s : 16 * s + 16, :] = b.act[128 * s : 128 * s + 16, :]
    parts = [dot(b.gpc[...], w[h].reshape(3072, 384)) for h in range(2)]
    both = jnp.concatenate(parts, axis=1)
    for s in range(4):
        b.gpc[16 * s : 16 * s + 16, :] = b.gp[128 * s : 128 * s + 16, :]
    rows = []
    for s in range(4):
        n, _ = normed(b.row[128 * s : 128 * s + 8, :] + both[16 * s : 16 * s + 8])
        rows.append((n * vec(b, 2) + vec(b, 3))[0:1])
    return rows


def thirds(w, depth):
    middle = jnp.concatenate((w[0, :, :, :, 256:384], w[1, :, :, :, 0:128]), axis=-1)
    for part in (w[0, :, :, :, 0:256], middle, w[1, :, :, :, 128:384]):
        yield part.reshape(depth, 256)


def side_by_side(a, c, rows):
    return jnp.concatenate((a.reshape(rows, 384), c.reshape(rows, 384)), axis=1)


def segment_down(b):
    for i, part in enumerate(thirds(b.w[4], 3072)):
        cols = slice(256 * i, 256 * i + 256)
        b.row[:, cols] += dot(b.act[...], part)

    gain, shift = vec(b, 2), vec(b, 3)

    @pl.loop(0, 16, unroll=2)
    def _(i):
        rows = off(i, 32, 32)
        n, inverse = normed(b.row[rows, :])
        b.n2[rows, :] = n.astype(BF)
        b.i2[rows, :] = inverse
        b.ob[rows, :] = (n * gain + shift).astype(BF)


def send_summaries(b, rows):
    places = b.table[b.t.i]
    for m in range(2):
        for s in range(2):
            b.src[1][m, s : s + 1, :] = rows[2 * m + s] + places[s : s + 1]
    send_rows(b, 1)


def plane_send(b, n, partial):
    b.ars[n] = partial.astype(BF)
    for k in (1, 2, 3):
        b.x.send(2 + n, b.ars.at[n], b.arb.at[n, k - 1], b.t.plane[k])


def plane_take(b, n):
    b.x.arrived(2 + n, b.arb.at[n])
    total = b.ars[n].astype(F32)
    for k in range(3):
        total = total + b.arb[n, k].astype(F32)
    return total


def document(b):
    t = b.t
    dp = b.dpu[0].reshape(768, 768)
    du = b.dpu[1].reshape(768, 768)
    lane = lax.broadcasted_iota(jnp.int32, (1, 256), 1)
    heads = [((lane >= 64 * h) & (lane < 64 * h + 64)).astype(F32).astype(BF) for h in range(3)]
    keep = b.dmask[...] > 0.0
    h_in = take_rows(b, 1)
    h_low = h_in.astype(BF)
    pr = dot(h_low, dp).astype(BF)
    q3, k3, v3 = pr[:, 0:256], pr[:, 256:512], pr[:, 512:768]
    qs = jnp.concatenate([q3 * m for m in heads], axis=0)
    scores = jnp.where(keep, dot_rt(qs, k3) * 0.125, floor_score)
    raised = jnp.exp(scores - jnp.max(scores, axis=-1, keepdims=True))
    shares = raised * (1.0 / jnp.sum(raised, axis=-1, keepdims=True))
    shares_low = shares.astype(BF)
    three = dot(shares_low, v3)
    ctx = sum(three[32 * h : 32 * h + 32] * heads[h].astype(F32) for h in range(3)).astype(BF)
    mixed = jnp.concatenate([dot(ctx, b.do[h]) for h in range(2)], axis=1)
    plane_send(b, 0, mixed)
    yield
    n1, i1 = normed(h_in + plane_take(b, 0))
    first = n1 * vec(b, 4) + vec(b, 5)
    first_low = first.astype(BF)
    active, slope = gelu_pair(dot(first_low, du))
    active = active.astype(BF)
    branch = jnp.concatenate([dot(active, b.dd[h].reshape(768, 384)) for h in range(2)], axis=1)
    plane_send(b, 1, branch)

    @pl.when(t.c == 0)
    def _():
        b.fq[0, t.z, t.q, :, 0:512] = active[:, 0:512]
        b.fz[0, t.z, :, 0:768] = h_low

    @pl.when(t.c == 1)
    def _():
        b.fq[1, t.z, t.q, :, 0:256] = active[:, 512:768]
        b.fq[1, t.z, t.q, :, 256:512] = ctx
        b.fz[1, t.z, :, 0:768] = first_low

    b.f.spread(0)
    b.e.spread(0)
    yield
    n2, i2 = normed(first + plane_take(b, 1))
    out = n2 * vec(b, 6) + vec(b, 7)
    g = take_rows(b, 0)
    delta = norm_back(g, n2, i2, vec(b, 6))
    branch_low = delta.astype(BF)
    back = sum(dot_rt(branch_low[:, 384 * h : 384 * h + 384], b.dd[h].reshape(768, 384)) for h in range(2))
    hidden_delta = (back * slope).astype(BF)
    plane_send(b, 2, dot_rt(hidden_delta, du))
    b.vg[6:7, :] = jnp.sum(g * n2, axis=0, keepdims=True) * 0.125
    b.vg[7:8, :] = jnp.sum(g, axis=0, keepdims=True) * 0.125
    for i in range(16):
        b.slots[2][i] = out[2 * i : 2 * i + 2]
    other_i = 8 * (1 - t.half) + 2 * t.q + t.c
    b.x.send(6, b.slots[2].at[other_i], b.soo, (4 * t.zo + t.q, t.c))

    def halves(ref, at, value):
        for h in range(2):

            @pl.when(t.c == h)
            def _():
                ref[(h,) + at] = value[:, 384 * h : 384 * h + 384]

    halves(b.fq, (t.z, t.q, slice(None), slice(512, 896)), hidden_delta)
    halves(b.fz, (t.z, slice(None), slice(768, 1152)), branch_low)
    b.f.relay(0)
    b.e.relay(0)
    b.f.spread(1)
    b.e.spread(1)
    yield
    first_delta = delta + plane_take(b, 2)
    mixed_delta = norm_back(first_delta, n1, i1, vec(b, 4))
    mixed_low = mixed_delta.astype(BF)
    ctx_delta = sum(dot_rt(mixed_low[:, 384 * h : 384 * h + 384], b.do[h]) for h in range(2)).astype(BF)
    cs = jnp.concatenate([ctx_delta * m for m in heads], axis=0)
    shares_delta = dot_rt(cs, v3)
    inner = jnp.sum(shares_delta * shares, axis=-1, keepdims=True)
    scores_delta = (shares * (shares_delta - inner)).astype(BF)
    dq3 = dot(scores_delta, k3) * 0.125
    dq = sum(dq3[32 * h : 32 * h + 32] * heads[h].astype(F32) for h in range(3))
    dk = dot_lt(scores_delta, qs) * 0.125
    dv = dot_lt(shares_low, cs)
    pd = jnp.concatenate((dq, dk, dv), axis=1).astype(BF)
    h_delta = dot_rt(pd, dp) + 0.25 * mixed_delta
    for i in range(16):
        b.slots[3][i] = h_delta[2 * i : 2 * i + 2]
    for k in (0, 1, 2, 3):
        if k:
            b.x.send(7, b.slots[3].at[8 * t.half + 2 * t.qq[k] + t.c], b.sdr.at[0, k], t.plane[k])
        b.x.send(
            8, b.slots[3].at[8 * (1 - t.half) + 2 * t.qq[k] + t.c], b.sdr.at[1, k], (4 * t.zo + t.qq[k], t.c)
        )
    b.sdr[0, 0] = b.slots[3][t.i]
    b.vg[4:5, :] = jnp.sum(first_delta * n1, axis=0, keepdims=True) * 0.125
    b.vg[5:6, :] = jnp.sum(first_delta, axis=0, keepdims=True) * 0.125
    halves(b.fq, (t.z, t.q, slice(None), slice(896, 1280)), pd)
    halves(b.fz, (t.z, slice(None), slice(1152, 1536)), mixed_low)
    b.f.relay(1)
    b.e.relay(1)
    b.f.first(0)
    b.e.first(0)
    yield
    b.f.second(0)
    b.x.arrived(6, b.soo)
    b.pairs[0][t.half] = b.slots[2][t.i]
    b.pairs[0][1 - t.half] = b.soo[...]
    yield
    b.x.arrived(7, b.sdr.at[0, pl.ds(0, 3)])
    b.x.arrived(8, b.sdr.at[1])
    b.pairs[1][t.half] = b.sdr[0, 0] + b.sdr[0, 1] + b.sdr[0, 2] + b.sdr[0, 3]
    b.pairs[1][1 - t.half] = b.sdr[1, 0] + b.sdr[1, 1] + b.sdr[1, 2] + b.sdr[1, 3]
    b.f.first(1)
    b.e.first(1)


def finish_output(b):
    first_row = lax.broadcasted_iota(jnp.int32, (16, 768), 0) == 0
    for m in range(2):
        for s in range(2):
            rows = pl.ds(128 * (2 * m + s), 16)
            fresh = jnp.where(first_row, b.pairs[0][m, s : s + 1, :], b.ob[rows, :].astype(F32))
            b.ob[rows, :] = fresh.astype(BF)
    b.put("out", b.ob)


def second_back(b):
    gain = vec(b, 2)

    def body(i, carry):
        gains, shifts = carry
        rows = off(i, 16, 16)
        late = (lax.broadcasted_iota(jnp.int32, (16, 768), 0) + 16 * lax.rem(i, 8)) == 0
        g = jnp.where(late, 0.0, b.cot[rows, :].astype(F32))
        n = b.n2[rows, :].astype(F32)
        delta = norm_back(g, n, b.i2[rows, :], gain)
        b.row[rows, :] = delta
        b.low[rows, :] = delta.astype(BF)
        return gains + g * n, shifts + g

    zero = jnp.zeros((16, 768), F32)
    gains, shifts = lax.fori_loop(0, 32, body, (zero, zero), unroll=2)
    b.vg[2:3, :] = jnp.sum(gains, axis=0, keepdims=True)
    b.vg[3:4, :] = jnp.sum(shifts, axis=0, keepdims=True)


def second_back_rows(b):
    gain = vec(b, 2)
    top = lax.broadcasted_iota(jnp.int32, (16, 768), 0) == 0
    gains, shifts = b.vg[2:3, :], b.vg[3:4, :]
    for s in range(4):
        rows = slice(128 * s, 128 * s + 16)
        g = b.pairs[1][s // 2, s % 2 : s % 2 + 1, :]
        n = b.n2[rows, :].astype(F32)
        delta = norm_back(jnp.where(top, g, 0.0), n, b.i2[rows, :], gain)
        b.row[rows, :] = jnp.where(top, delta, b.row[rows, :])
        low = jnp.where(top, delta, b.low[rows, :].astype(F32)).astype(BF)
        b.low[rows, :] = low
        b.lowc[16 * s : 16 * s + 16, :] = low
        gains += g * n[0:1]
        shifts += g
    b.vg[2:3, :] = gains
    b.vg[3:4, :] = shifts


def hidden_back_rows(b):
    w = b.w[4]

    @pl.loop(0, 4)
    def _(z):
        cols = off(z, 768)
        back = dot_rt(b.lowc[...], side_by_side(w[0, z], w[1, z], 768))
        delta = (back * b.gpc[:, cols].astype(F32)).astype(BF)
        b.gpc[:, cols] = delta
        for s in range(4):
            b.gp[pl.ds(128 * s, 16), cols] = delta[16 * s : 16 * s + 16]


def first_back_rows(b):
    w = b.w[3]
    top = lax.broadcasted_iota(jnp.int32, (16, 768), 0) == 0
    more = dot_rt(b.gpc[:, 0:1536], w[0].reshape(768, 1536)) + dot_rt(
        b.gpc[:, 1536:3072], w[1].reshape(768, 1536)
    )
    for s in range(4):
        rows = slice(128 * s, 128 * s + 16)
        b.row[rows, :] += jnp.where(top, more[16 * s : 16 * s + 16], 0.0)


def hidden_back(b):
    w = b.w[4]

    @pl.loop(0, 4)
    def _(z):
        cols = off(z, 768)
        for r in range(2):
            rows = pl.ds(256 * r, 256)
            back = dot_rt(b.low[rows, :], side_by_side(w[0, z], w[1, z], 768))
            b.gp[rows, cols] = (back * b.gp[rows, cols].astype(F32)).astype(BF)


def down_terms(b, r):
    t, w = b.t, b.w[4]
    for h in (t.o, t.c):
        for z in range(4):
            part = dot_lt(b.act[:, 768 * z : 768 * z + 768], b.low[:, off(h, 384)])
            w[h, z] = part.astype(BF).reshape(4, 192, 384)
            if h is t.o:
                r.pair_rows(z)


def first_back(b):
    w = b.w[3]

    @pl.loop(0, 2)
    def _(r):
        rows = off(r, 256, 256)
        for h in range(2):
            b.row[rows, :] += dot_rt(b.gp[rows, 1536 * h : 1536 * h + 1536], w[h].reshape(768, 1536))


def mixed_back(b):
    scale = vec(b, 0)

    def body(i, carry):
        scales, offsets = carry
        rows = off(i, 16, 16)
        g = b.row[rows, :]
        n = b.n1[rows, :].astype(F32)
        delta = norm_back(g, n, b.i1[rows, :], scale)
        b.row[rows, :] = delta
        b.low[rows, :] = delta.astype(BF)
        return scales + g * n, offsets + g

    zero = jnp.zeros((16, 768), F32)
    scales, offsets = lax.fori_loop(0, 32, body, (zero, zero), unroll=2)
    b.vg[0:1, :] = jnp.sum(scales, axis=0, keepdims=True)
    b.vg[1:2, :] = jnp.sum(offsets, axis=0, keepdims=True)


def context_back(b):
    w = b.w[2]
    b.flying.pop("out").wait()
    for r in range(2):
        rows = pl.ds(256 * r, 256)
        back = dot_rt(b.low[rows, :], side_by_side(w[0], w[1], 768))
        b.ob[rows, :] = back.astype(BF)


def attend_back(b, seg):
    low, high = lane_masks()
    rows = pl.ds(128 * seg, 128)

    lane = lax.broadcasted_iota(jnp.int32, (128, 128), 1)

    @pl.loop(0, 3)
    def _(i):
        pairs = (2 * i, 2 * i + 1)
        loaded = [[b.pr[rows, off(p + 6 * g, 128)] for g in range(3)] for p in pairs]
        deltas = [b.ob[rows, off(p, 128)] for p in pairs]
        shares = [b.sh[6 * seg + p] for p in pairs]
        stacked = [jnp.concatenate((q2 * low, q2 * high), axis=0) for q2, _, _ in loaded]
        cs = [jnp.concatenate((d2 * low, d2 * high), axis=0) for d2 in deltas]
        back = [dot_rt(c, v2) for c, (_, _, v2) in zip(cs, loaded)]
        wide = [v.astype(F32) for v in shares]
        inner = [jnp.sum(d * v, axis=-1, keepdims=True) for d, v in zip(back, wide)]
        ds = [(v * (d - n)).astype(BF) for v, d, n in zip(wide, back, inner)]
        dq = [dot(d, k2) * 0.125 for d, (_, k2, _) in zip(ds, loaded)]
        dk = [dot_lt(d, qs) * 0.125 for d, qs in zip(ds, stacked)]
        dv = [dot_lt(v, c) for v, c in zip(shares, cs)]
        for j, p in enumerate(pairs):
            b.pr[rows, off(p, 128)] = jnp.where(lane < 64, dq[j][:128], dq[j][128:]).astype(BF)
            b.pr[rows, off(p + 6, 128)] = dk[j].astype(BF)
            b.pr[rows, off(p + 12, 128)] = dv[j].astype(BF)


def input_back(b):
    w = b.w[1]

    @pl.loop(0, 2)
    def _(r):
        rows = off(r, 256, 256)
        for h in range(2):
            b.row[rows, :] += dot_rt(b.pr[rows, 1152 * h : 1152 * h + 1152], w[h].reshape(768, 1152))

    b.put("gin", b.row)


def column_terms(b, r, left, right):
    t, w = b.t, r.w
    n = len(r.windows)
    for h in (t.o, t.c):
        for j in range(n):
            part = dot_lt(left[...], right[:, off(n * h + j, 384)])
            w[h, :, :, :, pl.ds(384 * j, 384)] = part.astype(BF).reshape(4, 4, 48, 384)
            if h is t.o:
                r.pair(j)


def vectors_out(b):
    t, w = b.t, b.w[0]
    w[0] = jnp.transpose(b.vg[...]).reshape(4, 4, 48, 128)
    row = lax.broadcasted_iota(jnp.int32, (32, 768), 0)
    both = b.pairs[1][0] + b.pairs[1][1]
    places = jnp.where(row == 2 * t.i, both[0:1], 0.0) + jnp.where(row == 2 * t.i + 1, both[1:2], 0.0)
    b.vg[0:32, :] = places
    w[1] = jnp.transpose(b.vg[...]).reshape(4, 4, 48, 128)


def document_terms(b):
    t = b.t
    for k in range(3):
        b.f.finish(k)
        b.e.finish(k)
    b.f.drain()
    b.e.drain()
    own = 24 * t.dev
    part = 24 * lax.rem(t.dev, 8)
    fq, fz = b.fq, b.fz

    def rows_of(value, at, size):
        n = value.shape[1]
        b.flip[0:n, :] = jnp.transpose(value.astype(F32))
        return b.flip[pl.ds(pl.multiple_of(at, 8), size), :].astype(BF)

    def line(a):
        both = [fz[h, :, :, a : a + 384].reshape(128, 384) for h in range(2)]
        return jnp.concatenate(both, axis=1)

    def rank(q, a):
        both = [fq[h, :, q, :, a : a + 384].reshape(128, 384) for h in range(2)]
        return jnp.concatenate(both, axis=1)

    left = rows_of(fz[0, :, :, 0:768].reshape(128, 768), own, 24)
    for q in range(4):
        part_q = dot(left, rank(q, 896))
        for g in range(3):
            b.gdp[:, 768 * g + 192 * q : 768 * g + 192 * q + 192] = part_q[:, 256 * g : 256 * g + 192]
    left = rows_of(fq[1, :, t.z, :, 256:512].reshape(128, 256), part, 24)
    b.gdo[...] = dot(left, line(1152))
    left = rows_of(fz[1, :, :, 0:768].reshape(128, 768), own, 24)
    for q in range(4):
        b.gdu[:, 768 * q : 768 * q + 768] = dot(left, rank(q, 512))
    active = jnp.concatenate((fq[0, :, t.z, :, 0:512], fq[1, :, t.z, :, 0:256]), axis=-1)
    left = rows_of(active.reshape(128, 768), 4 * part, 96)
    b.gdd[...] = dot(left, line(768))
    for name in ("gdp", "gdo", "gdu", "gdd"):
        b.put(name, getattr(b, name))


def mega(*arrays):
    an = pl.BlockSpec(memory_space=pl.ANY)
    return pl.pallas_call(
        kernel,
        out_shape=[jax.ShapeDtypeStruct(shape, dt) for _, shape, dt in OUTS],
        in_specs=[an] * len(INS),
        out_specs=[an] * len(OUTS),
        scratch_shapes=[pltpu.VMEM(item.shape, item.dtype) for item in arrays]
        + [pltpu.VMEM(shape, dt) for _, shape, dt in OUTS[2:]]
        + [pltpu.VMEM(shape, dt) for items in SCRATCH.values() for shape, dt in items]
        + [pltpu.SemaphoreType.DMA(shape) for shape in SEMS.values()]
        + [pltpu.SemaphoreType.REGULAR] * 3,
        compiler_params=pltpu.CompilerParams(
            collective_id=1, has_side_effects=True, vmem_limit_bytes=65200 * 1024
        ),
    )(*arrays)


def hand_on_kernel(*refs):
    n = (len(refs) - 2) // 3
    src, dst, mid = refs[:n], refs[n : 2 * n], refs[2 * n : 3 * n]
    ins = [pltpu.make_async_copy(src[i], mid[i], refs[-2].at[i]) for i in range(n)]
    outs = [pltpu.make_async_copy(mid[i], dst[i], refs[-1].at[i]) for i in range(n)]
    for d in ins:
        d.start()
    for i in range(n):
        ins[i].wait()
        outs[i].start()
    for d in outs:
        d.wait()


def hand_on(*arrays):
    an = pl.BlockSpec(memory_space=pl.ANY)
    n = len(arrays)
    return pl.pallas_call(
        hand_on_kernel,
        out_shape=[jax.ShapeDtypeStruct(item.shape, item.dtype) for item in arrays],
        in_specs=[an] * n,
        out_specs=[an] * n,
        scratch_shapes=[pltpu.VMEM(item.shape, item.dtype) for item in arrays]
        + [pltpu.SemaphoreType.DMA((n,))] * 2,
        compiler_params=pltpu.CompilerParams(vmem_limit_bytes=63 * 2**20),
    )(*arrays)


def local_fast(tokens, token_counts, *rest):
    weights, cotangent = rest[:17], rest[17]
    width = tokens.shape[-1]
    rows = weights[0].shape[0]
    lane = jnp.arange(256)[None]
    small = jnp.pad(weights[16], ((0, 0), (128, 96)))
    for at, i in enumerate((4, 5, 6, 7, 12, 13, 14, 15)):
        small = jnp.where(lane == at, weights[i][:, None], small)
    small = small.astype(F32)
    outs = mega(
        tokens.reshape(-1, width),
        cotangent.reshape(-1, width),
        token_counts,
        small,
        *weights[:4],
        *weights[8:12],
    )
    gsmall = outs[2]
    out, gin, gsp, gso, gsu, gsd, gdp, gdo, gdu, gdd = hand_on(*outs[:2], *outs[3:])
    return (
        (out.reshape(tokens.shape), gin.reshape(tokens.shape), gsp, gso, gsu, gsd)
        + tuple(gsmall[:, i] for i in range(4))
        + (gdp, gdo, gdu, gdd)
        + tuple(gsmall[:, i] for i in range(4, 8))
        + (gsmall[:, 128:160],)
    )


def partner_2(value, axis, distance):
    mask = 2**distance
    pairs = [(source, source ^ mask) for source in range(lax.axis_size(axis))]
    return lax.ppermute(value, axis, pairs)


def product(left, right):
    return jnp.dot(left, right, preferred_element_type=jnp.float32)


def left_product(left, right):
    return lax.dot_general(
        left, right, (((0,), (0,)), ((), ())), preferred_element_type=jnp.float32
    )


def right_product(left, right):
    return lax.dot_general(
        left, right, (((1,), (1,)), ((), ())), preferred_element_type=jnp.float32
    )


def gelu_value(value):
    return 0.5 * value * (1.0 + lax.erf(value * root_half))


def gelu_slope(value):
    return (
        0.5 * (1.0 + lax.erf(value * root_half))
        + value * jnp.exp(-0.5 * value * value) * inverse_root_tau
    )


def norm_forward(value, gain, shift):
    centred = value - jnp.mean(value, axis=-1, keepdims=True)
    inverse = lax.rsqrt(jnp.mean(centred * centred, axis=-1, keepdims=True) + epsilon)
    normed = centred * inverse
    return (normed * gain + shift, normed, inverse)


def norm_backward(delta_out, normed, inverse, gain):
    scaled = delta_out * gain
    delta_in = inverse * (
        scaled
        - jnp.mean(scaled, axis=-1, keepdims=True)
        - normed * jnp.mean(scaled * normed, axis=-1, keepdims=True)
    )
    return (delta_in, jnp.sum(delta_out * normed, axis=0), jnp.sum(delta_out, axis=0))


def masked_scores(queries, keys, valid):
    scale = 1.0 / math.sqrt(queries.shape[-1])
    scores = (
        jnp.einsum("bqhe,bkhe->bhqk", queries, keys, preferred_element_type=jnp.float32) * scale
    )
    return jnp.where(valid[:, None], scores, floor_score)


def attend_forward(queries, keys, values, valid):
    scores = masked_scores(queries, keys, valid)
    highest = jnp.max(scores, axis=-1, keepdims=True)
    log_total = highest + jnp.log(jnp.sum(jnp.exp(scores - highest), axis=-1, keepdims=True))
    shares = jnp.exp(scores - log_total).astype(jnp.bfloat16)
    context = jnp.einsum("bhqk,bkhe->bqhe", shares, values, preferred_element_type=jnp.float32)
    return (context.astype(jnp.bfloat16), log_total)


def attend_backward(delta_context, queries, keys, values, valid, log_total):
    scale = 1.0 / math.sqrt(queries.shape[-1])
    shares = jnp.exp(masked_scores(queries, keys, valid) - log_total)
    delta_shares = jnp.einsum(
        "bqhe,bkhe->bhqk", delta_context, values, preferred_element_type=jnp.float32
    )
    delta_values = jnp.einsum(
        "bhqk,bqhe->bkhe",
        shares.astype(jnp.bfloat16),
        delta_context,
        preferred_element_type=jnp.float32,
    )
    inner = jnp.sum(delta_shares * shares, axis=-1, keepdims=True)
    delta_scores = (shares * (delta_shares - inner)).astype(jnp.bfloat16)
    delta_queries = (
        jnp.einsum("bhqk,bkhe->bqhe", delta_scores, keys, preferred_element_type=jnp.float32)
        * scale
    )
    delta_keys = (
        jnp.einsum("bhqk,bqhe->bkhe", delta_scores, queries, preferred_element_type=jnp.float32)
        * scale
    )
    return (delta_queries, delta_keys, delta_values)


def block_forward(inputs, layer, attend):
    (
        project_weight,
        output_weight,
        up_weight,
        down_weight,
        first_gain,
        first_shift,
        second_gain,
        second_shift,
    ) = layer
    inputs_low = inputs.astype(jnp.bfloat16)
    projected = product(inputs_low, project_weight).astype(jnp.bfloat16)
    context, attend_kept = attend(projected)
    mixed = product(context, output_weight)
    first, first_normed, first_inverse = norm_forward(
        inputs + mixed, first_gain.astype(jnp.float32), first_shift.astype(jnp.float32)
    )
    first_low = first.astype(jnp.bfloat16)
    hidden = product(first_low, up_weight)
    active = gelu_value(hidden).astype(jnp.bfloat16)
    second, second_normed, second_inverse = norm_forward(
        first + product(active, down_weight),
        second_gain.astype(jnp.float32),
        second_shift.astype(jnp.float32),
    )
    kept = (
        inputs_low,
        projected,
        context,
        attend_kept,
        first_normed,
        first_inverse,
        first_low,
        hidden,
        active,
        second_normed,
        second_inverse,
    )
    return (second, kept)


def block_backward(delta_out, kept, layer, attend_back):
    (
        project_weight,
        output_weight,
        up_weight,
        down_weight,
        first_gain,
        first_shift,
        second_gain,
        second_shift,
    ) = layer
    (
        inputs_low,
        projected,
        context,
        attend_kept,
        first_normed,
        first_inverse,
        first_low,
        hidden,
        active,
        second_normed,
        second_inverse,
    ) = kept
    delta_second, second_gain_delta, second_shift_delta = norm_backward(
        delta_out, second_normed, second_inverse, second_gain.astype(jnp.float32)
    )
    branch_low = delta_second.astype(jnp.bfloat16)
    delta_down = left_product(active, branch_low)
    delta_hidden = (right_product(branch_low, down_weight) * gelu_slope(hidden)).astype(
        jnp.bfloat16
    )
    delta_up = left_product(first_low, delta_hidden)
    delta_first = delta_second + right_product(delta_hidden, up_weight)
    delta_mixed, first_gain_delta, first_shift_delta = norm_backward(
        delta_first, first_normed, first_inverse, first_gain.astype(jnp.float32)
    )
    mixed_low = delta_mixed.astype(jnp.bfloat16)
    delta_output = left_product(context, mixed_low)
    delta_context = right_product(mixed_low, output_weight).astype(jnp.bfloat16)
    delta_projected = attend_back(delta_context, projected, attend_kept)
    delta_project = left_product(inputs_low, delta_projected)
    delta_inputs = delta_mixed + right_product(delta_projected, project_weight)
    return (
        delta_inputs,
        (
            delta_project,
            delta_output,
            delta_up,
            delta_down,
            first_gain_delta,
            first_shift_delta,
            second_gain_delta,
            second_shift_delta,
        ),
    )


def local(
    tokens,
    token_counts,
    segment_project,
    segment_output,
    segment_up,
    segment_down,
    segment_scale,
    segment_offset,
    segment_gain,
    segment_shift,
    document_project,
    document_output,
    document_up,
    document_down,
    document_scale,
    document_offset,
    document_gain,
    document_shift,
    position,
    cotangent,
):
    batches, segments, length, width = tokens.shape
    heads = HEADS
    head_width = width // heads
    rows_total = segments * length
    index = lax.axis_index(("seg", "rep"))
    first_segment = index * segments
    own_document = first_segment // DOC_SEGS
    positions = jnp.arange(length)
    slots = (first_segment + jnp.arange(segments)) % DOC_SEGS
    picker = (slots[:, None] == jnp.arange(DOC_SEGS)[None, :]).astype(jnp.float32)
    levels = (DOC_SEGS // segments).bit_length() - 1
    gathered_once = (
        lax.all_gather(segment_project, ("seg", "rep"), axis=0, tiled=True),
        lax.all_gather(segment_output, ("seg", "rep"), axis=0, tiled=True),
        lax.all_gather(segment_up, ("seg", "rep"), axis=0, tiled=True),
        lax.all_gather(segment_down, ("seg", "rep"), axis=0, tiled=True),
        lax.all_gather(segment_scale, ("seg", "rep"), axis=0, tiled=True),
        lax.all_gather(segment_offset, ("seg", "rep"), axis=0, tiled=True),
        lax.all_gather(segment_gain, ("seg", "rep"), axis=0, tiled=True),
        lax.all_gather(segment_shift, ("seg", "rep"), axis=0, tiled=True),
        lax.all_gather(document_project, ("seg", "rep"), axis=0, tiled=True),
        lax.all_gather(document_output, ("seg", "rep"), axis=0, tiled=True),
        lax.all_gather(document_up, ("seg", "rep"), axis=0, tiled=True),
        lax.all_gather(document_down, ("seg", "rep"), axis=0, tiled=True),
        lax.all_gather(document_scale, ("seg", "rep"), axis=0, tiled=True),
        lax.all_gather(document_offset, ("seg", "rep"), axis=0, tiled=True),
        lax.all_gather(document_gain, ("seg", "rep"), axis=0, tiled=True),
        lax.all_gather(document_shift, ("seg", "rep"), axis=0, tiled=True),
        lax.all_gather(position, ("seg", "rep"), axis=0, tiled=True),
    )
    outputs = []
    deltas = []
    totals = None
    for batch in range(batches):
        segment_layer = gathered_once[0:8]
        document_layer = gathered_once[8:16]
        table = jnp.transpose(gathered_once[16].astype(jnp.float32))
        counts_row = token_counts[batch]
        local_counts = lax.dynamic_slice_in_dim(counts_row, first_segment, segments)
        token_valid = (positions[None, :] < local_counts[:, None]) | (positions[None, :] == 0)
        segment_valid = token_valid[:, None, :]

        def segment_attend(projected):
            parts = projected.reshape(segments, length, 3, heads, head_width)
            context, log_total = attend_forward(
                parts[:, :, 0], parts[:, :, 1], parts[:, :, 2], segment_valid
            )
            return (context.reshape(rows_total, width), log_total)

        def segment_back(delta_context, projected, log_total):
            parts = projected.reshape(segments, length, 3, heads, head_width)
            delta_queries, delta_keys, delta_values = attend_backward(
                delta_context.reshape(segments, length, heads, head_width),
                parts[:, :, 0],
                parts[:, :, 1],
                parts[:, :, 2],
                segment_valid,
                log_total,
            )
            return (
                jnp.stack((delta_queries, delta_keys, delta_values), axis=2)
                .reshape(rows_total, 3 * width)
                .astype(jnp.bfloat16)
            )

        def document_attend(projected):
            queries = projected[:, :width].reshape(1, segments, heads, head_width)
            pairs = projected[:, width:]
            collected = pairs[None]
            for bit in range(levels):
                partner = partner_2(collected, ("seg", "rep"), bit)
                upper = jnp.right_shift(index, bit) % 2
                collected = jnp.where(
                    upper == 0,
                    jnp.concatenate((collected, partner), axis=0),
                    jnp.concatenate((partner, collected), axis=0),
                )
            collected = collected.reshape(DOC_SEGS, 2 * width)
            key_valid = lax.dynamic_slice_in_dim(counts_row, own_document * DOC_SEGS, DOC_SEGS) > 0
            keys = collected[:, :width].reshape(1, DOC_SEGS, heads, head_width)
            values = collected[:, width:].reshape(1, DOC_SEGS, heads, head_width)
            valid = key_valid[None, None, :]
            context, log_total = attend_forward(queries, keys, values, valid)
            return (context.reshape(segments, width), (collected, valid, log_total))

        def document_back(delta_context, projected, kept_rows):
            collected, valid, log_total = kept_rows
            queries = projected[:, :width].reshape(1, segments, heads, head_width)
            keys = collected[:, :width].reshape(1, DOC_SEGS, heads, head_width)
            values = collected[:, width:].reshape(1, DOC_SEGS, heads, head_width)
            delta_queries, delta_keys, delta_values = attend_backward(
                delta_context.reshape(1, segments, heads, head_width),
                queries,
                keys,
                values,
                valid,
                log_total,
            )
            delta_pairs = jnp.concatenate(
                (delta_keys.reshape(DOC_SEGS, width), delta_values.reshape(DOC_SEGS, width)), axis=1
            )
            folded = delta_pairs.reshape(DOC_SEGS // segments, segments, 2 * width)
            for bit in reversed(range(levels)):
                halves = folded.reshape(2, folded.shape[0] // 2, segments, 2 * width)
                upper = jnp.right_shift(index, bit) % 2
                keep = jnp.where(upper == 0, halves[0], halves[1])
                send = jnp.where(upper == 0, halves[1], halves[0])
                folded = keep + partner_2(send.astype(jnp.bfloat16), ("seg", "rep"), bit).astype(
                    send.dtype
                )
            own_pairs = folded.reshape(segments, 2 * width)
            return jnp.concatenate(
                (delta_queries.reshape(segments, width), own_pairs), axis=1
            ).astype(jnp.bfloat16)

        inputs = tokens[batch].astype(jnp.float32).reshape(rows_total, width)
        segment_rows, segment_kept = block_forward(inputs, segment_layer, segment_attend)
        segment_rows = segment_rows.reshape(segments, length, width)
        lookup = jnp.sum(picker[:, :, None] * table[None, :, :], axis=1)
        summary_rows = segment_rows[:, 0, :] + lookup
        summary_out, document_kept = block_forward(summary_rows, document_layer, document_attend)
        outputs.append(segment_rows.at[:, 0, :].set(summary_out).astype(jnp.bfloat16))
        incoming = cotangent[batch].astype(jnp.float32)
        delta_summary, document_deltas = block_backward(
            incoming[:, 0, :], document_kept, document_layer, document_back
        )
        delta_table = jnp.transpose(jnp.sum(picker[:, :, None] * delta_summary[:, None, :], axis=0))
        delta_rows = incoming.at[:, 0, :].set(delta_summary).reshape(rows_total, width)
        delta_inputs, segment_deltas = block_backward(
            delta_rows, segment_kept, segment_layer, segment_back
        )
        deltas.append(delta_inputs.reshape(segments, length, width))
        current = segment_deltas + document_deltas + (delta_table,)
        totals = (
            current
            if totals is None
            else tuple((left + right for left, right in zip(totals, current)))
        )
    groups = lax.axis_size("seg")
    shaped = tuple(
        (item.reshape((groups, item.shape[0] // groups) + item.shape[1:]) for item in totals)
    )
    received = (
        lax.all_to_all(
            shaped[0].astype(jnp.bfloat16), "seg", split_axis=0, concat_axis=0, tiled=True
        ).astype(jnp.float32),
        lax.all_to_all(
            shaped[1].astype(jnp.bfloat16), "seg", split_axis=0, concat_axis=0, tiled=True
        ).astype(jnp.float32),
        lax.all_to_all(
            shaped[2].astype(jnp.bfloat16), "seg", split_axis=0, concat_axis=0, tiled=True
        ).astype(jnp.float32),
        lax.all_to_all(
            shaped[3].astype(jnp.bfloat16), "seg", split_axis=0, concat_axis=0, tiled=True
        ).astype(jnp.float32),
        lax.all_to_all(
            shaped[4].astype(jnp.bfloat16), "seg", split_axis=0, concat_axis=0, tiled=True
        ).astype(jnp.float32),
        lax.all_to_all(
            shaped[5].astype(jnp.bfloat16), "seg", split_axis=0, concat_axis=0, tiled=True
        ).astype(jnp.float32),
        lax.all_to_all(
            shaped[6].astype(jnp.bfloat16), "seg", split_axis=0, concat_axis=0, tiled=True
        ).astype(jnp.float32),
        lax.all_to_all(
            shaped[7].astype(jnp.bfloat16), "seg", split_axis=0, concat_axis=0, tiled=True
        ).astype(jnp.float32),
        lax.all_to_all(
            shaped[8].astype(jnp.bfloat16), "seg", split_axis=0, concat_axis=0, tiled=True
        ).astype(jnp.float32),
        lax.all_to_all(
            shaped[9].astype(jnp.bfloat16), "seg", split_axis=0, concat_axis=0, tiled=True
        ).astype(jnp.float32),
        lax.all_to_all(
            shaped[10].astype(jnp.bfloat16), "seg", split_axis=0, concat_axis=0, tiled=True
        ).astype(jnp.float32),
        lax.all_to_all(
            shaped[11].astype(jnp.bfloat16), "seg", split_axis=0, concat_axis=0, tiled=True
        ).astype(jnp.float32),
        lax.all_to_all(
            shaped[12].astype(jnp.bfloat16), "seg", split_axis=0, concat_axis=0, tiled=True
        ).astype(jnp.float32),
        lax.all_to_all(
            shaped[13].astype(jnp.bfloat16), "seg", split_axis=0, concat_axis=0, tiled=True
        ).astype(jnp.float32),
        lax.all_to_all(
            shaped[14].astype(jnp.bfloat16), "seg", split_axis=0, concat_axis=0, tiled=True
        ).astype(jnp.float32),
        lax.all_to_all(
            shaped[15].astype(jnp.bfloat16), "seg", split_axis=0, concat_axis=0, tiled=True
        ).astype(jnp.float32),
        lax.all_to_all(
            shaped[16].astype(jnp.bfloat16), "seg", split_axis=0, concat_axis=0, tiled=True
        ).astype(jnp.float32),
    )
    summed = tuple((jnp.sum(item, axis=0) for item in received))
    reduced = (
        lax.psum_scatter(
            summed[0].astype(jnp.bfloat16), "rep", scatter_dimension=0, tiled=True
        ).astype(jnp.float32),
        lax.psum_scatter(
            summed[1].astype(jnp.bfloat16), "rep", scatter_dimension=0, tiled=True
        ).astype(jnp.float32),
        lax.psum_scatter(
            summed[2].astype(jnp.bfloat16), "rep", scatter_dimension=0, tiled=True
        ).astype(jnp.float32),
        lax.psum_scatter(
            summed[3].astype(jnp.bfloat16), "rep", scatter_dimension=0, tiled=True
        ).astype(jnp.float32),
        lax.psum_scatter(
            summed[4].astype(jnp.bfloat16), "rep", scatter_dimension=0, tiled=True
        ).astype(jnp.float32),
        lax.psum_scatter(
            summed[5].astype(jnp.bfloat16), "rep", scatter_dimension=0, tiled=True
        ).astype(jnp.float32),
        lax.psum_scatter(
            summed[6].astype(jnp.bfloat16), "rep", scatter_dimension=0, tiled=True
        ).astype(jnp.float32),
        lax.psum_scatter(
            summed[7].astype(jnp.bfloat16), "rep", scatter_dimension=0, tiled=True
        ).astype(jnp.float32),
        lax.psum_scatter(
            summed[8].astype(jnp.bfloat16), "rep", scatter_dimension=0, tiled=True
        ).astype(jnp.float32),
        lax.psum_scatter(
            summed[9].astype(jnp.bfloat16), "rep", scatter_dimension=0, tiled=True
        ).astype(jnp.float32),
        lax.psum_scatter(
            summed[10].astype(jnp.bfloat16), "rep", scatter_dimension=0, tiled=True
        ).astype(jnp.float32),
        lax.psum_scatter(
            summed[11].astype(jnp.bfloat16), "rep", scatter_dimension=0, tiled=True
        ).astype(jnp.float32),
        lax.psum_scatter(
            summed[12].astype(jnp.bfloat16), "rep", scatter_dimension=0, tiled=True
        ).astype(jnp.float32),
        lax.psum_scatter(
            summed[13].astype(jnp.bfloat16), "rep", scatter_dimension=0, tiled=True
        ).astype(jnp.float32),
        lax.psum_scatter(
            summed[14].astype(jnp.bfloat16), "rep", scatter_dimension=0, tiled=True
        ).astype(jnp.float32),
        lax.psum_scatter(
            summed[15].astype(jnp.bfloat16), "rep", scatter_dimension=0, tiled=True
        ).astype(jnp.float32),
        lax.psum_scatter(
            summed[16].astype(jnp.bfloat16), "rep", scatter_dimension=0, tiled=True
        ).astype(jnp.float32),
    )
    return (jnp.stack(outputs), jnp.stack(deltas)) + tuple(reduced)


def solution(mesh):
    sizes = dict(mesh.shape)
    body = local_fast if (sizes["seg"], sizes["rep"]) == (16, 2) else local
    return jax.shard_map(
        body,
        mesh=mesh,
        in_specs=(
            P(None, ("seg", "rep"), None, None),
            P(),
            P(("seg", "rep"), None),
            P(("seg", "rep"), None),
            P(("seg", "rep"), None),
            P(("seg", "rep"), None),
            P(("seg", "rep")),
            P(("seg", "rep")),
            P(("seg", "rep")),
            P(("seg", "rep")),
            P(("seg", "rep"), None),
            P(("seg", "rep"), None),
            P(("seg", "rep"), None),
            P(("seg", "rep"), None),
            P(("seg", "rep")),
            P(("seg", "rep")),
            P(("seg", "rep")),
            P(("seg", "rep")),
            P(("seg", "rep"), None),
            P(None, ("seg", "rep"), None, None),
        ),
        out_specs=(
            P(None, ("seg", "rep"), None, None),
            P(None, ("seg", "rep"), None, None),
            P(("seg", "rep"), None),
            P(("seg", "rep"), None),
            P(("seg", "rep"), None),
            P(("seg", "rep"), None),
            P(("seg", "rep")),
            P(("seg", "rep")),
            P(("seg", "rep")),
            P(("seg", "rep")),
            P(("seg", "rep"), None),
            P(("seg", "rep"), None),
            P(("seg", "rep"), None),
            P(("seg", "rep"), None),
            P(("seg", "rep")),
            P(("seg", "rep")),
            P(("seg", "rep")),
            P(("seg", "rep")),
            P(("seg", "rep"), None),
        ),
        check_vma=False,
    )
```

```python
import math
import jax
import jax.numpy as jnp
from jax import lax
from jax.experimental import pallas as pl
from jax.experimental.pallas import tpu as pltpu
from jax.sharding import PartitionSpec as P

MESH = pl.DeviceIdType.MESH
F32 = jnp.float32
BF = jnp.bfloat16
HEADS = 12
DOC_SEGS = 32
epsilon = 1e-05
floor_score = -1e30
root_half = 1.0 / math.sqrt(2.0)
inverse_root_tau = 1.0 / math.sqrt(2.0 * math.pi)


class Spot:
    def __init__(self):
        s, c = lax.axis_index("seg"), lax.axis_index("rep")
        z, y, x = lax.div(s, 4), lax.rem(lax.div(s, 2), 2), lax.rem(s, 2)
        self.s, self.c, self.z = s, c, z
        self.o = 1 - c
        y1, x1 = y + c * (1 - 2 * y), x + (1 - c) * (1 - 2 * x)
        y2, x2 = y + (1 - c) * (1 - 2 * y), x + c * (1 - 2 * x)
        self.q = 2 * y + x
        self.q1 = 2 * y1 + x1
        self.q2 = 2 * y2 + x2
        self.q12 = 3 - self.q
        self.sib = (s, 1 - c)
        self.n1 = (4 * z + self.q1, c)
        self.n2 = (4 * z + self.q2, c)
        self.diagonal = (4 * z + self.q12, c)
        self.zz = [lax.rem(z + k, 4) for k in (1, 2, 3)]
        odd, high = lax.rem(z, 2), lax.div(z, 2)
        self.middle = (z == 1) | (z == 2)
        self.end = (z == 0) | (z == 3)
        self.zs = [
            (4 * (1 + odd) + self.q, c),
            (4 * ((1 - odd) * (2 + high) + odd * high) + self.q, c),
        ]
        self.pass_from = jnp.where(z == 1, 2, 0)
        self.tip = (4 * jnp.where(z == 2, 3, 0) + self.q, c)
        self.zn = [(4 * zz + self.q, c) for zz in self.zz]
        self.qq = [lax.rem(self.q + k, 4) for k in (0, 1, 2, 3)]
        self.plane = [(4 * z + qq, c) for qq in self.qq]
        self.half = lax.rem(z, 2)
        self.zo = z + 1 - 2 * self.half
        self.i = 8 * self.half + 2 * self.q + c
        self.dev = 2 * s + c


def remote(src, dst, ssem, rsem, dev):
    return pltpu.make_async_remote_copy(
        src_ref=src, dst_ref=dst, send_sem=ssem, recv_sem=rsem, device_id=dev, device_id_type=MESH
    )


def enter(t):
    bar = pltpu.get_barrier_semaphore()
    everyone = [t.sib, t.n1, t.n2, t.diagonal] + t.zn
    for dev in everyone:
        pl.semaphore_signal(bar, inc=1, device_id=dev, device_id_type=MESH)
    pl.semaphore_wait(bar, len(everyone))


def pass_on(t, sem):
    for dev in (t.sib, t.n1, t.n2, t.diagonal):
        pl.semaphore_signal(sem, inc=1, device_id=dev, device_id_type=MESH)


class Sender:
    def __init__(self, t, ss, rs):
        self.t, self.ss, self.rs, self.pending = t, ss, rs, []

    def send(self, at, src, dst, dev):
        d = remote(src, dst, self.ss, self.rs.at[at], dev)
        d.start()
        self.pending.append(d)

    def arrived(self, at, ref):
        remote(ref, ref, self.ss, self.rs.at[at], self.t.sib).wait_recv()

    def drain(self):
        for d in self.pending:
            if isinstance(d, tuple):
                pl.when(d[0])(d[1].wait_send)
            else:
                d.wait_send()
        self.pending = []

    def z_spread(self, at, view):
        t = self.t
        for dev in t.zs:
            self.send(at, view(t.z), view(t.z), dev)

    def z_relay(self, at, at2, view):
        t = self.t
        two = view(pl.ds(t.pass_from, 2))
        d = remote(two, two, self.ss, self.rs.at[at2], t.tip)

        @pl.when(t.middle)
        def _():
            self.arrived(at, view(pl.ds(0, 3)))
            d.start()

        self.pending.append((t.middle, d))

    def z_last(self, at, at2, view):
        @pl.when(self.t.end)
        def _():
            self.arrived(at, view(0))
            self.arrived(at2, view(pl.ds(0, 2)))


def off(at, size, step=128):
    return pl.ds(pl.multiple_of(at * size, step), size)


def join_pair(t, shard, got, tmp, dest):
    rd, n2 = got.shape
    wide = tmp.shape[1]
    for j in range(0, n2, wide):
        mine = pl.ds(pl.multiple_of(t.c * n2 + j, 128), wide)
        tmp[off(t.c, rd, 8), :] = shard[:, mine].astype(F32)
        tmp[off(t.o, rd, 8), :] = got[:, j : j + wide].astype(F32)
        dest[:, pl.ds(j, wide)] = tmp[...].astype(dest.dtype)


class Gather(Sender):
    def __init__(self, t, far, shard, w, got, tmp, windows, ss, rs):
        super().__init__(t, ss, rs)
        self.far, self.shard, self.w, self.got, self.tmp, self.windows = far, shard, w, got, tmp, windows

    def pair(self):
        n2 = self.got.shape[1]
        self.send(5 * len(self.windows), self.far.at[:, off(self.t.o, n2)], self.got, self.t.sib)

    def join(self):
        t = self.t
        self.arrived(5 * len(self.windows), self.got)
        join_pair(t, self.shard, self.got, self.tmp, self.w.at[t.c, t.z, t.q])

    def pick(self, k, *lead):
        rows, cols = self.windows[k]
        return self.w.at[(self.t.c,) + lead + (pl.ds(*rows), pl.ds(*cols))]

    def line(self, k, q):
        return self.pick(k, slice(None), q)

    def view(self, k):
        return lambda at: self.pick(k, at, self.t.q)

    def spread(self, k):
        self.z_spread(5 * k, self.view(k))

    def relay(self, k):
        self.z_relay(5 * k, 5 * k + 1, self.view(k))

    def first(self, k):
        t = self.t
        self.z_last(5 * k, 5 * k + 1, self.view(k))
        line = self.line(k, t.q)
        self.send(5 * k + 2, line, line, t.n1)
        self.send(5 * k + 4, line, line, t.sib)

    def second(self, k):
        t = self.t
        line, other = self.line(k, t.q), self.line(k, t.q1)
        self.arrived(5 * k + 2, other)
        self.send(5 * k + 3, line, line, t.n2)
        self.send(5 * k + 3, other, other, t.n2)
        self.send(5 * k + 4, other, other, t.sib)

    def third(self, k):
        t = self.t
        self.arrived(5 * k + 3, self.pick(k, slice(None), pl.ds(0, 2)))
        for q in (t.q2, t.q12):
            self.send(5 * k + 4, self.line(k, q), self.line(k, q), t.sib)

    def finish(self, k):
        self.arrived(5 * k + 4, self.pick(k, slice(None), slice(None)))


class LineGather(Sender):
    def __init__(self, t, w, windows, ss, rs):
        super().__init__(t, ss, rs)
        self.w, self.windows = w, windows

    def view(self, k):
        cols = self.windows[k]
        return lambda at: self.w.at[self.t.c, at, :, pl.ds(*cols)]

    def spread(self, k):
        self.z_spread(3 * k, self.view(k))

    def relay(self, k):
        self.z_relay(3 * k, 3 * k + 1, self.view(k))

    def first(self, k):
        self.z_last(3 * k, 3 * k + 1, self.view(k))
        line = self.view(k)(slice(None))
        self.send(3 * k + 2, line, line, self.t.sib)

    def finish(self, k):
        self.arrived(3 * k + 2, self.view(k)(slice(None)))


class DocGather(Sender):
    def __init__(self, t, far, shards, stages, gots, tmps, dpu, do, dd, ss, rs, ls):
        super().__init__(t, ss, rs)
        self.far, self.shards, self.stages, self.gots, self.tmps = far, shards, stages, gots, tmps
        self.dpu, self.do, self.dd, self.ls = dpu, do, dd, ls
        main, down = stages
        self.views = [(lambda at, k=k: dpu.at[t.c, at, k]) for k in range(4)]
        self.views.append(lambda at: main.at[at, :, pl.ds(3072, 384)])
        self.views += [(lambda at, j=j: down.at[at, pl.ds(96 * j, 96)]) for j in range(2)]

    def pair(self):
        dp, do, du, dd = self.far
        for i, ref in enumerate((dp, do, du)):
            self.send(i, ref, self.gots[i], self.t.sib)
        self.send(3, dd.at[:, off(self.t.o, 384)], self.gots[3], self.t.sib)

    def join(self):
        t = self.t
        dp, do, du, dd = self.shards
        for i in range(4):
            self.arrived(i, self.gots[i])
        main, down = self.stages
        tmp = self.tmps[0]
        mine, other = off(t.c, 24, 8), off(t.o, 24, 8)

        def place(ref, got, a, n, b):
            tmp[mine, 0:n] = ref[:, a : a + n].astype(F32)
            tmp[other, 0:n] = got[:, a : a + n].astype(F32)
            wide = -(-n // 128) * 128
            main[t.z, :, b : b + wide] = tmp[:, 0:wide].astype(BF)

        @pl.when(t.c == 0)
        def _():
            tmp[...] = jnp.zeros(tmp.shape, F32)
            for r in range(4):
                for g in range(3):
                    place(dp, self.gots[0], 768 * g + 192 * r, 192, 768 * r + 256 * g)
            place(do, self.gots[1], 0, 384, 3072)

        @pl.when(t.c == 1)
        def _():
            for r in range(4):
                place(du, self.gots[2], 768 * r, 768, 768 * r)
            place(do, self.gots[1], 384, 384, 3072)

        join_pair(t, dd, self.gots[3], self.tmps[1], down.at[t.z])

    def ranks(self):
        t = self.t
        main = self.stages[0]
        for k in (1, 2, 3):
            self.send(18, main.at[t.z, :, off(t.qq[k], 768)], self.dpu.at[t.c, t.z, t.q], t.plane[k])
        d = pltpu.make_async_copy(main.at[t.z, :, off(t.q, 768)], self.dpu.at[t.c, t.z, t.q], self.ls.at[0])
        d.start()
        self.local = [d]

    def spread(self, k):
        t = self.t
        if k == 0:
            self.arrived(18, self.dpu.at[t.c, t.z, pl.ds(0, 3)])
            self.local.pop().wait()
        self.z_spread(4 + k, self.views[k])

    def relay(self, k):
        self.z_relay(4 + k, 11 + k, self.views[k])

    def plane(self, w):
        t = self.t
        main, down = self.stages
        self.z_last(4 + w, 11 + w, self.views[w])
        if w < 4:
            return
        for k in (1, 2, 3, 0):
            q = t.qq[k]
            if w == 4:
                src, at = main.at[q, :, pl.ds(3072, 384)], 19
                dst = self.do.at[t.c, pl.ds(pl.multiple_of(48 * t.q, 16), 48)]
            else:
                rows = pl.ds(96 * (w - 5), 96)
                src, dst, at = down.at[q, rows], self.dd.at[t.c, t.q, rows], 15 + w
            if k:
                self.send(at, src, dst, t.plane[k])
            else:
                d = pltpu.make_async_copy(src, dst, self.ls.at[at - 18])
                d.start()
                self.local.append(d)

    def share(self):
        t = self.t
        self.arrived(19, self.do.at[t.c, pl.ds(0, 144)])
        for j in range(2):
            self.arrived(20 + j, self.dd.at[t.c, pl.ds(0, 3), pl.ds(0, 96)])
        for d in self.local:
            d.wait()
        for i, ref in enumerate((self.dpu, self.do, self.dd)):
            view = ref.at[t.c, pl.ds(0, 192)] if i == 1 else ref.at[t.c]
            self.send(22 + i, view, view, t.sib)

    def finish(self, i):
        ref = (self.dpu, self.do, self.dd)[i]
        view = ref.at[self.t.o, pl.ds(0, 192)] if i == 1 else ref.at[self.t.o]
        self.arrived(22 + i, view)


class Reduce(Sender):
    def __init__(self, t, w, rc_, r1, r2, r3, fin, fin2, out, windows, ss, rs):
        super().__init__(t, ss, rs)
        self.w, self.rc, self.r1, self.r2, self.r3 = w, rc_, r1, r2, r3
        self.fin, self.fin2, self.out, self.windows = fin, fin2, out, windows
        self.by_rows = fin2.shape[0] == 96
        self.z_early = (1, 3) if len(windows) == 4 else (1,)

    def add_one(self, k, q, parts):
        (r, rn), (a, an) = self.windows[k]
        total = self.w[self.t.c, self.t.z, q, r : r + rn, a : a + an].astype(F32)
        for part in parts:
            total = total + part[r : r + rn, a : a + an].astype(F32)
        return total

    def z_send(self, k, at, q, slots):
        t = self.t
        for i in range(3):
            self.send(at, self.cut(self.w, k, t.c, t.zz[i], q), self.cut(slots, k, 2 - i), t.zn[i])

    def cut(self, ref, k, *lead):
        rows, cols = self.windows[k]
        lead += (slice(None),) * (len(ref.shape) - 2 - len(lead))
        return ref.at[lead + (pl.ds(*rows), pl.ds(*cols))]

    def pair(self, k):
        self.send(6 * k, self.cut(self.w, k, self.t.o), self.cut(self.rc, k), self.t.sib)

    def pair_rows(self, z):
        self.send(6 * z, self.w.at[self.t.o, z], self.rc.at[z], self.t.sib)

    def add(self, k, q, part):
        (r, rn), (a, an) = self.windows[k]
        w, c = self.w, self.t.c

        @pl.loop(0, 4)
        def _(z):
            at = (c, z, q, pl.ds(r, rn), pl.ds(a, an))
            w[at] = (w[at].astype(F32) + part[z, r : r + rn, a : a + an].astype(F32)).astype(w.dtype)

    def first(self, k):
        t = self.t
        if self.by_rows:
            for z in range(4 if k == 0 else 0):
                self.arrived(6 * z, self.rc.at[z])
        else:
            self.arrived(6 * k, self.cut(self.rc, k))
        for i, q in ((0, t.q2), (1, t.q12)):
            self.add(k, q, self.rc.at[:, q])
            self.send(
                6 * k + 1 + i, self.cut(self.w, k, t.c, slice(None), q), self.cut(self.r1, k, i, slice(None)), t.n2
            )
        for q in (t.q, t.q1):
            self.add(k, q, self.rc.at[:, q])

    def second(self, k):
        t = self.t
        self.arrived(6 * k + 2, self.cut(self.r1, k, 1, slice(None)))
        self.add(k, t.q1, self.r1.at[1])
        if k in self.z_early:
            self.z_send(k, 6 * k + 3, t.q1, self.r2)
            self.arrived(6 * k + 1, self.cut(self.r1, k, 0, slice(None)))
            self.add(k, t.q, self.r1.at[0])
            self.z_send(k, 6 * k + 4, t.q, self.r3)
            return
        self.send(6 * k + 3, self.cut(self.w, k, t.c, slice(None), t.q1), self.cut(self.r2, k, slice(None)), t.n1)
        self.arrived(6 * k + 1, self.cut(self.r1, k, 0, slice(None)))
        self.add(k, t.q, self.r1.at[0])

    def third(self, k):
        t = self.t
        if k in self.z_early:
            (r, rn), (a, an) = self.windows[k]
            self.arrived(6 * k + 3, self.cut(self.r2, k, pl.ds(0, 3)))
            total = self.add_one(k, t.q1, [self.r2.at[i] for i in range(3)])
            self.w[t.c, t.z, t.q1, r : r + rn, a : a + an] = total.astype(self.w.dtype)
            self.send(6 * k + 5, self.cut(self.w, k, t.c, t.z, t.q1), self.cut(self.r2, k, 3), t.n1)
            return
        self.arrived(6 * k + 3, self.cut(self.r2, k, slice(None)))
        self.add(k, t.q, self.r2)
        self.z_send(k, 6 * k + 4, t.q, self.r3)

    def fourth(self, k):
        t = self.t
        (r, rn), (a, an) = self.windows[k]
        self.arrived(6 * k + 4, self.cut(self.r3, k, slice(None)))
        parts = [self.r3.at[i] for i in range(3)]
        if k in self.z_early:
            self.arrived(6 * k + 5, self.cut(self.r2, k, 3))
            parts.append(self.r2.at[3])
        self.fin[r : r + rn, a : a + an] = self.add_one(k, t.q, parts)
        if k == len(self.windows) - 1:
            rd = self.fin.shape[0] // 2
            self.send(6 * len(self.windows), self.fin.at[off(t.o, rd, 8)], self.fin2, t.sib)

    def fifth(self):
        t = self.t
        rd, n2 = self.fin2.shape
        self.arrived(6 * len(self.windows), self.fin2)
        self.out[:, off(t.c, n2)] = self.fin[off(t.c, rd, 8), :]
        self.out[:, off(t.o, n2)] = self.fin2[...]


def dot(a, b):
    return jnp.dot(a, b, preferred_element_type=F32)


def dot_rt(a, b):
    return lax.dot_general(a, b, (((1,), (1,)), ((), ())), preferred_element_type=F32)


def dot_lt(a, b):
    return lax.dot_general(a, b, (((0,), (0,)), ((), ())), preferred_element_type=F32)


def normed(v):
    centred = v - jnp.mean(v, axis=-1, keepdims=True)
    inverse = lax.rsqrt(jnp.mean(centred * centred, axis=-1, keepdims=True) + epsilon)
    return centred * inverse, inverse


def norm_back(g, n, inverse, gain):
    v = g * gain
    return inverse * (
        v - jnp.mean(v, axis=-1, keepdims=True) - n * jnp.mean(v * n, axis=-1, keepdims=True)
    )


def gelu_pair(v):
    share = 0.5 * (1.0 + lax.erf(v * root_half))
    return v * share, share + v * jnp.exp(-0.5 * v * v) * inverse_root_tau


SIZES = ((24, 128, F32), (24, 1152, BF), (24, 384, BF), (24, 1536, BF), (96, 384, BF))
WINDOWS = (
    [((0, 48), (0, 128))],
    [((0, 48), (384 * j, 384)) for j in range(3)],
    [((0, 48), (0, 384))],
    [((0, 48), (384 * j, 384)) for j in range(4)],
    [((48 * j, 48), (0, 384)) for j in range(4)],
)
SCRATCH = {
    "got": [((rd, n2), dt) for rd, n2, dt in SIZES]
    + [((24, 2304), BF), ((24, 768), BF), ((24, 3072), BF), ((96, 384), BF)],
    "w": [((2, 4, 4, 2 * rd, n2), dt) for rd, n2, dt in SIZES],
    "fin": [((2 * rd, n2), F32) for rd, n2, dt in SIZES],
    "fin2": [((rd, n2), F32) for rd, n2, dt in SIZES],
    "rc": [((4, 4, 2 * rd, n2), dt) for rd, n2, dt in SIZES if n2 not in (1152, 384) or rd == 96],
    "r1": [((2, 4, 2 * rd, n2), dt) for rd, n2, dt in SIZES],
    "r2": [((4, 2 * rd, n2), dt) for rd, n2, dt in SIZES],
    "r3": [((3, 2 * rd, n2), dt) for rd, n2, dt in SIZES],
    "stage": [((4, 48, 3456), BF), ((4, 192, 384), BF)],
    "dpu": [((2, 4, 4, 48, 768), BF)],
    "do": [((2, 256, 384), BF)],
    "dd": [((2, 4, 192, 384), BF)],
    "tmask": [((4, 128), F32)],
    "dmask": [((1, 32), F32)],
    "vec": [((16, 768), F32)],
    "table": [((16, 2, 768), F32)],
    "pr": [((512, 2304), BF)],
    "ctx": [((512, 768), BF)],
    "sh": [((24, 256, 128), BF)],
    "n1": [((512, 768), BF)],
    "n2": [((512, 768), BF)],
    "inv": [((512, 2), F32)],
    "fl": [((512, 768), BF)],
    "act": [((512, 3072), BF)],
    "gp": [((512, 3072), BF)],
    "row": [((512, 768), F32)],
    "low": [((512, 768), BF)],
    "ob": [((512, 768), BF)],
    "src": [((2, 2, 768), F32)] * 2,
    "slots": [((16, 2, 768), F32)] * 4,
    "sdr": [((2, 4, 2, 768), F32)],
    "pairs": [((2, 2, 768), F32)] * 2,
    "soo": [((2, 768), F32)],
    "mat": [((32, 768), F32)],
    "ars": [((3, 32, 768), BF)],
    "gpc": [((64, 3072), BF)],
    "arb": [((3, 3, 32, 768), BF)],
    "fq": [((2, 4, 4, 32, 1280), BF)],
    "fz": [((2, 4, 32, 1536), BF)],
    "vg": [((128, 768), F32)],
    "flip": [((768, 128), F32)],
}
SEMS = {
    "gr0": (6,),
    "gr1": (16,),
    "gr2": (6,),
    "gr3": (21,),
    "gr4": (21,),
    "dr": (25,),
    "ls": (4,),
    "rr0": (7,),
    "rr1": (19,),
    "rr2": (7,),
    "rr3": (25,),
    "rr4": (25,),
    "xr": (9,),
    "fr": (15,),
    "er": (9,),
    "ss": (14,),
    "os": (11,),
    "ins": (12,),
}
INS = ("tok", "cot", "counts", "small", "sp", "so", "su", "sd", "dp", "dout", "du", "ddown")
OUTS = (
    ("out", (512, 768), BF),
    ("gin", (512, 768), F32),
    ("gsmall", (24, 256), F32),
    ("gsp", (24, 2304), F32),
    ("gso", (24, 768), F32),
    ("gsu", (24, 3072), F32),
    ("gsd", (96, 768), F32),
    ("gdp", (24, 2304), F32),
    ("gdo", (24, 768), F32),
    ("gdu", (24, 3072), F32),
    ("gdd", (96, 768), F32),
)


class Box:
    def put(self, name, ref):
        at = [out[0] for out in OUTS].index(name)
        d = pltpu.make_async_copy(ref, self.back[name], self.os.at[at])
        d.start()
        self.flying[name] = d

    def ready(self, *names):
        for name in names:
            self.coming[name].wait()


def kernel(*refs):
    b = Box()
    refs = list(refs)

    def take(n):
        got, refs[:n] = refs[:n], []
        return got

    b.far = {name: take(1)[0] for name in INS}
    b.back = {name: take(1)[0] for name, _, _ in OUTS}
    for name in INS:
        setattr(b, name, take(1)[0])
    for name, _, _ in OUTS[2:]:
        setattr(b, name, take(1)[0])
    for name, items in SCRATCH.items():
        got = take(len(items))
        setattr(b, name, got if len(got) > 1 else got[0])
    for name in SEMS:
        setattr(b, name, take(1)[0])
    b.credit, b.met, b.met2 = take(3)
    b.t = Spot()
    run(b)


FACTOR_WINDOWS = [((0, 32), (0, 512)), ((0, 32), (512, 384)), ((0, 32), (896, 384))]
LINE_WINDOWS = [(0, 768), (768, 384), (1152, 384)]


def run(b):
    t = b.t
    b.x = Sender(t, b.ss.at[0], b.xr)
    b.flying, b.coming = {}, {}
    for i, name in enumerate(INS):
        d = pltpu.make_async_copy(b.far[name], getattr(b, name), b.ins.at[i])
        d.start()
        b.coming[name] = d
    b.do[...] = jnp.zeros(b.do.shape, BF)
    b.vg[...] = jnp.zeros(b.vg.shape, F32)
    enter(t)
    pass_on(t, b.met)
    shards = (b.small, b.sp, b.so, b.su, b.sd)
    far = [b.far[name] for name in ("small", "sp", "so", "su", "sd")]
    gs = [
        Gather(t, far[i], shards[i], b.w[i], b.got[i], b.fin[i], WINDOWS[i], b.ss.at[1 + i], getattr(b, f"gr{i}"))
        for i in range(5)
    ]
    dg = DocGather(
        t,
        [b.far[name] for name in ("dp", "dout", "du", "ddown")],
        (b.dp, b.dout, b.du, b.ddown),
        b.stage,
        b.got[5:],
        (b.fin[1], b.fin[4]),
        b.dpu,
        b.do,
        b.dd,
        b.ss.at[6],
        b.dr,
        b.ls,
    )
    for g in gs:
        g.pair()
    dg.pair()
    b.f = Gather(t, None, None, b.fq, None, None, FACTOR_WINDOWS, b.ss.at[7], b.fr)
    b.e = LineGather(t, b.fz, LINE_WINDOWS, b.ss.at[8], b.er)

    events = [(g, k) for g in gs for k in range(len(g.windows))]
    lines = events + [(dg, k) for k in range(7)]
    clock, spreads, relays = [0], [0], [0]

    def do(name, at, among=events):
        if 0 <= at < len(among):
            getattr(among[at][0], name)(among[at][1])

    def relay(n):
        for _ in range(n):
            do("relay", relays[0], lines)
            relays[0] += 1
            do("spread", spreads[0], lines)
            spreads[0] += 1

    def tick(upto):
        while clock[0] <= upto:
            at = clock[0]
            busy = relays[0] < len(events)
            do("first", at)
            relay(1)
            do("second", at - 2)
            if busy:
                relay(1)
            do("third", at - 4)
            do("finish", at - 5)
            clock[0] += 1

    b.ready("small", "sp")
    gs[0].join()
    gs[1].join()
    for i in range(3):
        do("spread", i, lines)
    spreads[0] = 3
    b.ready("so", "su", "sd")
    for g in gs[2:]:
        g.join()
    pl.semaphore_wait(b.met, 4)
    pass_on(t, b.met2)
    relay(1)
    tick(0)
    b.ready("dp", "dout", "du", "ddown")
    dg.join()
    dg.ranks()
    tick(1)
    pl.semaphore_wait(b.met2, 4)
    b.ready("cot", "tok", "counts")
    masks_in(b)
    send_cotangents(b)
    tick(5)
    vectors_in(b)
    tick(8)
    segment_project(b)
    tick(9)
    for seg in range(4):
        attend(b, seg)
        tick(10 + seg // 2)
    segment_mix(b)
    for j in range(4):
        segment_up(b, j)
        if j < 3:
            tick(12 + j)
    for k in range(7):
        dg.plane(k)
    tick(17)
    send_summaries(b, summary_rows(b))
    steps = document(b)
    down = segment_down(b)
    next(down)
    dg.share()
    for g in gs:
        g.drain()
    for i in range(3):
        dg.finish(i)
    dg.drain()
    next(steps)
    next(down, None)
    next(steps)
    second_back(b)
    next(steps)
    hidden_back(b)
    next(steps)
    next(steps)
    first_back(b)
    next(steps, None)
    finish_output(b)
    b.f.spread(2)
    b.e.spread(2)

    small_rc, up_rc, down_rc = b.rc
    rcs = (small_rc, up_rc.at[:, :, :, 0:1152], up_rc.at[:, :, :, 1152:1536], up_rc, down_rc)
    rs = [
        Reduce(
            t,
            b.w[i],
            rcs[i],
            b.r1[i],
            b.r2[i],
            b.r3[i],
            b.fin[i],
            b.fin2[i],
            out,
            WINDOWS[i],
            b.ss.at[9 + i],
            getattr(b, f"rr{i}"),
        )
        for i, out in enumerate((b.gsmall, b.gsp, b.gso, b.gsu, b.gsd))
    ]
    for r, name in zip(rs, ("gsmall", "gsp", "gso", "gsu", "gsd")):
        r.name = name
    rsmall, rproject, routput, rup, rdown = rs
    terms = [(r, k) for r in (rdown, rup, routput, rproject, rsmall) for k in range(len(r.windows))]
    clock[0] = 0

    ends = {id(r): max(i for i, e in enumerate(terms) if e[0] is r) for r in rs}

    def tock(upto):
        while clock[0] <= upto:
            at = clock[0]
            do("first", at, terms)
            do("second", at - 2, terms)
            do("third", at - 4, terms)
            do("fourth", at - 6, terms)
            for r in rs:
                if ends[id(r)] == at - 7:
                    r.fifth()
                    b.put(r.name, r.out)
            clock[0] += 1

    second_back_rows(b)
    hidden_back_rows(b)
    b.f.relay(2)
    b.e.relay(2)
    b.f.second(1)
    b.f.third(0)
    down_terms(b, rdown)
    first_back_rows(b)
    b.f.first(2)
    b.e.first(2)
    b.f.third(1)
    tock(0)
    column_terms(b, rup, b.fl, b.gp)
    tock(1)
    b.f.second(2)
    mixed_back(b)
    tock(2)
    context_back(b)
    tock(3)
    b.f.third(2)
    attend_back(b, 0)
    tock(4)
    attend_back(b, 1)
    tock(5)
    attend_back(b, 2)
    tock(6)
    attend_back(b, 3)
    tock(7)
    pl.semaphore_signal(b.credit, inc=1, device_id=t.sib, device_id_type=MESH)
    pl.semaphore_wait(b.credit, 1)
    column_terms(b, routput, b.ctx, b.low)
    input_back(b)
    column_terms(b, rproject, b.tok, b.pr)
    tock(8)
    vectors_out(b)
    rsmall.pair(0)
    tock(10)
    document_terms(b)
    tock(len(terms) + 6)
    for r in rs:
        r.drain()
    b.x.drain()
    for d in b.flying.values():
        d.wait()


def send_cotangents(b):
    for m in range(2):
        for s in range(2):
            rows = b.cot[pl.ds(128 * (2 * m + s), 16), :].astype(F32)
            b.src[0][m, s : s + 1, :] = rows[0:1]
    send_rows(b, 0)


def send_rows(b, n):
    t, src, slots = b.t, b.src[n], b.slots[n]
    mine = src.at[t.half]
    other = src.at[1 - t.half]
    for k in (1, 2, 3):
        b.x.send(n, mine, slots.at[t.i], t.plane[k])
    for k in (0, 1, 2, 3):
        b.x.send(n, mine, slots.at[t.i], (4 * t.z + t.qq[k], t.o))
        b.x.send(n, other, slots.at[t.i], (4 * t.zo + t.qq[k], t.c))
        b.x.send(n, other, slots.at[t.i], (4 * t.zo + t.qq[k], t.o))
    slots[t.i] = src[t.half]


def take_rows(b, n):
    slots = b.slots[n]
    b.x.arrived(n, slots.at[pl.ds(0, 15)])
    for i in range(16):
        b.mat[2 * i : 2 * i + 2, :] = slots[i]
    return b.mat[...]


def vectors_in(b):
    small = b.w[0]
    b.vec[...] = jnp.transpose(small[0].reshape(768, 128))[0:16]
    table = jnp.transpose(small[1].reshape(768, 128))[0:32]
    for i in range(16):
        b.table[i] = table[2 * i : 2 * i + 2]


def masks_in(b):
    t = b.t
    rows = [b.counts[m : m + 1, :].astype(F32) for m in range(2)]
    lane = lax.broadcasted_iota(jnp.int32, (1, 64), 1)
    slot = lax.broadcasted_iota(jnp.int32, (1, 128), 1)
    for m in range(2):
        for s in range(2):
            own = jnp.sum(jnp.where(lane == 2 * t.dev + s, rows[m], 0.0), axis=1, keepdims=True)
            keep = (slot.astype(F32) < own) | (slot == 0)
            b.tmask[2 * m + s : 2 * m + s + 1, :] = jnp.where(keep, 1.0, 0.0)
    row = jnp.where(t.half == 0, rows[0], rows[1])
    row = jnp.where(lax.div(t.z, 2) == 0, row[:, 0:32], row[:, 32:64])
    b.dmask[...] = jnp.where(row > 0.0, 1.0, 0.0)


def vec(b, i):
    return b.vec[i : i + 1, :]


def segment_project(b):
    w = b.w[1]

    @pl.loop(0, 6)
    def _(i):
        h, j = lax.div(i, 3), lax.rem(i, 3)
        part = w[h, :, :, :, off(j, 384)].reshape(768, 384)
        b.pr[:, off(i, 384)] = dot(b.tok[...], part).astype(BF)


def lane_masks():
    lane = lax.broadcasted_iota(jnp.int32, (1, 128), 1)
    low = (lane < 64).astype(F32)
    return low.astype(BF), (1.0 - low).astype(BF)


def attend(b, seg):
    low, high = lane_masks()
    keep = b.tmask[seg : seg + 1, :] > 0.0
    rows = pl.ds(128 * seg, 128)

    lane = lax.broadcasted_iota(jnp.int32, (128, 128), 1)

    @pl.loop(0, 3)
    def _(i):
        pairs = (2 * i, 2 * i + 1)
        loaded = [[b.pr[rows, off(p + 6 * g, 128)] for g in range(3)] for p in pairs]
        stacked = [jnp.concatenate((q2 * low, q2 * high), axis=0) for q2, _, _ in loaded]
        scores = [
            jnp.where(keep, dot_rt(qs, k2) * 0.125, floor_score)
            for qs, (_, k2, _) in zip(stacked, loaded)
        ]
        raised = [jnp.exp(v - jnp.max(v, axis=-1, keepdims=True)) for v in scores]
        shares = [(v * (1.0 / jnp.sum(v, axis=-1, keepdims=True))).astype(BF) for v in raised]
        both = [dot(v, v2) for v, (_, _, v2) in zip(shares, loaded)]
        for p, share, two in zip(pairs, shares, both):
            b.sh[6 * seg + p] = share
            b.ctx[rows, off(p, 128)] = jnp.where(lane < 64, two[:128], two[128:]).astype(BF)


def segment_mix(b):
    w = b.w[2]
    for r in range(2):
        rows = pl.ds(256 * r, 256)
        for h in range(2):
            b.row[rows, pl.ds(384 * h, 384)] = dot(b.ctx[rows, :], w[h].reshape(768, 384))
    scale, offset = vec(b, 0), vec(b, 1)

    @pl.loop(0, 16)
    def _(i):
        rows = off(i, 32, 32)
        n, inverse = normed(b.tok[rows, :].astype(F32) + b.row[rows, :])
        first = n * scale + offset
        b.n1[rows, :] = n.astype(BF)
        b.inv[rows, 0:1] = inverse
        b.row[rows, :] = first
        b.fl[rows, :] = first.astype(BF)


def segment_up(b, j):
    w = b.w[3]
    hid = b.fin[4]
    for h, r in [(h, r) for h in range(2) for r in range(4)]:
        up = w[h, :, :, :, pl.ds(384 * j, 384)].reshape(768, 384)
        hid[0:128, :] = dot(b.fl[128 * r : 128 * r + 128, :], up)
        cols = pl.ds(1536 * h + 384 * j, 384)

        @pl.loop(0, 4)
        def _(i):
            rows = off(i + 4 * r, 32, 32)
            value, slope = gelu_pair(hid[off(i, 32, 32), :])
            b.act[rows, cols] = value.astype(BF)
            b.gp[rows, cols] = slope.astype(BF)


def summary_rows(b):
    w = b.w[4]
    for s in range(4):
        b.gpc[16 * s : 16 * s + 16, :] = b.act[128 * s : 128 * s + 16, :]
    parts = [dot(b.gpc[...], w[h].reshape(3072, 384)) for h in range(2)]
    both = jnp.concatenate(parts, axis=1)
    for s in range(4):
        b.gpc[16 * s : 16 * s + 16, :] = b.gp[128 * s : 128 * s + 16, :]
    rows = []
    for s in range(4):
        n, _ = normed(b.row[128 * s : 128 * s + 8, :] + both[16 * s : 16 * s + 8])
        rows.append((n * vec(b, 2) + vec(b, 3))[0:1])
    return rows


def thirds(w, depth):
    middle = jnp.concatenate((w[0, :, :, :, 256:384], w[1, :, :, :, 0:128]), axis=-1)
    for part in (w[0, :, :, :, 0:256], middle, w[1, :, :, :, 128:384]):
        yield part.reshape(depth, 256)


def side_by_side(a, c, rows):
    return jnp.concatenate((a.reshape(rows, 384), c.reshape(rows, 384)), axis=1)


def segment_down(b):
    for i, part in enumerate(thirds(b.w[4], 3072)):
        cols = slice(256 * i, 256 * i + 256)
        b.row[:, cols] += dot(b.act[...], part)
        if i == 1:
            yield

    gain, shift = vec(b, 2), vec(b, 3)

    @pl.loop(0, 16, unroll=2)
    def _(i):
        rows = off(i, 32, 32)
        n, inverse = normed(b.row[rows, :])
        b.n2[rows, :] = n.astype(BF)
        b.inv[rows, 1:2] = inverse
        b.ob[rows, :] = (n * gain + shift).astype(BF)


def send_summaries(b, rows):
    places = b.table[b.t.i]
    for m in range(2):
        for s in range(2):
            b.src[1][m, s : s + 1, :] = rows[2 * m + s] + places[s : s + 1]
    send_rows(b, 1)


def plane_send(b, n, partial):
    b.ars[n] = partial.astype(BF)
    for k in (1, 2, 3):
        b.x.send(2 + n, b.ars.at[n], b.arb.at[n, k - 1], b.t.plane[k])


def plane_take(b, n):
    b.x.arrived(2 + n, b.arb.at[n])
    total = b.ars[n].astype(F32)
    for k in range(3):
        total = total + b.arb[n, k].astype(F32)
    return total


def document(b):
    t = b.t
    dp = b.dpu[0].reshape(768, 768)
    du = b.dpu[1].reshape(768, 768)
    lane = lax.broadcasted_iota(jnp.int32, (1, 256), 1)
    heads = [((lane >= 64 * h) & (lane < 64 * h + 64)).astype(F32).astype(BF) for h in range(3)]
    keep = b.dmask[...] > 0.0
    h_in = take_rows(b, 1)
    h_low = h_in.astype(BF)
    pr = dot(h_low, dp).astype(BF)
    q3, k3, v3 = pr[:, 0:256], pr[:, 256:512], pr[:, 512:768]
    qs = jnp.concatenate([q3 * m for m in heads], axis=0)
    scores = jnp.where(keep, dot_rt(qs, k3) * 0.125, floor_score)
    raised = jnp.exp(scores - jnp.max(scores, axis=-1, keepdims=True))
    shares = raised * (1.0 / jnp.sum(raised, axis=-1, keepdims=True))
    shares_low = shares.astype(BF)
    three = dot(shares_low, v3)
    ctx = sum(three[32 * h : 32 * h + 32] * heads[h].astype(F32) for h in range(3)).astype(BF)
    mixed = jnp.concatenate([dot(ctx, b.do[h]) for h in range(2)], axis=1)
    plane_send(b, 0, mixed)
    yield
    n1, i1 = normed(h_in + plane_take(b, 0))
    first = n1 * vec(b, 4) + vec(b, 5)
    first_low = first.astype(BF)
    active, slope = gelu_pair(dot(first_low, du))
    active = active.astype(BF)
    branch = jnp.concatenate([dot(active, b.dd[h].reshape(768, 384)) for h in range(2)], axis=1)
    plane_send(b, 1, branch)

    @pl.when(t.c == 0)
    def _():
        b.fq[0, t.z, t.q, :, 0:512] = active[:, 0:512]
        b.fz[0, t.z, :, 0:768] = h_low

    @pl.when(t.c == 1)
    def _():
        b.fq[1, t.z, t.q, :, 0:256] = active[:, 512:768]
        b.fq[1, t.z, t.q, :, 256:512] = ctx
        b.fz[1, t.z, :, 0:768] = first_low

    b.f.spread(0)
    b.e.spread(0)
    yield
    n2, i2 = normed(first + plane_take(b, 1))
    out = n2 * vec(b, 6) + vec(b, 7)
    g = take_rows(b, 0)
    delta = norm_back(g, n2, i2, vec(b, 6))
    branch_low = delta.astype(BF)
    back = sum(dot_rt(branch_low[:, 384 * h : 384 * h + 384], b.dd[h].reshape(768, 384)) for h in range(2))
    hidden_delta = (back * slope).astype(BF)
    plane_send(b, 2, dot_rt(hidden_delta, du))
    b.vg[6:7, :] = jnp.sum(g * n2, axis=0, keepdims=True) * 0.125
    b.vg[7:8, :] = jnp.sum(g, axis=0, keepdims=True) * 0.125
    for i in range(16):
        b.slots[2][i] = out[2 * i : 2 * i + 2]
    other_i = 8 * (1 - t.half) + 2 * t.q + t.c
    b.x.send(6, b.slots[2].at[other_i], b.soo, (4 * t.zo + t.q, t.c))

    def halves(ref, at, value):
        for h in range(2):

            @pl.when(t.c == h)
            def _():
                ref[(h,) + at] = value[:, 384 * h : 384 * h + 384]

    halves(b.fq, (t.z, t.q, slice(None), slice(512, 896)), hidden_delta)
    halves(b.fz, (t.z, slice(None), slice(768, 1152)), branch_low)
    b.f.relay(0)
    b.e.relay(0)
    b.f.spread(1)
    b.e.spread(1)
    yield
    first_delta = delta + plane_take(b, 2)
    mixed_delta = norm_back(first_delta, n1, i1, vec(b, 4))
    mixed_low = mixed_delta.astype(BF)
    ctx_delta = sum(dot_rt(mixed_low[:, 384 * h : 384 * h + 384], b.do[h]) for h in range(2)).astype(BF)
    cs = jnp.concatenate([ctx_delta * m for m in heads], axis=0)
    shares_delta = dot_rt(cs, v3)
    inner = jnp.sum(shares_delta * shares, axis=-1, keepdims=True)
    scores_delta = (shares * (shares_delta - inner)).astype(BF)
    dq3 = dot(scores_delta, k3) * 0.125
    dq = sum(dq3[32 * h : 32 * h + 32] * heads[h].astype(F32) for h in range(3))
    dk = dot_lt(scores_delta, qs) * 0.125
    dv = dot_lt(shares_low, cs)
    pd = jnp.concatenate((dq, dk, dv), axis=1).astype(BF)
    h_delta = dot_rt(pd, dp) + 0.25 * mixed_delta
    for i in range(16):
        b.slots[3][i] = h_delta[2 * i : 2 * i + 2]
    for k in (0, 1, 2, 3):
        if k:
            b.x.send(7, b.slots[3].at[8 * t.half + 2 * t.qq[k] + t.c], b.sdr.at[0, k], t.plane[k])
        b.x.send(
            8, b.slots[3].at[8 * (1 - t.half) + 2 * t.qq[k] + t.c], b.sdr.at[1, k], (4 * t.zo + t.qq[k], t.c)
        )
    b.sdr[0, 0] = b.slots[3][t.i]
    b.vg[4:5, :] = jnp.sum(first_delta * n1, axis=0, keepdims=True) * 0.125
    b.vg[5:6, :] = jnp.sum(first_delta, axis=0, keepdims=True) * 0.125
    halves(b.fq, (t.z, t.q, slice(None), slice(896, 1280)), pd)
    halves(b.fz, (t.z, slice(None), slice(1152, 1536)), mixed_low)
    b.f.relay(1)
    b.e.relay(1)
    b.f.first(0)
    b.e.first(0)
    yield
    b.f.second(0)
    b.x.arrived(6, b.soo)
    b.pairs[0][t.half] = b.slots[2][t.i]
    b.pairs[0][1 - t.half] = b.soo[...]
    yield
    b.x.arrived(7, b.sdr.at[0, pl.ds(0, 3)])
    b.x.arrived(8, b.sdr.at[1])
    b.pairs[1][t.half] = b.sdr[0, 0] + b.sdr[0, 1] + b.sdr[0, 2] + b.sdr[0, 3]
    b.pairs[1][1 - t.half] = b.sdr[1, 0] + b.sdr[1, 1] + b.sdr[1, 2] + b.sdr[1, 3]
    b.f.first(1)
    b.e.first(1)


def finish_output(b):
    first_row = lax.broadcasted_iota(jnp.int32, (16, 768), 0) == 0
    for m in range(2):
        for s in range(2):
            rows = pl.ds(128 * (2 * m + s), 16)
            fresh = jnp.where(first_row, b.pairs[0][m, s : s + 1, :], b.ob[rows, :].astype(F32))
            b.ob[rows, :] = fresh.astype(BF)
    b.put("out", b.ob)


def second_back(b):
    gain = vec(b, 2)

    def body(i, carry):
        gains, shifts = carry
        rows = off(i, 16, 16)
        late = (lax.broadcasted_iota(jnp.int32, (16, 768), 0) + 16 * lax.rem(i, 8)) == 0
        g = jnp.where(late, 0.0, b.cot[rows, :].astype(F32))
        n = b.n2[rows, :].astype(F32)
        delta = norm_back(g, n, b.inv[rows, 1:2], gain)
        b.row[rows, :] = delta
        b.low[rows, :] = delta.astype(BF)
        return gains + g * n, shifts + g

    zero = jnp.zeros((16, 768), F32)
    gains, shifts = lax.fori_loop(0, 32, body, (zero, zero), unroll=2)
    b.vg[2:3, :] = jnp.sum(gains, axis=0, keepdims=True)
    b.vg[3:4, :] = jnp.sum(shifts, axis=0, keepdims=True)


def second_back_rows(b):
    gain = vec(b, 2)
    top = lax.broadcasted_iota(jnp.int32, (16, 768), 0) == 0
    gains, shifts = b.vg[2:3, :], b.vg[3:4, :]
    for s in range(4):
        rows = slice(128 * s, 128 * s + 16)
        g = b.pairs[1][s // 2, s % 2 : s % 2 + 1, :]
        n = b.n2[rows, :].astype(F32)
        delta = norm_back(jnp.where(top, g, 0.0), n, b.inv[rows, 1:2], gain)
        b.row[rows, :] = jnp.where(top, delta, b.row[rows, :])
        low = jnp.where(top, delta, b.low[rows, :].astype(F32)).astype(BF)
        b.low[rows, :] = low
        gains += g * n[0:1]
        shifts += g
    b.vg[2:3, :] = gains
    b.vg[3:4, :] = shifts


def hidden_back_rows(b):
    w = b.w[4]

    @pl.loop(0, 4)
    def _(z):
        cols = off(z, 768)
        low = jnp.concatenate([b.low[128 * s : 128 * s + 16, :] for s in range(4)], axis=0)
        back = dot_rt(low, side_by_side(w[0, z], w[1, z], 768))
        delta = (back * b.gpc[:, cols].astype(F32)).astype(BF)
        b.gpc[:, cols] = delta
        for s in range(4):
            b.gp[pl.ds(128 * s, 16), cols] = delta[16 * s : 16 * s + 16]


def first_back_rows(b):
    w = b.w[3]
    top = lax.broadcasted_iota(jnp.int32, (16, 768), 0) == 0
    more = dot_rt(b.gpc[:, 0:1536], w[0].reshape(768, 1536)) + dot_rt(
        b.gpc[:, 1536:3072], w[1].reshape(768, 1536)
    )
    for s in range(4):
        rows = slice(128 * s, 128 * s + 16)
        b.row[rows, :] += jnp.where(top, more[16 * s : 16 * s + 16], 0.0)


def hidden_back(b):
    w = b.w[4]

    @pl.loop(0, 4)
    def _(z):
        cols = off(z, 768)
        for r in range(2):
            rows = pl.ds(256 * r, 256)
            back = dot_rt(b.low[rows, :], side_by_side(w[0, z], w[1, z], 768))
            b.gp[rows, cols] = (back * b.gp[rows, cols].astype(F32)).astype(BF)


def down_terms(b, r):
    t, w = b.t, b.w[4]
    for h in (t.o, t.c):
        for z in range(4):
            part = dot_lt(b.act[:, 768 * z : 768 * z + 768], b.low[:, off(h, 384)])
            w[h, z] = part.astype(BF).reshape(4, 192, 384)
            if h is t.o:
                r.pair_rows(z)


def first_back(b):
    w = b.w[3]

    @pl.loop(0, 2)
    def _(r):
        rows = off(r, 256, 256)
        for h in range(2):
            b.row[rows, :] += dot_rt(b.gp[rows, 1536 * h : 1536 * h + 1536], w[h].reshape(768, 1536))


def mixed_back(b):
    scale = vec(b, 0)

    def body(i, carry):
        scales, offsets = carry
        rows = off(i, 16, 16)
        g = b.row[rows, :]
        n = b.n1[rows, :].astype(F32)
        delta = norm_back(g, n, b.inv[rows, 0:1], scale)
        b.row[rows, :] = delta
        b.low[rows, :] = delta.astype(BF)
        return scales + g * n, offsets + g

    zero = jnp.zeros((16, 768), F32)
    scales, offsets = lax.fori_loop(0, 32, body, (zero, zero), unroll=2)
    b.vg[0:1, :] = jnp.sum(scales, axis=0, keepdims=True)
    b.vg[1:2, :] = jnp.sum(offsets, axis=0, keepdims=True)


def context_back(b):
    w = b.w[2]
    b.flying.pop("out").wait()
    for r in range(2):
        rows = pl.ds(256 * r, 256)
        back = dot_rt(b.low[rows, :], side_by_side(w[0], w[1], 768))
        b.ob[rows, :] = back.astype(BF)


def attend_back(b, seg):
    low, high = lane_masks()
    rows = pl.ds(128 * seg, 128)

    lane = lax.broadcasted_iota(jnp.int32, (128, 128), 1)

    @pl.loop(0, 3)
    def _(i):
        pairs = (2 * i, 2 * i + 1)
        loaded = [[b.pr[rows, off(p + 6 * g, 128)] for g in range(3)] for p in pairs]
        deltas = [b.ob[rows, off(p, 128)] for p in pairs]
        shares = [b.sh[6 * seg + p] for p in pairs]
        stacked = [jnp.concatenate((q2 * low, q2 * high), axis=0) for q2, _, _ in loaded]
        cs = [jnp.concatenate((d2 * low, d2 * high), axis=0) for d2 in deltas]
        back = [dot_rt(c, v2) for c, (_, _, v2) in zip(cs, loaded)]
        wide = [v.astype(F32) for v in shares]
        inner = [jnp.sum(d * v, axis=-1, keepdims=True) for d, v in zip(back, wide)]
        ds = [(v * (d - n)).astype(BF) for v, d, n in zip(wide, back, inner)]
        dq = [dot(d, k2) * 0.125 for d, (_, k2, _) in zip(ds, loaded)]
        dk = [dot_lt(d, qs) * 0.125 for d, qs in zip(ds, stacked)]
        dv = [dot_lt(v, c) for v, c in zip(shares, cs)]
        for j, p in enumerate(pairs):
            b.pr[rows, off(p, 128)] = jnp.where(lane < 64, dq[j][:128], dq[j][128:]).astype(BF)
            b.pr[rows, off(p + 6, 128)] = dk[j].astype(BF)
            b.pr[rows, off(p + 12, 128)] = dv[j].astype(BF)


def input_back(b):
    w = b.w[1]

    @pl.loop(0, 2)
    def _(r):
        rows = off(r, 256, 256)
        for h in range(2):
            b.row[rows, :] += dot_rt(b.pr[rows, 1152 * h : 1152 * h + 1152], w[h].reshape(768, 1152))

    b.put("gin", b.row)


def column_terms(b, r, left, right):
    t, w = b.t, r.w
    n = len(r.windows)
    for h in (t.o, t.c):
        for j in range(n):
            part = dot_lt(left[...], right[:, off(n * h + j, 384)])
            w[h, :, :, :, pl.ds(384 * j, 384)] = part.astype(BF).reshape(4, 4, 48, 384)
            if h is t.o:
                r.pair(j)


def vectors_out(b):
    t, w = b.t, b.w[0]
    w[0] = jnp.transpose(b.vg[...]).reshape(4, 4, 48, 128)
    row = lax.broadcasted_iota(jnp.int32, (32, 768), 0)
    both = b.pairs[1][0] + b.pairs[1][1]
    places = jnp.where(row == 2 * t.i, both[0:1], 0.0) + jnp.where(row == 2 * t.i + 1, both[1:2], 0.0)
    b.vg[0:32, :] = places
    w[1] = jnp.transpose(b.vg[...]).reshape(4, 4, 48, 128)


def document_terms(b):
    t = b.t
    for k in range(3):
        b.f.finish(k)
        b.e.finish(k)
    b.f.drain()
    b.e.drain()
    own = 24 * t.dev
    part = 24 * lax.rem(t.dev, 8)
    fq, fz = b.fq, b.fz

    def rows_of(value, at, size):
        n = value.shape[1]
        b.flip[0:n, :] = jnp.transpose(value.astype(F32))
        return b.flip[pl.ds(pl.multiple_of(at, 8), size), :].astype(BF)

    def line(a):
        both = [fz[h, :, :, a : a + 384].reshape(128, 384) for h in range(2)]
        return jnp.concatenate(both, axis=1)

    def rank(q, a):
        both = [fq[h, :, q, :, a : a + 384].reshape(128, 384) for h in range(2)]
        return jnp.concatenate(both, axis=1)

    left = rows_of(fz[0, :, :, 0:768].reshape(128, 768), own, 24)
    for q in range(4):
        part_q = dot(left, rank(q, 896))
        for g in range(3):
            b.gdp[:, 768 * g + 192 * q : 768 * g + 192 * q + 192] = part_q[:, 256 * g : 256 * g + 192]
    left = rows_of(fq[1, :, t.z, :, 256:512].reshape(128, 256), part, 24)
    b.gdo[...] = dot(left, line(1152))
    left = rows_of(fz[1, :, :, 0:768].reshape(128, 768), own, 24)
    for q in range(4):
        b.gdu[:, 768 * q : 768 * q + 768] = dot(left, rank(q, 512))
    active = jnp.concatenate((fq[0, :, t.z, :, 0:512], fq[1, :, t.z, :, 0:256]), axis=-1)
    left = rows_of(active.reshape(128, 768), 4 * part, 96)
    b.gdd[...] = dot(left, line(768))
    for name in ("gdp", "gdo", "gdu", "gdd"):
        b.put(name, getattr(b, name))


def mega(*arrays):
    an = pl.BlockSpec(memory_space=pl.ANY)
    return pl.pallas_call(
        kernel,
        out_shape=[jax.ShapeDtypeStruct(shape, dt) for _, shape, dt in OUTS],
        in_specs=[an] * len(INS),
        out_specs=[an] * len(OUTS),
        scratch_shapes=[pltpu.VMEM(item.shape, item.dtype) for item in arrays]
        + [pltpu.VMEM(shape, dt) for _, shape, dt in OUTS[2:]]
        + [pltpu.VMEM(shape, dt) for items in SCRATCH.values() for shape, dt in items]
        + [pltpu.SemaphoreType.DMA(shape) for shape in SEMS.values()]
        + [pltpu.SemaphoreType.REGULAR] * 3,
        compiler_params=pltpu.CompilerParams(
            collective_id=1, has_side_effects=True, vmem_limit_bytes=65440 * 1024
        ),
    )(*arrays)


def hand_on_kernel(*refs):
    n = (len(refs) - 2) // 3
    src, dst, mid = refs[:n], refs[n : 2 * n], refs[2 * n : 3 * n]
    ins = [pltpu.make_async_copy(src[i], mid[i], refs[-2].at[i]) for i in range(n)]
    outs = [pltpu.make_async_copy(mid[i], dst[i], refs[-1].at[i]) for i in range(n)]
    for d in ins:
        d.start()
    for i in range(n):
        ins[i].wait()
        outs[i].start()
    for d in outs:
        d.wait()


def hand_on(*arrays):
    an = pl.BlockSpec(memory_space=pl.ANY)
    n = len(arrays)
    return pl.pallas_call(
        hand_on_kernel,
        out_shape=[jax.ShapeDtypeStruct(item.shape, item.dtype) for item in arrays],
        in_specs=[an] * n,
        out_specs=[an] * n,
        scratch_shapes=[pltpu.VMEM(item.shape, item.dtype) for item in arrays]
        + [pltpu.SemaphoreType.DMA((n,))] * 2,
        compiler_params=pltpu.CompilerParams(vmem_limit_bytes=63 * 2**20),
    )(*arrays)


def local_fast(tokens, token_counts, *rest):
    weights, cotangent = rest[:17], rest[17]
    width = tokens.shape[-1]
    rows = weights[0].shape[0]
    lane = jnp.arange(256)[None]
    small = jnp.pad(weights[16], ((0, 0), (128, 96)))
    for at, i in enumerate((4, 5, 6, 7, 12, 13, 14, 15)):
        small = jnp.where(lane == at, weights[i][:, None], small)
    small = small.astype(F32)
    outs = mega(
        tokens.reshape(-1, width),
        cotangent.reshape(-1, width),
        token_counts,
        small,
        *weights[:4],
        *weights[8:12],
    )
    gsmall = outs[2]
    out, gin, gsp, gso, gsu, gsd, gdp, gdo, gdu, gdd = hand_on(*outs[:2], *outs[3:])
    return (
        (out.reshape(tokens.shape), gin.reshape(tokens.shape), gsp, gso, gsu, gsd)
        + tuple(gsmall[:, i] for i in range(4))
        + (gdp, gdo, gdu, gdd)
        + tuple(gsmall[:, i] for i in range(4, 8))
        + (gsmall[:, 128:160],)
    )


def partner_2(value, axis, distance):
    mask = 2**distance
    pairs = [(source, source ^ mask) for source in range(lax.axis_size(axis))]
    return lax.ppermute(value, axis, pairs)


def product(left, right):
    return jnp.dot(left, right, preferred_element_type=jnp.float32)


def left_product(left, right):
    return lax.dot_general(
        left, right, (((0,), (0,)), ((), ())), preferred_element_type=jnp.float32
    )


def right_product(left, right):
    return lax.dot_general(
        left, right, (((1,), (1,)), ((), ())), preferred_element_type=jnp.float32
    )


def gelu_value(value):
    return 0.5 * value * (1.0 + lax.erf(value * root_half))


def gelu_slope(value):
    return (
        0.5 * (1.0 + lax.erf(value * root_half))
        + value * jnp.exp(-0.5 * value * value) * inverse_root_tau
    )


def norm_forward(value, gain, shift):
    centred = value - jnp.mean(value, axis=-1, keepdims=True)
    inverse = lax.rsqrt(jnp.mean(centred * centred, axis=-1, keepdims=True) + epsilon)
    normed = centred * inverse
    return (normed * gain + shift, normed, inverse)


def norm_backward(delta_out, normed, inverse, gain):
    scaled = delta_out * gain
    delta_in = inverse * (
        scaled
        - jnp.mean(scaled, axis=-1, keepdims=True)
        - normed * jnp.mean(scaled * normed, axis=-1, keepdims=True)
    )
    return (delta_in, jnp.sum(delta_out * normed, axis=0), jnp.sum(delta_out, axis=0))


def masked_scores(queries, keys, valid):
    scale = 1.0 / math.sqrt(queries.shape[-1])
    scores = (
        jnp.einsum("bqhe,bkhe->bhqk", queries, keys, preferred_element_type=jnp.float32) * scale
    )
    return jnp.where(valid[:, None], scores, floor_score)


def attend_forward(queries, keys, values, valid):
    scores = masked_scores(queries, keys, valid)
    highest = jnp.max(scores, axis=-1, keepdims=True)
    log_total = highest + jnp.log(jnp.sum(jnp.exp(scores - highest), axis=-1, keepdims=True))
    shares = jnp.exp(scores - log_total).astype(jnp.bfloat16)
    context = jnp.einsum("bhqk,bkhe->bqhe", shares, values, preferred_element_type=jnp.float32)
    return (context.astype(jnp.bfloat16), log_total)


def attend_backward(delta_context, queries, keys, values, valid, log_total):
    scale = 1.0 / math.sqrt(queries.shape[-1])
    shares = jnp.exp(masked_scores(queries, keys, valid) - log_total)
    delta_shares = jnp.einsum(
        "bqhe,bkhe->bhqk", delta_context, values, preferred_element_type=jnp.float32
    )
    delta_values = jnp.einsum(
        "bhqk,bqhe->bkhe",
        shares.astype(jnp.bfloat16),
        delta_context,
        preferred_element_type=jnp.float32,
    )
    inner = jnp.sum(delta_shares * shares, axis=-1, keepdims=True)
    delta_scores = (shares * (delta_shares - inner)).astype(jnp.bfloat16)
    delta_queries = (
        jnp.einsum("bhqk,bkhe->bqhe", delta_scores, keys, preferred_element_type=jnp.float32)
        * scale
    )
    delta_keys = (
        jnp.einsum("bhqk,bqhe->bkhe", delta_scores, queries, preferred_element_type=jnp.float32)
        * scale
    )
    return (delta_queries, delta_keys, delta_values)


def block_forward(inputs, layer, attend):
    (
        project_weight,
        output_weight,
        up_weight,
        down_weight,
        first_gain,
        first_shift,
        second_gain,
        second_shift,
    ) = layer
    inputs_low = inputs.astype(jnp.bfloat16)
    projected = product(inputs_low, project_weight).astype(jnp.bfloat16)
    context, attend_kept = attend(projected)
    mixed = product(context, output_weight)
    first, first_normed, first_inverse = norm_forward(
        inputs + mixed, first_gain.astype(jnp.float32), first_shift.astype(jnp.float32)
    )
    first_low = first.astype(jnp.bfloat16)
    hidden = product(first_low, up_weight)
    active = gelu_value(hidden).astype(jnp.bfloat16)
    second, second_normed, second_inverse = norm_forward(
        first + product(active, down_weight),
        second_gain.astype(jnp.float32),
        second_shift.astype(jnp.float32),
    )
    kept = (
        inputs_low,
        projected,
        context,
        attend_kept,
        first_normed,
        first_inverse,
        first_low,
        hidden,
        active,
        second_normed,
        second_inverse,
    )
    return (second, kept)


def block_backward(delta_out, kept, layer, attend_back):
    (
        project_weight,
        output_weight,
        up_weight,
        down_weight,
        first_gain,
        first_shift,
        second_gain,
        second_shift,
    ) = layer
    (
        inputs_low,
        projected,
        context,
        attend_kept,
        first_normed,
        first_inverse,
        first_low,
        hidden,
        active,
        second_normed,
        second_inverse,
    ) = kept
    delta_second, second_gain_delta, second_shift_delta = norm_backward(
        delta_out, second_normed, second_inverse, second_gain.astype(jnp.float32)
    )
    branch_low = delta_second.astype(jnp.bfloat16)
    delta_down = left_product(active, branch_low)
    delta_hidden = (right_product(branch_low, down_weight) * gelu_slope(hidden)).astype(
        jnp.bfloat16
    )
    delta_up = left_product(first_low, delta_hidden)
    delta_first = delta_second + right_product(delta_hidden, up_weight)
    delta_mixed, first_gain_delta, first_shift_delta = norm_backward(
        delta_first, first_normed, first_inverse, first_gain.astype(jnp.float32)
    )
    mixed_low = delta_mixed.astype(jnp.bfloat16)
    delta_output = left_product(context, mixed_low)
    delta_context = right_product(mixed_low, output_weight).astype(jnp.bfloat16)
    delta_projected = attend_back(delta_context, projected, attend_kept)
    delta_project = left_product(inputs_low, delta_projected)
    delta_inputs = delta_mixed + right_product(delta_projected, project_weight)
    return (
        delta_inputs,
        (
            delta_project,
            delta_output,
            delta_up,
            delta_down,
            first_gain_delta,
            first_shift_delta,
            second_gain_delta,
            second_shift_delta,
        ),
    )


def local(
    tokens,
    token_counts,
    segment_project,
    segment_output,
    segment_up,
    segment_down,
    segment_scale,
    segment_offset,
    segment_gain,
    segment_shift,
    document_project,
    document_output,
    document_up,
    document_down,
    document_scale,
    document_offset,
    document_gain,
    document_shift,
    position,
    cotangent,
):
    batches, segments, length, width = tokens.shape
    heads = HEADS
    head_width = width // heads
    rows_total = segments * length
    index = lax.axis_index(("seg", "rep"))
    first_segment = index * segments
    own_document = first_segment // DOC_SEGS
    positions = jnp.arange(length)
    slots = (first_segment + jnp.arange(segments)) % DOC_SEGS
    picker = (slots[:, None] == jnp.arange(DOC_SEGS)[None, :]).astype(jnp.float32)
    levels = (DOC_SEGS // segments).bit_length() - 1
    gathered_once = (
        lax.all_gather(segment_project, ("seg", "rep"), axis=0, tiled=True),
        lax.all_gather(segment_output, ("seg", "rep"), axis=0, tiled=True),
        lax.all_gather(segment_up, ("seg", "rep"), axis=0, tiled=True),
        lax.all_gather(segment_down, ("seg", "rep"), axis=0, tiled=True),
        lax.all_gather(segment_scale, ("seg", "rep"), axis=0, tiled=True),
        lax.all_gather(segment_offset, ("seg", "rep"), axis=0, tiled=True),
        lax.all_gather(segment_gain, ("seg", "rep"), axis=0, tiled=True),
        lax.all_gather(segment_shift, ("seg", "rep"), axis=0, tiled=True),
        lax.all_gather(document_project, ("seg", "rep"), axis=0, tiled=True),
        lax.all_gather(document_output, ("seg", "rep"), axis=0, tiled=True),
        lax.all_gather(document_up, ("seg", "rep"), axis=0, tiled=True),
        lax.all_gather(document_down, ("seg", "rep"), axis=0, tiled=True),
        lax.all_gather(document_scale, ("seg", "rep"), axis=0, tiled=True),
        lax.all_gather(document_offset, ("seg", "rep"), axis=0, tiled=True),
        lax.all_gather(document_gain, ("seg", "rep"), axis=0, tiled=True),
        lax.all_gather(document_shift, ("seg", "rep"), axis=0, tiled=True),
        lax.all_gather(position, ("seg", "rep"), axis=0, tiled=True),
    )
    outputs = []
    deltas = []
    totals = None
    for batch in range(batches):
        segment_layer = gathered_once[0:8]
        document_layer = gathered_once[8:16]
        table = jnp.transpose(gathered_once[16].astype(jnp.float32))
        counts_row = token_counts[batch]
        local_counts = lax.dynamic_slice_in_dim(counts_row, first_segment, segments)
        token_valid = (positions[None, :] < local_counts[:, None]) | (positions[None, :] == 0)
        segment_valid = token_valid[:, None, :]

        def segment_attend(projected):
            parts = projected.reshape(segments, length, 3, heads, head_width)
            context, log_total = attend_forward(
                parts[:, :, 0], parts[:, :, 1], parts[:, :, 2], segment_valid
            )
            return (context.reshape(rows_total, width), log_total)

        def segment_back(delta_context, projected, log_total):
            parts = projected.reshape(segments, length, 3, heads, head_width)
            delta_queries, delta_keys, delta_values = attend_backward(
                delta_context.reshape(segments, length, heads, head_width),
                parts[:, :, 0],
                parts[:, :, 1],
                parts[:, :, 2],
                segment_valid,
                log_total,
            )
            return (
                jnp.stack((delta_queries, delta_keys, delta_values), axis=2)
                .reshape(rows_total, 3 * width)
                .astype(jnp.bfloat16)
            )

        def document_attend(projected):
            queries = projected[:, :width].reshape(1, segments, heads, head_width)
            pairs = projected[:, width:]
            collected = pairs[None]
            for bit in range(levels):
                partner = partner_2(collected, ("seg", "rep"), bit)
                upper = jnp.right_shift(index, bit) % 2
                collected = jnp.where(
                    upper == 0,
                    jnp.concatenate((collected, partner), axis=0),
                    jnp.concatenate((partner, collected), axis=0),
                )
            collected = collected.reshape(DOC_SEGS, 2 * width)
            key_valid = lax.dynamic_slice_in_dim(counts_row, own_document * DOC_SEGS, DOC_SEGS) > 0
            keys = collected[:, :width].reshape(1, DOC_SEGS, heads, head_width)
            values = collected[:, width:].reshape(1, DOC_SEGS, heads, head_width)
            valid = key_valid[None, None, :]
            context, log_total = attend_forward(queries, keys, values, valid)
            return (context.reshape(segments, width), (collected, valid, log_total))

        def document_back(delta_context, projected, kept_rows):
            collected, valid, log_total = kept_rows
            queries = projected[:, :width].reshape(1, segments, heads, head_width)
            keys = collected[:, :width].reshape(1, DOC_SEGS, heads, head_width)
            values = collected[:, width:].reshape(1, DOC_SEGS, heads, head_width)
            delta_queries, delta_keys, delta_values = attend_backward(
                delta_context.reshape(1, segments, heads, head_width),
                queries,
                keys,
                values,
                valid,
                log_total,
            )
            delta_pairs = jnp.concatenate(
                (delta_keys.reshape(DOC_SEGS, width), delta_values.reshape(DOC_SEGS, width)), axis=1
            )
            folded = delta_pairs.reshape(DOC_SEGS // segments, segments, 2 * width)
            for bit in reversed(range(levels)):
                halves = folded.reshape(2, folded.shape[0] // 2, segments, 2 * width)
                upper = jnp.right_shift(index, bit) % 2
                keep = jnp.where(upper == 0, halves[0], halves[1])
                send = jnp.where(upper == 0, halves[1], halves[0])
                folded = keep + partner_2(send.astype(jnp.bfloat16), ("seg", "rep"), bit).astype(
                    send.dtype
                )
            own_pairs = folded.reshape(segments, 2 * width)
            return jnp.concatenate(
                (delta_queries.reshape(segments, width), own_pairs), axis=1
            ).astype(jnp.bfloat16)

        inputs = tokens[batch].astype(jnp.float32).reshape(rows_total, width)
        segment_rows, segment_kept = block_forward(inputs, segment_layer, segment_attend)
        segment_rows = segment_rows.reshape(segments, length, width)
        lookup = jnp.sum(picker[:, :, None] * table[None, :, :], axis=1)
        summary_rows = segment_rows[:, 0, :] + lookup
        summary_out, document_kept = block_forward(summary_rows, document_layer, document_attend)
        outputs.append(segment_rows.at[:, 0, :].set(summary_out).astype(jnp.bfloat16))
        incoming = cotangent[batch].astype(jnp.float32)
        delta_summary, document_deltas = block_backward(
            incoming[:, 0, :], document_kept, document_layer, document_back
        )
        delta_table = jnp.transpose(jnp.sum(picker[:, :, None] * delta_summary[:, None, :], axis=0))
        delta_rows = incoming.at[:, 0, :].set(delta_summary).reshape(rows_total, width)
        delta_inputs, segment_deltas = block_backward(
            delta_rows, segment_kept, segment_layer, segment_back
        )
        deltas.append(delta_inputs.reshape(segments, length, width))
        current = segment_deltas + document_deltas + (delta_table,)
        totals = (
            current
            if totals is None
            else tuple((left + right for left, right in zip(totals, current)))
        )
    groups = lax.axis_size("seg")
    shaped = tuple(
        (item.reshape((groups, item.shape[0] // groups) + item.shape[1:]) for item in totals)
    )
    received = (
        lax.all_to_all(
            shaped[0].astype(jnp.bfloat16), "seg", split_axis=0, concat_axis=0, tiled=True
        ).astype(jnp.float32),
        lax.all_to_all(
            shaped[1].astype(jnp.bfloat16), "seg", split_axis=0, concat_axis=0, tiled=True
        ).astype(jnp.float32),
        lax.all_to_all(
            shaped[2].astype(jnp.bfloat16), "seg", split_axis=0, concat_axis=0, tiled=True
        ).astype(jnp.float32),
        lax.all_to_all(
            shaped[3].astype(jnp.bfloat16), "seg", split_axis=0, concat_axis=0, tiled=True
        ).astype(jnp.float32),
        lax.all_to_all(
            shaped[4].astype(jnp.bfloat16), "seg", split_axis=0, concat_axis=0, tiled=True
        ).astype(jnp.float32),
        lax.all_to_all(
            shaped[5].astype(jnp.bfloat16), "seg", split_axis=0, concat_axis=0, tiled=True
        ).astype(jnp.float32),
        lax.all_to_all(
            shaped[6].astype(jnp.bfloat16), "seg", split_axis=0, concat_axis=0, tiled=True
        ).astype(jnp.float32),
        lax.all_to_all(
            shaped[7].astype(jnp.bfloat16), "seg", split_axis=0, concat_axis=0, tiled=True
        ).astype(jnp.float32),
        lax.all_to_all(
            shaped[8].astype(jnp.bfloat16), "seg", split_axis=0, concat_axis=0, tiled=True
        ).astype(jnp.float32),
        lax.all_to_all(
            shaped[9].astype(jnp.bfloat16), "seg", split_axis=0, concat_axis=0, tiled=True
        ).astype(jnp.float32),
        lax.all_to_all(
            shaped[10].astype(jnp.bfloat16), "seg", split_axis=0, concat_axis=0, tiled=True
        ).astype(jnp.float32),
        lax.all_to_all(
            shaped[11].astype(jnp.bfloat16), "seg", split_axis=0, concat_axis=0, tiled=True
        ).astype(jnp.float32),
        lax.all_to_all(
            shaped[12].astype(jnp.bfloat16), "seg", split_axis=0, concat_axis=0, tiled=True
        ).astype(jnp.float32),
        lax.all_to_all(
            shaped[13].astype(jnp.bfloat16), "seg", split_axis=0, concat_axis=0, tiled=True
        ).astype(jnp.float32),
        lax.all_to_all(
            shaped[14].astype(jnp.bfloat16), "seg", split_axis=0, concat_axis=0, tiled=True
        ).astype(jnp.float32),
        lax.all_to_all(
            shaped[15].astype(jnp.bfloat16), "seg", split_axis=0, concat_axis=0, tiled=True
        ).astype(jnp.float32),
        lax.all_to_all(
            shaped[16].astype(jnp.bfloat16), "seg", split_axis=0, concat_axis=0, tiled=True
        ).astype(jnp.float32),
    )
    summed = tuple((jnp.sum(item, axis=0) for item in received))
    reduced = (
        lax.psum_scatter(
            summed[0].astype(jnp.bfloat16), "rep", scatter_dimension=0, tiled=True
        ).astype(jnp.float32),
        lax.psum_scatter(
            summed[1].astype(jnp.bfloat16), "rep", scatter_dimension=0, tiled=True
        ).astype(jnp.float32),
        lax.psum_scatter(
            summed[2].astype(jnp.bfloat16), "rep", scatter_dimension=0, tiled=True
        ).astype(jnp.float32),
        lax.psum_scatter(
            summed[3].astype(jnp.bfloat16), "rep", scatter_dimension=0, tiled=True
        ).astype(jnp.float32),
        lax.psum_scatter(
            summed[4].astype(jnp.bfloat16), "rep", scatter_dimension=0, tiled=True
        ).astype(jnp.float32),
        lax.psum_scatter(
            summed[5].astype(jnp.bfloat16), "rep", scatter_dimension=0, tiled=True
        ).astype(jnp.float32),
        lax.psum_scatter(
            summed[6].astype(jnp.bfloat16), "rep", scatter_dimension=0, tiled=True
        ).astype(jnp.float32),
        lax.psum_scatter(
            summed[7].astype(jnp.bfloat16), "rep", scatter_dimension=0, tiled=True
        ).astype(jnp.float32),
        lax.psum_scatter(
            summed[8].astype(jnp.bfloat16), "rep", scatter_dimension=0, tiled=True
        ).astype(jnp.float32),
        lax.psum_scatter(
            summed[9].astype(jnp.bfloat16), "rep", scatter_dimension=0, tiled=True
        ).astype(jnp.float32),
        lax.psum_scatter(
            summed[10].astype(jnp.bfloat16), "rep", scatter_dimension=0, tiled=True
        ).astype(jnp.float32),
        lax.psum_scatter(
            summed[11].astype(jnp.bfloat16), "rep", scatter_dimension=0, tiled=True
        ).astype(jnp.float32),
        lax.psum_scatter(
            summed[12].astype(jnp.bfloat16), "rep", scatter_dimension=0, tiled=True
        ).astype(jnp.float32),
        lax.psum_scatter(
            summed[13].astype(jnp.bfloat16), "rep", scatter_dimension=0, tiled=True
        ).astype(jnp.float32),
        lax.psum_scatter(
            summed[14].astype(jnp.bfloat16), "rep", scatter_dimension=0, tiled=True
        ).astype(jnp.float32),
        lax.psum_scatter(
            summed[15].astype(jnp.bfloat16), "rep", scatter_dimension=0, tiled=True
        ).astype(jnp.float32),
        lax.psum_scatter(
            summed[16].astype(jnp.bfloat16), "rep", scatter_dimension=0, tiled=True
        ).astype(jnp.float32),
    )
    return (jnp.stack(outputs), jnp.stack(deltas)) + tuple(reduced)


def solution(mesh):
    sizes = dict(mesh.shape)
    body = local_fast if (sizes["seg"], sizes["rep"]) == (16, 2) else local
    return jax.shard_map(
        body,
        mesh=mesh,
        in_specs=(
            P(None, ("seg", "rep"), None, None),
            P(),
            P(("seg", "rep"), None),
            P(("seg", "rep"), None),
            P(("seg", "rep"), None),
            P(("seg", "rep"), None),
            P(("seg", "rep")),
            P(("seg", "rep")),
            P(("seg", "rep")),
            P(("seg", "rep")),
            P(("seg", "rep"), None),
            P(("seg", "rep"), None),
            P(("seg", "rep"), None),
            P(("seg", "rep"), None),
            P(("seg", "rep")),
            P(("seg", "rep")),
            P(("seg", "rep")),
            P(("seg", "rep")),
            P(("seg", "rep"), None),
            P(None, ("seg", "rep"), None, None),
        ),
        out_specs=(
            P(None, ("seg", "rep"), None, None),
            P(None, ("seg", "rep"), None, None),
            P(("seg", "rep"), None),
            P(("seg", "rep"), None),
            P(("seg", "rep"), None),
            P(("seg", "rep"), None),
            P(("seg", "rep")),
            P(("seg", "rep")),
            P(("seg", "rep")),
            P(("seg", "rep")),
            P(("seg", "rep"), None),
            P(("seg", "rep"), None),
            P(("seg", "rep"), None),
            P(("seg", "rep"), None),
            P(("seg", "rep")),
            P(("seg", "rep")),
            P(("seg", "rep")),
            P(("seg", "rep")),
            P(("seg", "rep"), None),
        ),
        check_vma=False,
    )
```
